32 devices in a mesh: head: 16 (over z, y, x), seq: 2 (over core).
Axes of the slice: x: 2, y: 2, z: 4, core: 2. Of those that a mesh axis runs over, the one named last changes fastest.
Arguments:
- tokens: bfloat16 [2, 2048, 2048], P('seq', 'head'), may hold values from -6 to 6
- cotangent: bfloat16 [2, 2048, 2048], P('seq', 'head'), may hold values from -6 to 6
- segment_ids: int32 [2, 2048], P('seq', 'head'), may hold values from 0 to 3, never falling along the last dimension, each value on 1 to 1024 neighbouring positions
- owner_map: int32 [256], replicated, may hold values from 0 to 255, each once
- weights: float32 [256, 512, 512], P(('head', 'seq')), may hold values from -0.125 to 0.125
- norm_gains: float32 [4, 2048], replicated, may hold values from 0.5 to 1.5
- left_stats: float32 [256, 512, 512], P(('head', 'seq')), as said below
- right_stats: float32 [256, 512, 512], P(('head', 'seq')), as said below
- left_root: float32 [256, 512, 512], P(('head', 'seq')), as said below
- right_root: float32 [256, 512, 512], P(('head', 'seq')), as said below
Outputs:
- output: bfloat16 [2, 2048, 2048], P('seq', 'head')
- input_grad: float32 [2, 2048, 2048], P('seq', 'head')
- grad_slots: float32 [256, 512, 512], P(('head', 'seq'))
- left_new: float32 [256, 512, 512], P(('head', 'seq'))
- right_new: float32 [256, 512, 512], P(('head', 'seq'))
- new_weights: float32 [256, 512, 512], P(('head', 'seq'))
- gain_grads: float32 [4, 2048], replicated
- new_gains: float32 [4, 2048], replicated
The draws below stay inside these ranges and needn't reach their ends.
Inputs may be any that keep to these rules, and one draw needn't show every extreme that they name: `segment_ids`: within each row ids never fall, each sequence spans 1 to 1024 positions, and one spans exactly 1024. `owner_map`: each block number stands in exactly one slot. `left_stats`: each slot's matrix is symmetric. `right_stats`: each slot's matrix is symmetric. `left_root`: each slot's matrix is symmetric. `right_root`: each slot's matrix is symmetric.
All inputs are finite; a program needn't handle non-finite values.
Results may differ from the reference program's by a relative error of at most 0.015.
Values may be sent and summed in bfloat16 or wider, within the bound.
No kernel may reach another device: no remote copies, remote signals or barrier semaphores. Data moves between devices by JAX's collectives and lax.ppermute only.
A program may use at most 512 MiB of HBM per device.

```python
import math
import jax
import jax.numpy as jnp
import numpy as np
from jax import lax

D = 2048
FF = 8192
HEADS = 16
SEGMAX = 1024
BS = 512
ROW_LEN = 2048
ROWS = 2
TOKENS = 4096
SEGS = 4
NB = 256


def symmetric_noise(key, salt):
    folded = jax.random.fold_in(key, salt)
    first_key, second_key = jax.random.split(folded)
    noise = jnp.clip(jax.random.normal(first_key, (NB, BS, BS), jnp.float32), -3.0, 3.0)
    mirror = (noise + jnp.swapaxes(noise, 1, 2)) * 0.7071
    identity = jnp.eye(BS, dtype=jnp.float32)
    return (mirror * (1.0 - identity), identity, second_key)


def statistic(key, salt):
    mirror, identity, second_key = symmetric_noise(key, salt)
    factors = jnp.exp(jax.random.uniform(second_key, (NB, BS), jnp.float32, -0.69, 2.08))
    level = 1.0 * BS * TOKENS
    return level * (factors[:, :, None] * identity + 0.6 / BS ** 0.5 * mirror)


def inverse_root(key, salt):
    mirror, identity, second_key = symmetric_noise(key, salt)
    factors = jnp.exp(jax.random.uniform(second_key, (NB, BS), jnp.float32, -0.69, 0.69))
    level = (2.0 * BS * TOKENS) ** (-0.25)
    return level * (factors[:, :, None] * identity + 0.3 / BS ** 0.5 * mirror)


def draw_left_stats(key, part):
    return statistic(key, 11)


def draw_right_stats(key, part):
    return statistic(key, 23)


def draw_left_root(key, part):
    return inverse_root(key, 37)


def draw_right_root(key, part):
    return inverse_root(key, 41)


def steps_of(own_key, dims, cuts, low, largest):
    level, own = 1.0, jax.random.fold_in(own_key, 6)
    for dim, parts in cuts:
        heights = jnp.exp(jax.random.uniform(jax.random.fold_in(own, dim), (parts,), jnp.float32, low / len(cuts), largest / len(cuts)))
        level = level * jnp.repeat(heights, dims[dim] // parts).reshape([-1 if axis == dim else 1 for axis in range(len(dims))])
    return level


def length_profile(count, total, bound, lean):
    portions = [(1 << 20) // math.isqrt(rank ** lean) + 1 for rank in range(2, count + 1)]
    rest, holding = total - bound - (count - 1), [1] * (count - 1)
    while rest > 0:
        movable = [i for i in range(count - 1) if holding[i] < bound]
        pool, budget = sum([portions[i] for i in movable]), rest
        for i in movable:
            addition = min(bound - holding[i], max(1, budget * portions[i] // pool), rest)
            holding[i] = holding[i] + addition
            rest = rest - addition
    return np.array([bound] + holding)


def ragged_sizes(key, amount, total, reach, lean):
    if amount == 2:
        one = jax.random.randint(key, (), max(1, total - reach), min(reach, total - 1) + 1)
        return jnp.stack([one, total - one])
    sizes = jnp.asarray(length_profile(amount, total, reach, lean), jnp.int32)
    twos = (amount - 1) // 2
    donor, taker = sizes[1:1 + 2 * twos:2], sizes[2:2 + 2 * twos:2]
    room = jnp.minimum(donor - 1, reach - taker)
    moved = jax.random.randint(jax.random.fold_in(key, 1), (twos,), 0, 1 << 20) % (room + 1)
    sizes = sizes.at[1:1 + 2 * twos:2].set(donor - moved).at[2:2 + 2 * twos:2].set(taker + moved)
    return sizes[jax.random.permutation(jax.random.fold_in(key, 2), amount)]


def gaussian(own_key, dims, width, bound, cuts=(), kind=jnp.bfloat16):
    loudness = steps_of(own_key, dims, cuts, -0.22, 0.18) if cuts else 1.0
    values = jax.random.normal(own_key, dims, jnp.float32) * width * loudness
    return jnp.minimum(jnp.maximum(values, -bound), bound).astype(kind)


def setup_inputs(seed: int = 0) -> dict:
    key_list = jax.random.split(jax.random.key(seed), 11)
    return {
        "tokens": gaussian(key_list[0], (ROWS, ROW_LEN, D), 1.0, 6.0, ((0, 2), (1, 16))),
        "cotangent": gaussian(key_list[1], (ROWS, ROW_LEN, D), 1.0, 6.0, ((0, 2), (1, 16))),
        "segment_ids": jax.vmap(lambda own: jnp.searchsorted(jnp.cumsum(ragged_sizes(own, SEGS, ROW_LEN, SEGMAX, 2)), jnp.arange(ROW_LEN), side="right"))(jax.random.split(key_list[2], ROWS)).reshape((ROWS, ROW_LEN)).astype(jnp.int32),
        "owner_map": jax.random.permutation(key_list[3], NB).astype(jnp.int32),
        "weights": gaussian(key_list[4], (NB, BS, BS), D ** -0.5, 0.125, ((0, 32),), jnp.float32),
        "norm_gains": jnp.clip(1.0 + 0.1 * jax.random.normal(key_list[5], (4, D), jnp.float32), 0.5, 1.5),
        "left_stats": draw_left_stats(jax.random.fold_in(key_list[10], 71), 0),
        "right_stats": draw_right_stats(jax.random.fold_in(key_list[10], 71), 0),
        "left_root": draw_left_root(jax.random.fold_in(key_list[10], 71), 0),
        "right_root": draw_right_root(jax.random.fold_in(key_list[10], 71), 0),
    }


@jax.custom_vjp
def low(v):
    return lax.optimization_barrier(v.astype(jnp.bfloat16)).astype(jnp.float32)

@jax.custom_vjp
def low_back(v):
    return v

def low_keep(v):
    return (low(v), None)

def low_pass(kept, grad):
    return (grad,)

def back_keep(v):
    return (v, None)

def back_low(kept, grad):
    return (low(grad),)
low.defvjp(low_keep, low_pass)
low_back.defvjp(back_keep, back_low)
epsilon = 1e-06
rope_base = 500000.0
decay_rate = 0.5
step_rate = 0.5
gain_rate = 0.3
highest = lax.Precision.HIGHEST

def matmul(left_side, right_side):
    return jnp.dot(left_side, right_side, precision=highest, preferred_element_type=jnp.float32)

def rms_norm(values, gain_vec):
    return values * lax.rsqrt(lax.optimization_barrier(jnp.mean(values * values, axis=-1, keepdims=True)) + epsilon) * gain_vec

def positions_of(segment_row):
    length = segment_row.shape[0]
    indices = jnp.arange(length, dtype=jnp.int32)
    earlier = jnp.concatenate([jnp.full((1,), -1, jnp.int32), segment_row[:-1]])
    begins = lax.cummax(jnp.where(segment_row != earlier, indices, 0), axis=0)
    return indices - begins

def rotate(vectors, places, head_count):
    token_count = vectors.shape[0]
    head_size = vectors.shape[1] // head_count
    half_size = head_size // 2
    frequency = rope_base ** (-2.0 * jnp.arange(half_size, dtype=jnp.float32) / head_size)
    angles = places.astype(jnp.float32)[:, None] * frequency[None, :]
    cosine = jnp.cos(angles)[:, None, :]
    sine_part = jnp.sin(angles)[:, None, :]
    grouped = vectors.reshape(token_count, head_count, head_size)
    first_half = grouped[..., :half_size]
    second_half = grouped[..., half_size:]
    turned = jnp.concatenate([first_half * cosine - second_half * sine_part, second_half * cosine + first_half * sine_part], axis=-1)
    return turned.reshape(token_count, head_count * head_size)

def layer_row(row, segment_row, w_query, w_key, w_value, w_output, w_gate, w_up, w_down, gains_now):
    places = positions_of(segment_row)
    length = row.shape[0]
    head_size = row.shape[1] // HEADS
    query = low_back(low(rotate(rms_norm(low_back(matmul(row, low(w_query))), gains_now[2]), places, HEADS)))
    key_vecs = low_back(low(rotate(rms_norm(low_back(matmul(row, low(w_key))), gains_now[3]), places, HEADS)))
    value_vecs = low_back(low(matmul(row, low(w_value))))
    query_heads = query.reshape(length, HEADS, head_size)
    key_heads = key_vecs.reshape(length, HEADS, head_size)
    value_heads = value_vecs.reshape(length, HEADS, head_size)
    scores = low_back(jnp.einsum('qhd,khd->hqk', query_heads, key_heads, precision=highest) * head_size ** (-0.5))
    indices = jnp.arange(length, dtype=jnp.int32)
    allowed = (segment_row[:, None] == segment_row[None, :]) & (indices[None, :] <= indices[:, None])
    scores = jnp.where(allowed[None], scores, -1e+30)
    attention = jax.nn.softmax(scores, axis=-1)
    mixture = jnp.einsum('hqk,khd->qhd', low(attention), value_heads, precision=highest).reshape(length, HEADS * head_size)
    attended = low_back(low(mixture))
    out_attn = low_back(matmul(attended, low(w_output)))
    resid = row + rms_norm(out_attn, gains_now[0])
    resid_low = low(resid)
    gate_out = low_back(matmul(resid_low, low(w_gate)))
    upward = low_back(matmul(resid_low, low(w_up)))
    hidden = low(jax.nn.silu(gate_out) * upward)
    down_out = low_back(matmul(hidden, low(w_down)))
    return resid + rms_norm(down_out, gains_now[1])

def matrix_shapes():
    return [(D, D)] * 4 + [(D, FF), (D, FF), (FF, D)]

def to_matrices(blocks):
    matrices = []
    offset = 0
    for row_count, col_count in matrix_shapes():
        number = row_count // BS * (col_count // BS)
        grid = blocks[offset:offset + number].reshape(row_count // BS, col_count // BS, BS, BS)
        matrices.append(grid.transpose(0, 2, 1, 3).reshape(row_count, col_count))
        offset = offset + number
    return matrices

def to_blocks(matrices):
    pieces = []
    for matrix in matrices:
        row_count, col_count = matrix.shape
        grid = matrix.reshape(row_count // BS, BS, col_count // BS, BS).transpose(0, 2, 1, 3)
        pieces.append(grid.reshape(-1, BS, BS))
    return jnp.concatenate(pieces, axis=0)

def batched(left_side, right_side, form):
    return jnp.einsum(form, left_side, right_side, precision=highest)

def reference(tokens, cotangent, segment_ids, owner_map, weights, norm_gains, left_stats, right_stats, left_root, right_root):
    inverse = jnp.zeros((NB,), jnp.int32).at[owner_map].set(jnp.arange(NB, dtype=jnp.int32))
    matrices = to_matrices(weights[inverse])

    def forward(inputs, w_query, w_key, w_value, w_output, w_gate, w_up, w_down, gains_now):

        def one_row(paired):
            return jax.checkpoint(layer_row)(paired[0], paired[1], w_query, w_key, w_value, w_output, w_gate, w_up, w_down, gains_now)
        return lax.map(one_row, (inputs, segment_ids))
    result, pullback = jax.vjp(forward, tokens.astype(jnp.float32), *matrices, norm_gains)
    grads = pullback(cotangent.astype(jnp.float32))
    grad_slots = to_blocks(list(grads[1:8]))[owner_map]
    gain_grads = grads[8]
    left_new = decay_rate * left_stats + (1.0 - decay_rate) * batched(grad_slots, grad_slots, 'sij,skj->sik')
    right_new = decay_rate * right_stats + (1.0 - decay_rate) * batched(grad_slots, grad_slots, 'sji,sjk->sik')
    update = batched(batched(left_root, grad_slots, 'sij,sjk->sik'), right_root, 'sij,sjk->sik')
    new_weights = weights - step_rate * update
    new_gains = norm_gains - gain_rate * gain_grads * lax.rsqrt(lax.optimization_barrier(jnp.mean(gain_grads * gain_grads, axis=1, keepdims=True)) + epsilon)
    return (result.astype(jnp.bfloat16), grads[0], grad_slots, left_new, right_new, new_weights, gain_grads, new_gains)
```

```python
import jax
import jax.numpy as jnp
from jax import lax
from jax.sharding import Mesh
from jax.sharding import PartitionSpec as P

FF = 8192
HEADS = 16
SEGMAX = 1024
QB = 512
Z = 4

epsilon = 1e-06
rope_base = 500000.0
decay_rate = 0.5
step_rate = 0.5
gain_rate = 0.3
bf16 = jnp.bfloat16
f32 = jnp.float32
EVERY = ("hz", "hp", "seq")


def mm(left_side, right_side):
    return jnp.dot(left_side, right_side, preferred_element_type=f32)


def mm_nt(left_side, right_side):
    return lax.dot_general(
        left_side, right_side, (((1,), (1,)), ((), ())), preferred_element_type=f32
    )


def mm_tn(left_side, right_side):
    return lax.dot_general(
        left_side, right_side, (((0,), (0,)), ((), ())), preferred_element_type=f32
    )


def rms_norm(values, gain_vec):
    return (
        values * lax.rsqrt(jnp.mean(values * values, axis=-1, keepdims=True) + epsilon) * gain_vec
    )


def positions_of(segment_row):
    length = segment_row.shape[0]
    indices = jnp.arange(length, dtype=jnp.int32)
    earlier = jnp.concatenate([jnp.full((1,), -1, jnp.int32), segment_row[:-1]])
    begins = lax.cummax(jnp.where(segment_row != earlier, indices, 0), axis=0)
    return indices - begins


UP = [(i, (i + 1) % Z) for i in range(Z)]


def ring_gather(block):
    blocks = [block]
    for _ in range(Z - 1):
        blocks.append(lax.ppermute(blocks[-1], "hz", UP))
    return blocks


def ring_scatter(part_of):
    total = part_of(1).astype(bf16)
    for k in (2, 3):
        total = (lax.ppermute(total, "hz", UP).astype(f32) + part_of(k)).astype(bf16)
    return lax.ppermute(total, "hz", UP).astype(f32) + part_of(0)


def sum_z(values):
    values = values + lax.ppermute(values, "hz", [(i, i ^ 1) for i in range(Z)])
    return values + lax.ppermute(values, "hz", [(i, i ^ 2) for i in range(Z)])


def body(
    tokens,
    cotangent,
    segment_ids,
    owner_map,
    weights,
    norm_gains,
    left_stats,
    right_stats,
    left_root,
    right_root,
):
    model_width = tokens.shape[2]
    local_count = tokens.shape[1]
    slots, side = weights.shape[0], weights.shape[1]
    total_blocks = owner_map.shape[0]
    PN, S = lax.axis_size("hp"), lax.axis_size("seq")
    n = Z * PN * S
    rep = PN * S
    rows = side // n
    head_size = model_width // HEADS
    quarter = model_width // Z
    score_scale = head_size ** (-0.5)
    zi, pi = lax.axis_index("hz"), lax.axis_index("hp")
    relative = (zi - jnp.arange(Z, dtype=jnp.int32)) % Z
    inputs = tokens[0]

    d_blocks, f_blocks = model_width // side, FF // side
    number = jnp.arange(total_blocks, dtype=jnp.int32)
    square = d_blocks * d_blocks
    tall = d_blocks * f_blocks
    lists = []
    grid = number[:square].reshape(d_blocks, Z, d_blocks // Z)
    for m in range(3):
        lists.append((grid + m * square).transpose(1, 0, 2).reshape(Z, -1))
    lists.append((number[:square] + 3 * square).reshape(Z, -1))
    grid = number[:tall].reshape(d_blocks, Z, f_blocks // Z).transpose(1, 0, 2).reshape(Z, -1)
    lists.append(grid + 4 * square)
    lists.append(grid + 4 * square + tall)
    lists.append(number[:tall].reshape(Z, -1) + 4 * square + 2 * tall)
    inverse = jnp.zeros((total_blocks,), jnp.int32).at[owner_map].set(number)

    low = weights.astype(bf16).reshape(slots, PN, S, Z, rows, side)
    low = low.transpose(3, 1, 2, 0, 4, 5).reshape(n * slots, rows, side)
    spread = lax.all_to_all(low, EVERY, 0, 0, tiled=True)

    def fetch(block_lists):
        order = jnp.concatenate(block_lists, axis=1)
        picked = jnp.take(spread, inverse[order.reshape(-1)], axis=0)
        got = lax.all_to_all(picked, "hz", 0, 0, tiled=True)
        got = got.reshape(Z, -1, rows, side).transpose(1, 0, 2, 3).reshape(-1, Z * rows, side)
        return lax.all_gather(got, ("hp", "seq"), axis=0, tiled=False)

    qkvo = fetch(lists[:4])
    gateup = fetch(lists[4:6])
    downs = fetch(lists[6:])

    def matrix(gathered, row_blocks):
        shaped = gathered.reshape(rep, row_blocks, -1, Z * rows, side)
        return shaped.transpose(1, 0, 3, 2, 4).reshape(row_blocks * side, -1)

    w_query, w_key, w_value = (
        matrix(qkvo[:, m * d_blocks : (m + 1) * d_blocks], d_blocks) for m in range(3)
    )
    w_output = matrix(qkvo[:, 3 * d_blocks :], d_blocks // Z)
    half = gateup.shape[1] // 2
    w_gate, w_up = matrix(gateup[:, :half], d_blocks), matrix(gateup[:, half:], d_blocks)
    w_down = matrix(downs, f_blocks // Z)

    group = Z * PN
    row_ids = lax.all_to_all(
        jnp.broadcast_to(segment_ids, (group, local_count)), ("hz", "hp"), 0, 0, tiled=True
    ).reshape(-1)
    row_length = row_ids.shape[0]
    tokens_g = lax.all_gather(inputs, "hz", axis=0, tiled=True)
    places = lax.dynamic_slice_in_dim(
        positions_of(row_ids).reshape(Z, PN, local_count), pi, 1, axis=1
    ).reshape(-1)
    group_tokens = Z * local_count
    half_size = head_size // 2
    frequency = rope_base ** (-2.0 * jnp.arange(half_size, dtype=f32) / head_size)
    angles = places.astype(f32)[:, None] * frequency[None, :]
    cosine = jnp.cos(angles)[:, None, :]
    sine = jnp.sin(angles)[:, None, :]

    def rope(values, sign):
        grouped = values.reshape(group_tokens, -1, head_size)
        first, second = grouped[..., :half_size], grouped[..., half_size:]
        turned = jnp.concatenate(
            [first * cosine - second * sine * sign, second * cosine + first * sine * sign], axis=-1
        )
        return turned.reshape(group_tokens, -1)

    gains_z = lax.dynamic_slice_in_dim(norm_gains[2:4], zi * quarter, quarter, axis=1)

    query_raw = mm(tokens_g, w_query)
    key_raw = mm(tokens_g, w_key)
    value_low = mm(tokens_g, w_value).astype(bf16)
    squares = jnp.stack([jnp.sum(query_raw * query_raw, -1), jnp.sum(key_raw * key_raw, -1)])
    invs = lax.rsqrt(sum_z(squares) / model_width + epsilon)
    query_hat, key_hat = query_raw * invs[0][:, None], key_raw * invs[1][:, None]
    query_low = rope(query_hat * gains_z[0], 1.0).astype(bf16)
    key_low = rope(key_hat * gains_z[1], 1.0).astype(bf16)

    def to_heads(stack):
        m = stack.shape[0]
        shaped = stack.reshape(m, Z, local_count, PN, -1).transpose(3, 0, 1, 2, 4)
        got = lax.all_to_all(shaped, "hp", 0, 0, tiled=True)
        return got.transpose(1, 2, 0, 3, 4).reshape(m, row_length, -1)

    def to_groups(stack):
        m = stack.shape[0]
        shaped = stack.reshape(m, Z, PN, local_count, -1).transpose(2, 0, 1, 3, 4)
        got = lax.all_to_all(shaped, "hp", 0, 0, tiled=True)
        return got.transpose(1, 2, 3, 0, 4).reshape(m, group_tokens, -1)

    qkv_rows = to_heads(jnp.stack([query_low, key_low, value_low]))
    query_rows, key_rows, value_rows = qkv_rows[0], qkv_rows[1], qkv_rows[2]
    local_width = query_rows.shape[1]
    local_heads = local_width // head_size
    window = min(QB + SEGMAX, row_length)
    block_count = row_length // QB
    starts = jnp.arange(block_count, dtype=jnp.int32) * QB

    def block_scores(query_start):
        key_start = jnp.clip(query_start + QB - window, 0, row_length - window)
        query_blk = lax.dynamic_slice_in_dim(query_rows, query_start, QB).reshape(
            QB, local_heads, head_size
        )
        key_blk = lax.dynamic_slice_in_dim(key_rows, key_start, window).reshape(
            window, local_heads, head_size
        )
        value_blk = lax.dynamic_slice_in_dim(value_rows, key_start, window).reshape(
            window, local_heads, head_size
        )
        raw_scores = (
            jnp.einsum("qhd,khd->hqk", query_blk, key_blk, preferred_element_type=f32)
            * score_scale
        )
        query_ids = lax.dynamic_slice_in_dim(row_ids, query_start, QB)
        key_ids = lax.dynamic_slice_in_dim(row_ids, key_start, window)
        query_place = query_start + jnp.arange(QB, dtype=jnp.int32)
        key_place = key_start + jnp.arange(window, dtype=jnp.int32)
        allowed = (query_ids[:, None] == key_ids[None, :]) & (
            key_place[None, :] <= query_place[:, None]
        )
        scores = jnp.where(allowed[None], raw_scores, -1e30)
        return (scores, query_blk, key_blk, value_blk, key_start)

    def attend(query_start):
        scores, query_blk, key_blk, value_blk, key_start = block_scores(query_start)
        top_score = jnp.max(scores, axis=-1, keepdims=True)
        expo = jnp.exp(scores - top_score)
        totals = jnp.sum(expo, axis=-1, keepdims=True)
        attention = (expo / totals).astype(bf16)
        mixture = jnp.einsum("hqk,khd->qhd", attention, value_blk, preferred_element_type=f32)
        return (
            mixture.reshape(QB, local_width).astype(bf16),
            (top_score + jnp.log(totals))[..., 0],
        )

    mixed_blocks, log_sums = lax.map(attend, starts)
    attended = to_groups(mixed_blocks.reshape(1, row_length, local_width))[0]
    attended_rel = jnp.take(attended.reshape(Z, local_count, quarter), relative, axis=0)
    attn_raw = ring_scatter(lambda k: mm(attended_rel[k], w_output))
    resid = inputs.astype(f32) + rms_norm(attn_raw, norm_gains[0])
    resid_low = resid.astype(bf16)

    resid_blocks = ring_gather(resid_low)
    gates = [mm(b, w_gate) for b in resid_blocks]
    ups = [mm(b, w_up) for b in resid_blocks]
    hiddens = [(jax.nn.silu(g) * u).astype(bf16) for g, u in zip(gates, ups)]
    down_raw = ring_scatter(lambda k: mm(hiddens[k], w_down))
    output = (resid + rms_norm(down_raw, norm_gains[1])).astype(bf16)[None]

    upstream = cotangent[0].astype(f32)
    _, down_norm_back = jax.vjp(rms_norm, down_raw, norm_gains[1])
    down_grad, gain_mlp_grad = down_norm_back(upstream)
    down_blocks = ring_gather(down_grad.astype(bf16))
    gate_lows, up_lows = [], []
    for block, gate, up in zip(down_blocks, gates, ups):
        hidden_grad = mm_nt(block, w_down)
        sigma = jax.nn.sigmoid(gate)
        gate_lows.append((hidden_grad * up * sigma * (1.0 + gate * (1.0 - sigma))).astype(bf16))
        up_lows.append((hidden_grad * gate * sigma).astype(bf16))
    resid_grad = upstream + ring_scatter(
        lambda k: mm_nt(gate_lows[k], w_gate) + mm_nt(up_lows[k], w_up)
    )

    def send_grads(pieces):
        joined = jnp.concatenate(pieces, axis=1)
        summed = lax.psum_scatter(joined, ("hp", "seq"), scatter_dimension=0, tiled=True)
        summed = summed.reshape(-1, Z, rows, side).transpose(1, 0, 2, 3)
        return lax.all_to_all(summed, "hz", 0, 0, tiled=True)

    def pieces_of(matrix_grad, row_blocks):
        shaped = matrix_grad.astype(bf16).reshape(row_blocks, rep, Z * rows, -1, side)
        return shaped.transpose(1, 0, 3, 2, 4).reshape(rep, -1, Z * rows, side)

    resid_all = jnp.concatenate(resid_blocks)
    gate_all, up_all = jnp.concatenate(gate_lows), jnp.concatenate(up_lows)
    hidden_all, down_all = jnp.concatenate(hiddens), jnp.concatenate(down_blocks)
    down_sent = send_grads([pieces_of(mm_tn(hidden_all, down_all), f_blocks // Z)])
    gateup_sent = send_grads(
        [
            pieces_of(mm_tn(resid_all, gate_all), d_blocks),
            pieces_of(mm_tn(resid_all, up_all), d_blocks),
        ]
    )

    _, attn_norm_back = jax.vjp(rms_norm, attn_raw, norm_gains[0])
    attn_grad, gain_attn_grad = attn_norm_back(resid_grad)
    attn_blocks = ring_gather(attn_grad.astype(bf16))
    attn_all = jnp.concatenate(attn_blocks)
    attended_grad = mm_nt(attn_all, w_output).astype(bf16)
    output_grad_w = mm_tn(attended_rel.reshape(group_tokens, quarter), attn_all)
    grad_abs = jnp.take(attended_grad.reshape(Z, local_count, quarter), relative, axis=0)
    grad_rows = to_heads(grad_abs.reshape(1, group_tokens, quarter))[0]

    def attend_back(carry, paired):
        key_acc, value_acc = carry
        query_start, log_sum = paired
        scores, query_blk, key_blk, value_blk, key_start = block_scores(query_start)
        attention = jnp.exp(scores - log_sum[..., None])
        grad_blk = lax.dynamic_slice_in_dim(grad_rows, query_start, QB).reshape(
            QB, local_heads, head_size
        )
        prob_grad = jnp.einsum("qhd,khd->hqk", grad_blk, value_blk, preferred_element_type=f32)
        center = jnp.sum(attention * prob_grad, axis=-1, keepdims=True)
        score_grad = (attention * (prob_grad - center)).astype(bf16)
        query_grad = (
            jnp.einsum("hqk,khd->qhd", score_grad, key_blk, preferred_element_type=f32)
            * score_scale
        )
        key_part = (
            jnp.einsum("hqk,qhd->khd", score_grad, query_blk, preferred_element_type=f32)
            * score_scale
        )
        value_part = jnp.einsum(
            "hqk,qhd->khd", attention.astype(bf16), grad_blk, preferred_element_type=f32
        )
        key_now = lax.dynamic_slice_in_dim(key_acc, key_start, window)
        value_now = lax.dynamic_slice_in_dim(value_acc, key_start, window)
        key_acc = lax.dynamic_update_slice_in_dim(key_acc, key_now + key_part, key_start, 0)
        value_acc = lax.dynamic_update_slice_in_dim(value_acc, value_now + value_part, key_start, 0)
        return ((key_acc, value_acc), query_grad.reshape(QB, local_width))

    zero_rows = jnp.zeros((row_length, local_heads, head_size), f32)
    (key_total, value_total), query_blocks = lax.scan(
        attend_back, (zero_rows, zero_rows), (starts, log_sums)
    )
    back = to_groups(
        jnp.stack(
            [
                query_blocks.reshape(row_length, local_width).astype(bf16),
                key_total.reshape(row_length, local_width).astype(bf16),
                value_total.reshape(row_length, local_width).astype(bf16),
            ]
        )
    )
    value_back = back[2]
    query_turn, key_turn = rope(back[0].astype(f32), -1.0), rope(back[1].astype(f32), -1.0)
    gain_query = jnp.sum(query_turn * query_hat, axis=0)
    gain_key = jnp.sum(key_turn * key_hat, axis=0)
    query_turn, key_turn = query_turn * gains_z[0], key_turn * gains_z[1]
    dots = sum_z(jnp.stack([jnp.sum(query_turn * query_hat, -1), jnp.sum(key_turn * key_hat, -1)]))
    dots = dots / model_width
    query_back = ((query_turn - query_hat * dots[0][:, None]) * invs[0][:, None]).astype(bf16)
    key_back = ((key_turn - key_hat * dots[1][:, None]) * invs[1][:, None]).astype(bf16)
    attn_sent = send_grads(
        [
            pieces_of(mm_tn(tokens_g, query_back), d_blocks),
            pieces_of(mm_tn(tokens_g, key_back), d_blocks),
            pieces_of(mm_tn(tokens_g, value_back), d_blocks),
            pieces_of(output_grad_w, d_blocks // Z),
        ]
    )
    back_rel = jnp.take(
        jnp.stack([query_back, key_back, value_back]).reshape(3, Z, local_count, quarter),
        relative,
        axis=1,
    )
    input_grad = resid_grad + ring_scatter(
        lambda k: mm_nt(back_rel[0, k], w_query)
        + mm_nt(back_rel[1, k], w_key)
        + mm_nt(back_rel[2, k], w_value)
    )

    spots = jnp.zeros((2, model_width), f32)
    spots = lax.dynamic_update_slice(spots, jnp.stack([gain_query, gain_key]), (0, zi * quarter))
    gain_local = jnp.concatenate([jnp.stack([gain_attn_grad, gain_mlp_grad]), spots])
    shares = lax.all_to_all(gain_local.reshape(n, -1), EVERY, 0, 0, tiled=True)
    share = jnp.sum(shares, axis=0)
    gain_grads = lax.all_to_all(
        jnp.broadcast_to(share, (n, share.shape[0])), EVERY, 0, 0, tiled=True
    ).reshape(gain_local.shape)

    sent = jnp.concatenate([attn_sent, gateup_sent, down_sent], axis=1)
    sent = sent.reshape(total_blocks, rows, side)
    order = jnp.concatenate(lists, axis=1).reshape(-1)
    where_is = jnp.zeros((total_blocks,), jnp.int32).at[order].set(number)
    to_slots = jnp.take(sent, where_is[owner_map], axis=0)
    got = lax.all_to_all(to_slots, EVERY, 0, 0, tiled=True)
    got = got.reshape(Z, PN, S, slots, rows, side).transpose(3, 1, 2, 0, 4, 5)
    grad_low = got.reshape(slots, side, side)
    grad_slots = grad_low.astype(f32)

    def batched(left_side, right_side, form):
        return jnp.einsum(form, left_side, right_side, preferred_element_type=f32)

    left_new = decay_rate * left_stats + (1.0 - decay_rate) * batched(
        grad_low, grad_low, "sij,skj->sik"
    )
    right_new = decay_rate * right_stats + (1.0 - decay_rate) * batched(
        grad_low, grad_low, "sji,sjk->sik"
    )
    middle = batched(left_root.astype(bf16), grad_low, "sij,sjk->sik").astype(bf16)
    update = batched(middle, right_root.astype(bf16), "sij,sjk->sik")
    new_weights = weights - step_rate * update
    new_gains = norm_gains - gain_rate * gain_grads * lax.rsqrt(
        jnp.mean(gain_grads * gain_grads, axis=1, keepdims=True) + epsilon
    )
    return (
        output,
        input_grad[None],
        grad_slots,
        left_new,
        right_new,
        new_weights,
        gain_grads,
        new_gains,
    )


def solution(mesh):
    heads, seqs = mesh.shape["head"], mesh.shape["seq"]
    fine = Mesh(mesh.devices.reshape(Z, heads // Z, seqs), EVERY)
    tok = P("seq", ("hz", "hp"), None)
    slot = P(EVERY, None, None)
    return jax.shard_map(
        body,
        mesh=fine,
        in_specs=(tok, tok, P("seq", ("hz", "hp")), P(), slot, P(), slot, slot, slot, slot),
        out_specs=(tok, tok, slot, slot, slot, slot, P(), P()),
        check_vma=False,
    )
```

```python
import functools

import jax
import jax.numpy as jnp
from jax import lax
from jax.experimental import pallas as pl
from jax.experimental.pallas import tpu as pltpu
from jax.sharding import Mesh
from jax.sharding import PartitionSpec as P

FF = 8192
HEADS = 16
SEGMAX = 1024
QB = 256
Z = 4

epsilon = 1e-06
rope_base = 500000.0
decay_rate = 0.5
step_rate = 0.5
gain_rate = 0.3
bf16 = jnp.bfloat16
f32 = jnp.float32
EVERY = ("hz", "hp", "seq")
GROUP = ("hz", "hp")
VMEM_LIMIT = 48 * 1024 * 1024


def mm(left_side, right_side):
    return jnp.dot(left_side, right_side, preferred_element_type=f32)


def mm_nt(left_side, right_side):
    return lax.dot_general(
        left_side, right_side, (((1,), (1,)), ((), ())), preferred_element_type=f32
    )


def mm_tn(left_side, right_side):
    return lax.dot_general(
        left_side, right_side, (((0,), (0,)), ((), ())), preferred_element_type=f32
    )


def params():
    return pltpu.CompilerParams(vmem_limit_bytes=VMEM_LIMIT)


def cost(flops, nbytes, exps=0):
    return pl.CostEstimate(flops=int(flops), bytes_accessed=int(nbytes), transcendentals=int(exps))


def nbytes(*arrays):
    return sum(a.size * a.dtype.itemsize for a in arrays)


def gate_up_kernel(x_ref, g_ref, u_ref, gate_ref, up_ref, hidden_ref):
    side = g_ref.shape[-1]
    for w_ref, y_ref in ((g_ref, gate_ref), (u_ref, up_ref)):
        total = None
        for r in range(w_ref.shape[1]):
            part = mm(x_ref[:, r * side : (r + 1) * side], w_ref[:, r, 0].reshape(side, side))
            total = part if total is None else total + part
        y_ref[...] = total
    gate = gate_ref[...]
    hidden_ref[...] = (gate * jax.nn.sigmoid(gate) * up_ref[...]).astype(bf16)


def gate_up(x, w):
    rep, R, C, part, side = w.shape
    count, half = x.shape[0], C // 2
    wide = jax.ShapeDtypeStruct((count, half * side), f32)
    outs = [wide, wide, jax.ShapeDtypeStruct((count, half * side), bf16)]
    col = pl.BlockSpec((count, side), lambda c: (0, c))
    return pl.pallas_call(
        gate_up_kernel,
        grid=(half,),
        in_specs=[
            pl.BlockSpec(x.shape, lambda c: (0, 0)),
            pl.BlockSpec((rep, R, 1, part, side), lambda c: (0, 0, c, 0, 0)),
            pl.BlockSpec((rep, R, 1, part, side), lambda c: (0, 0, c + half, 0, 0)),
        ],
        out_specs=[col, col, col],
        out_shape=outs,
        compiler_params=params(),
        cost_estimate=cost(2 * count * R * C * side * side, nbytes(x, w, *outs)),
    )(x, w, w)


def nn_kernel(x_ref, w_ref, y_ref):
    side = w_ref.shape[-1]
    total = None
    for r in range(w_ref.shape[1]):
        part = mm(x_ref[:, r * side : (r + 1) * side], w_ref[:, r, 0].reshape(side, side))
        total = part if total is None else total + part
    y_ref[...] = total


def nn(x, w):
    rep, R, C, part, side = w.shape
    count = x.shape[0]
    out = jax.ShapeDtypeStruct((count, C * side), f32)
    return pl.pallas_call(
        nn_kernel,
        grid=(C,),
        in_specs=[
            pl.BlockSpec(x.shape, lambda c: (0, 0)),
            pl.BlockSpec((rep, R, 1, part, side), lambda c: (0, 0, c, 0, 0)),
        ],
        out_specs=pl.BlockSpec((count, side), lambda c: (0, c)),
        out_shape=out,
        compiler_params=params(),
        cost_estimate=cost(2 * count * R * C * side * side, nbytes(x, w, out)),
    )(x, w)


def hidden_back_kernel(x_ref, w_ref, gate_ref, up_ref, y_ref):
    side = w_ref.shape[-1]
    total = None
    for c in range(w_ref.shape[2]):
        part = mm_nt(x_ref[:, c * side : (c + 1) * side], w_ref[:, 0, c].reshape(side, side))
        total = part if total is None else total + part
    gate = gate_ref[...]
    sigma = jax.nn.sigmoid(gate)
    y_ref[0] = (total * up_ref[...] * sigma * (1.0 + gate * (1.0 - sigma))).astype(bf16)
    y_ref[1] = (total * gate * sigma).astype(bf16)


def hidden_back(x, w, gate, up):
    rep, R, C, part, side = w.shape
    count = x.shape[0]
    out = jax.ShapeDtypeStruct((2, count, R * side), bf16)
    col = pl.BlockSpec((count, side), lambda r: (0, r))
    return pl.pallas_call(
        hidden_back_kernel,
        grid=(R,),
        in_specs=[
            pl.BlockSpec(x.shape, lambda r: (0, 0)),
            pl.BlockSpec((rep, 1, C, part, side), lambda r: (0, r, 0, 0, 0)),
            col,
            col,
        ],
        out_specs=pl.BlockSpec((2, count, side), lambda r: (0, 0, r)),
        out_shape=out,
        compiler_params=params(),
        cost_estimate=cost(2 * count * R * C * side * side, nbytes(x, w, gate, up, out)),
    )(x, w, gate, up)


def nt_kernel(x_ref, w_ref, y_ref):
    side = w_ref.shape[-1]
    per = x_ref.shape[2] // side
    total = None
    for c in range(w_ref.shape[2]):
        x = x_ref[c // per, :, (c % per) * side : (c % per + 1) * side]
        part = mm_nt(x, w_ref[:, 0, c].reshape(side, side))
        total = part if total is None else total + part
    y_ref[...] = total


def nt(x, w):
    rep, R, C, part, side = w.shape
    count = x.shape[1]
    out = jax.ShapeDtypeStruct((count, R * side), f32)
    return pl.pallas_call(
        nt_kernel,
        grid=(R,),
        in_specs=[
            pl.BlockSpec(x.shape, lambda r: (0, 0, 0)),
            pl.BlockSpec((rep, 1, C, part, side), lambda r: (0, r, 0, 0, 0)),
        ],
        out_specs=pl.BlockSpec((count, side), lambda r: (0, r)),
        out_shape=out,
        compiler_params=params(),
        cost_estimate=cost(2 * count * R * C * side * side, nbytes(x, w, out)),
    )(x, w)


def tn_kernel(*refs):
    y_ref, half = refs[-1], (len(refs) - 1) // 2
    rep, _, _, part, side = y_ref.shape
    left = jnp.concatenate([r[...] for r in refs[:half]], axis=0)
    right = jnp.concatenate([r[0] for r in refs[half:-1]], axis=0)
    y_ref[:, 0, 0] = mm_tn(left, right).astype(bf16).reshape(rep, part, side)


def tn(lefts, rights, rep, side):
    count = lefts[0].shape[0]
    R = lefts[0].shape[1] // side
    m, per = rights[0].shape[0], rights[0].shape[2] // side
    C = m * per
    out = jax.ShapeDtypeStruct((rep, R, C, side // rep, side), bf16)
    left_spec = pl.BlockSpec((count, side), lambda r, c: (0, r))
    right_spec = pl.BlockSpec((1, count, side), lambda r, c: (c // per, 0, c % per))
    total = count * len(lefts)
    return pl.pallas_call(
        tn_kernel,
        grid=(R, C),
        in_specs=[left_spec] * len(lefts) + [right_spec] * len(rights),
        out_specs=pl.BlockSpec((rep, 1, 1, side // rep, side), lambda r, c: (0, r, c, 0, 0)),
        out_shape=out,
        compiler_params=params(),
        cost_estimate=cost(2 * total * R * C * side * side, nbytes(*lefts, *rights, out)),
    )(*lefts, *rights)


def scores_of(q, k, begin, q_start, k_start, scale):
    scores = mm_nt(k, q) * scale
    key_place = k_start + lax.broadcasted_iota(jnp.int32, scores.shape, 0)
    query_place = q_start + lax.broadcasted_iota(jnp.int32, scores.shape, 1)
    return jnp.where((key_place >= begin) & (key_place <= query_place), scores, -1e30)


def window_start(i, block, window, length):
    start = jnp.clip(i * block + block - window, 0, length - window)
    return pl.multiple_of(start, 128)


def attend_kernel(scale, window, q_ref, k_ref, v_ref, b_ref, o_ref, lse_ref):
    block, length = q_ref.shape[0], k_ref.shape[0]
    i = pl.program_id(0)
    start = window_start(i, block, window, length)
    scores = scores_of(
        q_ref[...], k_ref[pl.ds(start, window), :], b_ref[...], i * block, start, scale
    )
    top = jnp.max(scores, axis=0, keepdims=True)
    expo = jnp.exp(scores - top)
    total = jnp.sum(expo, axis=0, keepdims=True)
    attention = (expo * (1.0 / total)).astype(bf16)
    o_ref[...] = mm_tn(attention, v_ref[pl.ds(start, window), :]).astype(bf16)
    lse_ref[...] = top + jnp.log(total)


def attend(q, k, v, begins, scale):
    length, width = q.shape
    window = min(QB + SEGMAX, length)
    full = pl.BlockSpec((length, width), lambda i: (0, 0))
    rows = pl.BlockSpec((QB, width), lambda i: (i, 0))
    line = pl.BlockSpec((1, QB), lambda i: (0, i))
    return pl.pallas_call(
        functools.partial(attend_kernel, scale, window),
        grid=(length // QB,),
        in_specs=[rows, full, full, line],
        out_specs=[rows, line],
        out_shape=[
            jax.ShapeDtypeStruct((length, width), bf16),
            jax.ShapeDtypeStruct((1, length), f32),
        ],
        compiler_params=params(),
        cost_estimate=cost(4 * length * window * width, 4 * nbytes(q), length * window),
    )(q, k, v, begins)


def attend_back_kernel(
    scale, window, q_ref, d_ref, k_ref, v_ref, b_ref, lse_ref, dq_ref, dk_ref, dv_ref, ka, va
):
    block, length = q_ref.shape[0], k_ref.shape[0]
    i = pl.program_id(0)
    start = window_start(i, block, window, length)
    span = pl.ds(start, window)

    @pl.when(i == 0)
    def _():
        ka[...] = jnp.zeros_like(ka)
        va[...] = jnp.zeros_like(va)

    q, d, k = q_ref[...], d_ref[...], k_ref[span, :]
    scores = scores_of(q, k, b_ref[...], i * block, start, scale)
    attention = jnp.exp(scores - lse_ref[...])
    prob_grad = mm_nt(v_ref[span, :], d)
    center = jnp.sum(attention * prob_grad, axis=0, keepdims=True)
    score_grad = (attention * (prob_grad - center)).astype(bf16)
    dq_ref[...] = (mm_tn(score_grad, k) * scale).astype(bf16)
    ka[span, :] += mm(score_grad, q) * scale
    va[span, :] += mm(attention.astype(bf16), d)

    @pl.when(i == pl.num_programs(0) - 1)
    def _():
        dk_ref[...] = ka[...].astype(bf16)
        dv_ref[...] = va[...].astype(bf16)


def attend_back(q, d, k, v, begins, lse, scale):
    length, width = q.shape
    window = min(QB + SEGMAX, length)
    full = pl.BlockSpec((length, width), lambda i: (0, 0))
    rows = pl.BlockSpec((QB, width), lambda i: (i, 0))
    line = pl.BlockSpec((1, QB), lambda i: (0, i))
    return pl.pallas_call(
        functools.partial(attend_back_kernel, scale, window),
        grid=(length // QB,),
        in_specs=[rows, rows, full, full, line, line],
        out_specs=[rows, full, full],
        out_shape=[jax.ShapeDtypeStruct((length, width), bf16)] * 3,
        scratch_shapes=[pltpu.VMEM((length, width), f32)] * 2,
        compiler_params=params(),
        cost_estimate=cost(10 * length * window * width, 8 * nbytes(q), length * window),
    )(q, d, k, v, begins, lse)


def shampoo_kernel(g_ref, ls_ref, rs_ref, lr_ref, rr_ref, w_ref, go_ref, lo_ref, ro_ref, wo_ref):
    g = g_ref[0]
    go_ref[0] = g.astype(f32)
    lo_ref[0] = decay_rate * ls_ref[0] + (1.0 - decay_rate) * mm_nt(g, g)
    ro_ref[0] = decay_rate * rs_ref[0] + (1.0 - decay_rate) * mm_tn(g, g)
    middle = mm(lr_ref[0].astype(bf16), g).astype(bf16)
    wo_ref[0] = w_ref[0] - step_rate * mm(middle, rr_ref[0].astype(bf16))


def shampoo(g, *rest):
    slots, side, _ = g.shape
    spec = pl.BlockSpec((1, side, side), lambda s: (s, 0, 0))
    return pl.pallas_call(
        shampoo_kernel,
        grid=(slots,),
        in_specs=[spec] * 6,
        out_specs=[spec] * 4,
        out_shape=[jax.ShapeDtypeStruct(g.shape, f32)] * 4,
        compiler_params=params(),
        cost_estimate=cost(8 * slots * side**3, 38 * g.size),
    )(g, *rest)


def rms_norm(values, gain_vec):
    return (
        values * lax.rsqrt(jnp.mean(values * values, axis=-1, keepdims=True) + epsilon) * gain_vec
    )


def begins_of(segment_row):
    length = segment_row.shape[0]
    indices = jnp.arange(length, dtype=jnp.int32)
    earlier = jnp.concatenate([jnp.full((1,), -1, jnp.int32), segment_row[:-1]])
    return lax.cummax(jnp.where(segment_row != earlier, indices, 0), axis=0)


UP = [(i, (i + 1) % Z) for i in range(Z)]


def ring_gather(block):
    blocks = [block]
    for _ in range(Z - 1):
        blocks.append(lax.ppermute(blocks[-1], "hz", UP))
    return blocks


def ring_scatter(part_of):
    total = part_of(1).astype(bf16)
    for k in (2, 3):
        total = (lax.ppermute(total, "hz", UP).astype(f32) + part_of(k)).astype(bf16)
    return lax.ppermute(total, "hz", UP).astype(f32) + part_of(0)


def sum_group(values):
    size = lax.axis_size(GROUP)
    spread = jnp.broadcast_to(values, (size,) + values.shape)
    return jnp.sum(lax.all_to_all(spread, GROUP, 0, 0, tiled=True), axis=0)


def sum_seq_scatter(values):
    S = lax.axis_size("seq")
    if S != 2:
        return lax.psum_scatter(values, "seq", scatter_dimension=0, tiled=False)
    c = lax.axis_index("seq")
    mine = lax.dynamic_index_in_dim(values, c, 0, keepdims=False)
    other = lax.dynamic_index_in_dim(values, 1 - c, 0, keepdims=False)
    got = lax.ppermute(other, "seq", [(0, 1), (1, 0)])
    return (mine.astype(f32) + got.astype(f32)).astype(bf16)


def body(
    tokens,
    cotangent,
    segment_ids,
    owner_map,
    weights,
    norm_gains,
    left_stats,
    right_stats,
    left_root,
    right_root,
):
    model_width = tokens.shape[2]
    local_count = tokens.shape[1]
    slots, side = weights.shape[0], weights.shape[1]
    total_blocks = owner_map.shape[0]
    PN, S = lax.axis_size("hp"), lax.axis_size("seq")
    n = Z * PN * S
    rep = PN * S
    rows = side // n
    part = Z * rows
    head_size = model_width // HEADS
    quarter = model_width // Z
    score_scale = head_size ** (-0.5)
    zi, pi = lax.axis_index("hz"), lax.axis_index("hp")
    head = zi * PN + pi
    relative = (zi - jnp.arange(Z, dtype=jnp.int32)) % Z
    inputs = tokens[0]

    D, F = model_width // side, FF // side
    number = jnp.arange(total_blocks, dtype=jnp.int32)
    square, tall = D * D, D * F
    qkv_number = number[: 3 * square].reshape(3, D, Z, D // Z)
    qkv_list = qkv_number.transpose(2, 1, 0, 3).reshape(Z, -1)
    out_list = number[3 * square : 4 * square]
    gateup_list = number[4 * square : 4 * square + 2 * tall].reshape(2, D, Z, F // Z)
    gateup_list = gateup_list.transpose(2, 1, 0, 3).reshape(Z, -1)
    down_list = number[4 * square + 2 * tall :].reshape(Z, -1)
    inverse = jnp.zeros((total_blocks,), jnp.int32).at[owner_map].set(number)

    low = weights.astype(bf16).reshape(slots, PN, S, Z, rows, side)
    low = low.transpose(3, 1, 2, 0, 4, 5).reshape(n * slots, rows, side)
    spread = lax.all_to_all(low, EVERY, 0, 0, tiled=True)

    def pick(numbers):
        return jnp.take(spread, inverse[numbers], axis=0)

    heads_send = pick(number[: 3 * square]).reshape(3, D, Z, rows, PN, head_size)
    heads_send = heads_send.transpose(2, 4, 0, 1, 3, 5)[:, :, None]
    heads_send = jnp.broadcast_to(heads_send, (Z, PN, S, 3, D, rows, head_size))
    heads_got = lax.all_to_all(
        heads_send.reshape(n, 3, D, rows, head_size), EVERY, 0, 0, tiled=True
    ).reshape(Z, PN, S, 3, D, rows, head_size)
    w_heads = heads_got.transpose(4, 1, 2, 0, 5, 3, 6).reshape(model_width, 3 * head_size)

    out_all = lax.all_gather(pick(out_list), EVERY, axis=0, tiled=False)
    out_all = out_all.reshape(Z, PN, S, D, D, rows, side)
    w_output = out_all.transpose(3, 1, 2, 0, 5, 4, 6).reshape(model_width, model_width)

    def fetch(numbers, R):
        got = lax.all_to_all(pick(numbers.reshape(-1)), "hz", 0, 0, tiled=True)
        got = got.reshape(Z, R, -1, rows, side).transpose(1, 2, 0, 3, 4)
        return lax.all_gather(
            got.reshape(R, -1, part, side), ("hp", "seq"), axis=0, tiled=False
        )

    w_gateup = fetch(gateup_list, D)
    w_down = fetch(down_list, F // Z)
    w_qkv = fetch(qkv_list, D)

    group = Z * PN
    row_ids = lax.all_to_all(
        jnp.broadcast_to(segment_ids, (group, local_count)), GROUP, 0, 0, tiled=True
    ).reshape(-1)
    length = row_ids.shape[0]
    tokens_row = lax.all_gather(inputs, GROUP, axis=0, tiled=True)
    begins = begins_of(row_ids)
    places = jnp.arange(length, dtype=jnp.int32) - begins
    half_size = head_size // 2
    frequency = rope_base ** (-2.0 * jnp.arange(half_size, dtype=f32) / head_size)
    angles = places.astype(f32)[:, None] * frequency[None, :]
    cosine, sine = jnp.cos(angles), jnp.sin(angles)

    def rope(values, sign):
        first, second = values[:, :half_size], values[:, half_size:]
        return jnp.concatenate(
            [first * cosine - second * sine * sign, second * cosine + first * sine * sign], axis=-1
        )

    gains_head = lax.dynamic_slice_in_dim(norm_gains[2:4], head * head_size, head_size, axis=1)

    raw = mm(tokens_row, w_heads)
    query_raw, key_raw = raw[:, :head_size], raw[:, head_size : 2 * head_size]
    value_row = raw[:, 2 * head_size :].astype(bf16)
    squares = jnp.stack([jnp.sum(query_raw * query_raw, -1), jnp.sum(key_raw * key_raw, -1)])
    invs = lax.rsqrt(sum_group(squares) / model_width + epsilon)
    query_hat, key_hat = query_raw * invs[0][:, None], key_raw * invs[1][:, None]
    query_row = rope(query_hat * gains_head[0], 1.0).astype(bf16)
    key_row = rope(key_hat * gains_head[1], 1.0).astype(bf16)

    begin_line = begins[None, :]
    mixed, log_sums = attend(query_row, key_row, value_row, begin_line, score_scale)
    attended = lax.all_to_all(
        mixed.reshape(group, local_count, head_size), GROUP, 0, 0, tiled=True
    )
    attended = attended.transpose(1, 0, 2).reshape(local_count, model_width)
    attn_raw = mm(attended, w_output)
    resid = inputs.astype(f32) + rms_norm(attn_raw, norm_gains[0])

    resid_blocks = ring_gather(resid.astype(bf16))
    gates, ups, hiddens = zip(*[gate_up(b, w_gateup) for b in resid_blocks])
    down_raw = ring_scatter(lambda k: nn(hiddens[k], w_down))
    output = (resid + rms_norm(down_raw, norm_gains[1])).astype(bf16)[None]

    upstream = cotangent[0].astype(f32)
    _, down_norm_back = jax.vjp(rms_norm, down_raw, norm_gains[1])
    down_grad, gain_mlp_grad = down_norm_back(upstream)
    down_blocks = ring_gather(down_grad.astype(bf16))
    gateup_grads = [
        hidden_back(b, w_down, gate, up) for b, gate, up in zip(down_blocks, gates, ups)
    ]
    resid_grad = upstream + ring_scatter(lambda k: nt(gateup_grads[k], w_gateup))

    def send_grads(pieces):
        pieces = pieces.reshape(rep, -1, part, side)
        summed = lax.psum_scatter(pieces, ("hp", "seq"), scatter_dimension=0, tiled=True)
        summed = summed.reshape(-1, Z, rows, side).transpose(1, 0, 2, 3)
        return lax.all_to_all(summed, "hz", 0, 0, tiled=True)

    down_sent = send_grads(tn(hiddens, [b[None] for b in down_blocks], rep, side))
    gateup_sent = send_grads(tn(resid_blocks, gateup_grads, rep, side))

    _, attn_norm_back = jax.vjp(rms_norm, attn_raw, norm_gains[0])
    attn_grad, gain_attn_grad = attn_norm_back(resid_grad)
    attn_low = attn_grad.astype(bf16)
    attended_grad = mm_nt(attn_low, w_output).astype(bf16)
    grad_row = lax.all_to_all(
        attended_grad.reshape(local_count, group, head_size).transpose(1, 0, 2),
        GROUP,
        0,
        0,
        tiled=True,
    ).reshape(length, head_size)

    def to_groups(stack):
        m = stack.shape[0]
        shaped = stack.reshape(m, Z, PN, local_count, head_size).transpose(2, 0, 1, 3, 4)
        got = lax.all_to_all(shaped, "hp", 0, 0, tiled=True)
        got = jnp.take(got, relative, axis=2)
        return got.transpose(2, 1, 3, 0, 4).reshape(Z, m, local_count, quarter)

    attended_rel = to_groups(mixed[None])
    attn_blocks = ring_gather(attn_low)
    out_sent = send_grads(
        tn([attended_rel[k, 0] for k in range(Z)], [b[None] for b in attn_blocks], rep, side)
    )

    query_grad, key_grad, value_grad = attend_back(
        query_row, grad_row, key_row, value_row, begin_line, log_sums, score_scale
    )
    query_turn, key_turn = rope(query_grad.astype(f32), -1.0), rope(key_grad.astype(f32), -1.0)
    gain_query = jnp.sum(query_turn * query_hat, axis=0)
    gain_key = jnp.sum(key_turn * key_hat, axis=0)
    query_turn, key_turn = query_turn * gains_head[0], key_turn * gains_head[1]
    dots = sum_group(
        jnp.stack([jnp.sum(query_turn * query_hat, -1), jnp.sum(key_turn * key_hat, -1)])
    )
    dots = dots / model_width
    query_back = ((query_turn - query_hat * dots[0][:, None]) * invs[0][:, None]).astype(bf16)
    key_back = ((key_turn - key_hat * dots[1][:, None]) * invs[1][:, None]).astype(bf16)

    back_rel = to_groups(jnp.stack([query_back, key_back, value_grad]))
    input_grad = resid_grad + ring_scatter(lambda k: nt(back_rel[k], w_qkv))

    back_row = jnp.concatenate([query_back, key_back, value_grad], axis=1)
    heads_grad = mm_tn(tokens_row, back_row).astype(bf16)
    heads_grad = heads_grad.reshape(D, PN, S, Z, rows, 3, head_size).transpose(2, 3, 1, 5, 0, 4, 6)
    heads_sum = sum_seq_scatter(heads_grad)
    heads_sent = lax.all_to_all(
        heads_sum.reshape(group, 3, D, rows, head_size), GROUP, 0, 0, tiled=True
    ).reshape(Z, PN, 3, D, rows, head_size)
    heads_sent = heads_sent.transpose(2, 3, 0, 4, 1, 5).reshape(3 * square, rows, side)

    spots = jnp.zeros((2, model_width), f32)
    spots = lax.dynamic_update_slice(spots, jnp.stack([gain_query, gain_key]), (0, head * head_size))
    gain_local = jnp.concatenate([jnp.stack([gain_attn_grad, gain_mlp_grad]), spots])
    shares = lax.all_to_all(gain_local.reshape(n, -1), EVERY, 0, 0, tiled=True)
    share = jnp.sum(shares, axis=0)
    gain_grads = lax.all_to_all(
        jnp.broadcast_to(share, (n, share.shape[0])), EVERY, 0, 0, tiled=True
    ).reshape(gain_local.shape)

    flat = [a.reshape(-1, rows, side) for a in (heads_sent, out_sent, gateup_sent, down_sent)]
    sent = jnp.concatenate(flat, axis=0)
    order = [number[: 3 * square], out_list, gateup_list.reshape(-1), down_list.reshape(-1)]
    where_is = jnp.zeros((total_blocks,), jnp.int32).at[jnp.concatenate(order)].set(number)
    to_slots = jnp.take(sent, where_is[owner_map], axis=0)
    got = lax.all_to_all(to_slots, EVERY, 0, 0, tiled=True)
    got = got.reshape(Z, PN, S, slots, rows, side).transpose(3, 1, 2, 0, 4, 5)
    grad_slots, left_new, right_new, new_weights = shampoo(
        got.reshape(slots, side, side), left_stats, right_stats, left_root, right_root, weights
    )
    new_gains = norm_gains - gain_rate * gain_grads * lax.rsqrt(
        jnp.mean(gain_grads * gain_grads, axis=1, keepdims=True) + epsilon
    )
    return (
        output,
        input_grad[None],
        grad_slots,
        left_new,
        right_new,
        new_weights,
        gain_grads,
        new_gains,
    )


def solution(mesh):
    heads, seqs = mesh.shape["head"], mesh.shape["seq"]
    fine = Mesh(mesh.devices.reshape(Z, heads // Z, seqs), EVERY)
    tok = P("seq", GROUP, None)
    slot = P(EVERY, None, None)
    return jax.shard_map(
        body,
        mesh=fine,
        in_specs=(tok, tok, P("seq", GROUP), P(), slot, P(), slot, slot, slot, slot),
        out_specs=(tok, tok, slot, slot, slot, slot, P(), P()),
        check_vma=False,
    )
```

```python
import functools

import jax
import jax.numpy as jnp
from jax import lax
from jax.experimental import pallas as pl
from jax.experimental.pallas import tpu as pltpu
from jax.sharding import Mesh
from jax.sharding import PartitionSpec as P

FF = 8192
HEADS = 16
SEGMAX = 1024
QB = 256
Z = 4

epsilon = 1e-06
rope_base = 500000.0
decay_rate = 0.5
step_rate = 0.5
gain_rate = 0.3
bf16 = jnp.bfloat16
f32 = jnp.float32
EVERY = ("hz", "hp", "seq")
GROUP = ("hz", "hp")
VMEM_LIMIT = 48 * 1024 * 1024


def mm(left_side, right_side):
    return jnp.dot(left_side, right_side, preferred_element_type=f32)


def mm_nt(left_side, right_side):
    return lax.dot_general(
        left_side, right_side, (((1,), (1,)), ((), ())), preferred_element_type=f32
    )


def mm_tn(left_side, right_side):
    return lax.dot_general(
        left_side, right_side, (((0,), (0,)), ((), ())), preferred_element_type=f32
    )


def params():
    return pltpu.CompilerParams(vmem_limit_bytes=VMEM_LIMIT)


def cost(flops, nbytes, exps=0):
    part = 0.1
    return pl.CostEstimate(
        flops=int(part * flops), bytes_accessed=int(part * nbytes), transcendentals=int(part * exps)
    )


def nbytes(*arrays):
    return sum(a.size * a.dtype.itemsize for a in arrays)


def join(refs):
    return refs[0][...] if len(refs) == 1 else jnp.concatenate([r[...] for r in refs], axis=-2)


def whole(array):
    return pl.BlockSpec(array.shape, lambda *_: (0,) * array.ndim)


def gate_up_kernel(*refs):
    *x_refs, g_ref, u_ref, gate_ref, up_ref, hidden_ref = refs
    x, side = join(x_refs), g_ref.shape[-1]
    for w_ref, y_ref in ((g_ref, gate_ref), (u_ref, up_ref)):
        total = None
        for r in range(w_ref.shape[1]):
            part = mm(x[:, r * side : (r + 1) * side], w_ref[:, r, 0].reshape(side, side))
            total = part if total is None else total + part
        y_ref[...] = total
    gate = gate_ref[...]
    hidden_ref[...] = (gate * jax.nn.sigmoid(gate) * up_ref[...]).astype(bf16)


def gate_up(xs, w):
    rep, R, C, part, side = w.shape
    count, half = sum(x.shape[0] for x in xs), C // 2
    wide = jax.ShapeDtypeStruct((count, half * side), f32)
    outs = [wide, wide, jax.ShapeDtypeStruct((count, half * side), bf16)]
    col = pl.BlockSpec((count, side), lambda c: (0, c))
    return pl.pallas_call(
        gate_up_kernel,
        grid=(half,),
        in_specs=[
            *[whole(x) for x in xs],
            pl.BlockSpec((rep, R, 1, part, side), lambda c: (0, 0, c, 0, 0)),
            pl.BlockSpec((rep, R, 1, part, side), lambda c: (0, 0, c + half, 0, 0)),
        ],
        out_specs=[col, col, col],
        out_shape=outs,
        compiler_params=params(),
        cost_estimate=cost(2 * count * R * C * side * side, nbytes(*xs, w, *outs)),
    )(*xs, w, w)


def nn_kernel(x_ref, w_ref, *refs):
    y_ref = refs[-1]
    side = w_ref.shape[-1]
    total = None
    for r in range(w_ref.shape[1]):
        part = mm(x_ref[:, r * side : (r + 1) * side], w_ref[:, r, 0].reshape(side, side))
        total = part if total is None else total + part
    y_ref[...] = total


def nn(x, w, *others, columns=None, row=None):
    rep, R, C, part, side = w.shape
    count = x.shape[0]
    if row is None:
        block, index = (rep, R, 1, part, side), lambda c: (0, 0, c, 0, 0)
        steps = columns or C
    else:
        block, index = (rep, 1, 1, part, side), lambda c: (0, c, row, 0, 0)
        steps = R
    out = jax.ShapeDtypeStruct((count, steps * side), f32)
    return pl.pallas_call(
        nn_kernel,
        grid=(steps,),
        in_specs=[pl.BlockSpec(x.shape, lambda c: (0, 0)), pl.BlockSpec(block, index)]
        + [pl.BlockSpec(memory_space=pl.ANY)] * len(others),
        out_specs=pl.BlockSpec((count, side), lambda c: (0, c)),
        out_shape=out,
        compiler_params=params(),
        cost_estimate=cost(
            2 * count * x.shape[1] * steps * side, nbytes(x, out) + 2 * x.shape[1] * steps * side
        ),
    )(x, w, *others)


def hidden_back_kernel(half, *refs):
    w_ref, gate_ref, up_ref = refs[half : half + 3]
    x, y_ref, side = join(refs[:half]), refs[-1], w_ref.shape[-1]
    total = None
    for c in range(w_ref.shape[2]):
        part = mm_nt(x[:, c * side : (c + 1) * side], w_ref[:, 0, c].reshape(side, side))
        total = part if total is None else total + part
    gate = gate_ref[...]
    sigma = jax.nn.sigmoid(gate)
    y_ref[0] = (total * up_ref[...] * sigma * (1.0 + gate * (1.0 - sigma))).astype(bf16)
    y_ref[1] = (total * gate * sigma).astype(bf16)


def hidden_back(xs, w, gate, up, *others):
    rep, R, C, part, side = w.shape
    count = gate.shape[0]
    out = jax.ShapeDtypeStruct((2, count, R * side), bf16)
    col = pl.BlockSpec((count, side), lambda r: (0, r))
    return pl.pallas_call(
        functools.partial(hidden_back_kernel, len(xs)),
        grid=(R,),
        in_specs=[
            *[whole(x) for x in xs],
            pl.BlockSpec((rep, 1, C, part, side), lambda r: (0, r, 0, 0, 0)),
            col,
            col,
            *[pl.BlockSpec(memory_space=pl.ANY)] * len(others),
        ],
        out_specs=pl.BlockSpec((2, count, side), lambda r: (0, 0, r)),
        out_shape=out,
        compiler_params=params(),
        cost_estimate=cost(2 * count * R * C * side * side, nbytes(*xs, w, gate, up, out)),
    )(*xs, w, gate, up, *others)


def nt_kernel(half, *refs):
    x, w_ref, y_ref = join(refs[:half]), refs[half], refs[-1]
    side = w_ref.shape[-1]
    per = x.shape[2] // side
    total = None
    for c in range(w_ref.shape[1] * w_ref.shape[2]):
        left = x[c // per, :, (c % per) * side : (c % per + 1) * side]
        w = w_ref[:, c // w_ref.shape[2], c % w_ref.shape[2]].reshape(side, side)
        part = mm_nt(left, w)
        total = part if total is None else total + part
    y_ref[...] = total


def nt(xs, w, *others, row=None):
    rep, R, C, part, side = w.shape
    count, depth = sum(x.shape[1] for x in xs), xs[0].shape[0] * xs[0].shape[2]
    if row is None:
        block, index = (rep, 1, depth // side, part, side), lambda r: (0, r, 0, 0, 0)
        steps = R
    else:
        block, index = (rep, R, 1, part, side), lambda r: (0, 0, row, 0, 0)
        steps = 1
    out = jax.ShapeDtypeStruct((count, steps * side), f32)
    return pl.pallas_call(
        functools.partial(nt_kernel, len(xs)),
        grid=(steps,),
        in_specs=[
            *[whole(x) for x in xs],
            pl.BlockSpec(block, index),
            *[pl.BlockSpec(memory_space=pl.ANY)] * len(others),
        ],
        out_specs=pl.BlockSpec((count, side), lambda r: (0, r)),
        out_shape=out,
        compiler_params=params(),
        cost_estimate=cost(
            2 * count * depth * steps * side, nbytes(*xs, out) + 2 * depth * steps * side
        ),
    )(*xs, w, *others)


def tn_kernel(lefts, rights, *refs):
    y_ref = refs[-1]
    rep, _, _, part, side = y_ref.shape
    left, right = join(refs[:lefts]), join(refs[lefts : lefts + rights])
    y_ref[:, 0, 0] = mm_tn(left, right[0]).astype(bf16).reshape(rep, part, side)


def tn(lefts, rights, rep, side, *others, only=None):
    R = lefts[0].shape[1] // side
    m, per = rights[0].shape[0], rights[0].shape[2] // side
    first, C = (0, m * per) if only is None else (only, per)
    out = jax.ShapeDtypeStruct((rep, R, C, side // rep, side), bf16)
    total = sum(x.shape[0] for x in lefts)
    return pl.pallas_call(
        functools.partial(tn_kernel, len(lefts), len(rights)),
        grid=(R, C),
        in_specs=[pl.BlockSpec((x.shape[0], side), lambda r, c: (0, r)) for x in lefts]
        + [
            pl.BlockSpec((1, x.shape[1], side), lambda r, c: (first + c // per, 0, c % per))
            for x in rights
        ]
        + [pl.BlockSpec(memory_space=pl.ANY)] * len(others),
        out_specs=pl.BlockSpec((rep, 1, 1, side // rep, side), lambda r, c: (0, r, c, 0, 0)),
        out_shape=out,
        compiler_params=params(),
        cost_estimate=cost(2 * total * R * C * side * side, nbytes(*lefts, *rights, out)),
    )(*lefts, *rights, *others)


def heads_kernel(half, *refs):
    y_ref = refs[-1]
    rep, _, part, width = y_ref.shape
    left = jnp.concatenate([r[...] for r in refs[:half]], axis=0)
    right = jnp.concatenate([r[...] for r in refs[half : 2 * half]], axis=0)
    y_ref[:, 0] = mm_tn(left, right).astype(bf16).reshape(rep, part, width)


def heads_tn(lefts, rights, rep, side, *others):
    count, R = lefts[0].shape[0], lefts[0].shape[1] // side
    width = rights[0].shape[1]
    out = jax.ShapeDtypeStruct((rep, R, side // rep, width), bf16)
    return pl.pallas_call(
        functools.partial(heads_kernel, len(lefts)),
        grid=(R,),
        in_specs=[pl.BlockSpec((count, side), lambda r: (0, r))] * len(lefts)
        + [pl.BlockSpec((count, width), lambda r: (0, 0))] * len(rights)
        + [pl.BlockSpec(memory_space=pl.ANY)] * len(others),
        out_specs=pl.BlockSpec((rep, 1, side // rep, width), lambda r: (0, r, 0, 0)),
        out_shape=out,
        compiler_params=params(),
        cost_estimate=cost(
            2 * count * len(lefts) * R * side * width, nbytes(*lefts, *rights, out)
        ),
    )(*lefts, *rights, *others)


def scores_of(q, k, begin, q_start, k_start, scale):
    scores = mm_nt(k, q) * scale
    key_place = k_start + lax.broadcasted_iota(jnp.int32, scores.shape, 0)
    query_place = q_start + lax.broadcasted_iota(jnp.int32, scores.shape, 1)
    return jnp.where((key_place >= begin) & (key_place <= query_place), scores, -1e30)


def window_start(i, block, window, length):
    start = jnp.clip(i * block + block - window, 0, length - window)
    return pl.multiple_of(start, 128)


def attend_kernel(scale, window, q_ref, k_ref, v_ref, b_ref, o_ref, lse_ref):
    block, length = q_ref.shape[0], k_ref.shape[0]
    i = pl.program_id(0)
    start = window_start(i, block, window, length)
    scores = scores_of(
        q_ref[...], k_ref[pl.ds(start, window), :], b_ref[...], i * block, start, scale
    )
    top = jnp.max(scores, axis=0, keepdims=True)
    expo = jnp.exp(scores - top)
    total = jnp.sum(expo, axis=0, keepdims=True)
    attention = (expo * (1.0 / total)).astype(bf16)
    o_ref[...] = mm_tn(attention, v_ref[pl.ds(start, window), :]).astype(bf16)
    lse_ref[...] = top + jnp.log(total)


def attend(q, k, v, begins, scale):
    length, width = q.shape
    window = min(QB + SEGMAX, length)
    full = pl.BlockSpec((length, width), lambda i: (0, 0))
    rows = pl.BlockSpec((QB, width), lambda i: (i, 0))
    line = pl.BlockSpec((1, QB), lambda i: (0, i))
    return pl.pallas_call(
        functools.partial(attend_kernel, scale, window),
        grid=(length // QB,),
        in_specs=[rows, full, full, line],
        out_specs=[rows, line],
        out_shape=[
            jax.ShapeDtypeStruct((length, width), bf16),
            jax.ShapeDtypeStruct((1, length), f32),
        ],
        compiler_params=params(),
        cost_estimate=cost(4 * length * window * width, 4 * nbytes(q), length * window),
    )(q, k, v, begins)


def attend_back_kernel(
    scale, window, q_ref, d_ref, k_ref, v_ref, b_ref, lse_ref, *refs
):
    dq_ref, dk_ref, dv_ref, ka, va = refs[-5:]
    block, length = q_ref.shape[0], k_ref.shape[0]
    i = pl.program_id(0)
    start = window_start(i, block, window, length)
    span = pl.ds(start, window)

    @pl.when(i == 0)
    def _():
        ka[...] = jnp.zeros_like(ka)
        va[...] = jnp.zeros_like(va)

    q, d, k = q_ref[...], d_ref[...], k_ref[span, :]
    scores = scores_of(q, k, b_ref[...], i * block, start, scale)
    attention = jnp.exp(scores - lse_ref[...])
    prob_grad = mm_nt(v_ref[span, :], d)
    center = jnp.sum(attention * prob_grad, axis=0, keepdims=True)
    score_grad = (attention * (prob_grad - center)).astype(bf16)
    dq_ref[...] = (mm_tn(score_grad, k) * scale).astype(bf16)
    ka[span, :] += mm(score_grad, q) * scale
    va[span, :] += mm(attention.astype(bf16), d)

    @pl.when(i == pl.num_programs(0) - 1)
    def _():
        dk_ref[...] = ka[...].astype(bf16)
        dv_ref[...] = va[...].astype(bf16)


def attend_back(q, d, k, v, begins, lse, scale, *others):
    length, width = q.shape
    window = min(QB + SEGMAX, length)
    full = pl.BlockSpec((length, width), lambda i: (0, 0))
    rows = pl.BlockSpec((QB, width), lambda i: (i, 0))
    line = pl.BlockSpec((1, QB), lambda i: (0, i))
    return pl.pallas_call(
        functools.partial(attend_back_kernel, scale, window),
        grid=(length // QB,),
        in_specs=[rows, rows, full, full, line, line]
        + [pl.BlockSpec(memory_space=pl.ANY)] * len(others),
        out_specs=[rows, full, full],
        out_shape=[jax.ShapeDtypeStruct((length, width), bf16)] * 3,
        scratch_shapes=[pltpu.VMEM((length, width), f32)] * 2,
        compiler_params=params(),
        cost_estimate=cost(10 * length * window * width, 8 * nbytes(q), length * window),
    )(q, d, k, v, begins, lse, *others)


def shampoo_kernel(g_ref, ls_ref, rs_ref, lr_ref, rr_ref, w_ref, go_ref, lo_ref, ro_ref, wo_ref):
    g = g_ref[0]
    go_ref[0] = g.astype(f32)
    lo_ref[0] = decay_rate * ls_ref[0] + (1.0 - decay_rate) * mm_nt(g, g)
    ro_ref[0] = decay_rate * rs_ref[0] + (1.0 - decay_rate) * mm_tn(g, g)
    middle = mm(lr_ref[0].astype(bf16), g).astype(bf16)
    wo_ref[0] = w_ref[0] - step_rate * mm(middle, rr_ref[0].astype(bf16))


def shampoo(g, *rest):
    slots, side, _ = g.shape
    spec = pl.BlockSpec((1, side, side), lambda s: (s, 0, 0))
    return pl.pallas_call(
        shampoo_kernel,
        grid=(slots,),
        in_specs=[spec] * 6,
        out_specs=[spec] * 4,
        out_shape=[jax.ShapeDtypeStruct(g.shape, f32)] * 4,
        compiler_params=params(),
        cost_estimate=cost(8 * slots * side**3, 38 * g.size),
    )(g, *rest)


def rms_norm(values, gain_vec):
    return (
        values * lax.rsqrt(jnp.mean(values * values, axis=-1, keepdims=True) + epsilon) * gain_vec
    )


def begins_of(segment_row):
    length = segment_row.shape[0]
    indices = jnp.arange(length, dtype=jnp.int32)
    earlier = jnp.concatenate([jnp.full((1,), -1, jnp.int32), segment_row[:-1]])
    return lax.cummax(jnp.where(segment_row != earlier, indices, 0), axis=0)


UP = [(i, (i + 1) % Z) for i in range(Z)]


def ring_gather(block, *others):
    blocks = [block]
    for k in range(Z - 1):
        got = lax.ppermute(blocks[-1], "hz", UP)
        blocks.append(after(got, others[k]) if k < len(others) else got)
    return blocks


def ring_scatter(part_of):
    total = part_of(1).astype(bf16)
    for k in (2, 3):
        total = (lax.ppermute(total, "hz", UP).astype(f32) + part_of(k)).astype(bf16)
    return lax.ppermute(total, "hz", UP).astype(f32) + part_of(0)


def none_kernel(*refs):
    pass


def after(value, *others):
    anywhere = pl.BlockSpec(memory_space=pl.ANY)
    return pl.pallas_call(
        none_kernel,
        in_specs=[anywhere] * (1 + len(others)),
        out_specs=anywhere,
        out_shape=jax.ShapeDtypeStruct(value.shape, value.dtype),
        input_output_aliases={0: 0},
    )(value, *others)


def exchange_z(part_for):
    got = [part_for(0)]
    for j in range(1, Z):
        got.append(lax.ppermute(part_for(j), "hz", [(i, (i + j) % Z) for i in range(Z)]))
    return jnp.stack(got)


def swap(value, bit):
    size = lax.axis_size("hp")
    return lax.ppermute(value, "hp", [(i, i ^ bit) for i in range(size)])


def plane_scatter(pieces):
    PN, S = lax.axis_size("hp"), lax.axis_size("seq")
    if S != 2 or PN != 4:
        return lax.psum_scatter(pieces, ("hp", "seq"), scatter_dimension=0, tiled=False)
    p = lax.axis_index("hp")
    chip = sum_seq_scatter(pieces.reshape((PN, S) + pieces.shape[1:]), 1)
    half = chip.shape[1] // 2

    def add(mine, got):
        return (mine.astype(f32) + got.astype(f32)).astype(bf16)

    def pair(values, first, second):
        return jnp.take(values, jnp.stack([p ^ first, p ^ second]), axis=0, mode="clip")

    one, two = chip[:, :half], chip[:, half:]
    one_got, two_got = swap(pair(one, 1, 3), 1), swap(pair(two, 2, 3), 2)
    one, two = add(pair(one, 0, 2), one_got), add(pair(two, 0, 1), two_got)
    one_got, two_got = swap(one[1], 2), swap(two[1], 1)
    return jnp.concatenate([add(one[0], one_got), add(two[0], two_got)])


def from_group(values):
    size = lax.axis_size(GROUP)
    spread = jnp.broadcast_to(values, (size,) + values.shape)
    return lax.all_to_all(spread, GROUP, 0, 0, tiled=True)


def sum_seq_scatter(values, axis):
    S = lax.axis_size("seq")
    if S != 2:
        return lax.psum_scatter(values, "seq", scatter_dimension=axis, tiled=False)
    c = lax.axis_index("seq")
    mine = lax.dynamic_index_in_dim(values, c, axis, keepdims=False)
    other = lax.dynamic_index_in_dim(values, 1 - c, axis, keepdims=False)
    got = lax.ppermute(other, "seq", [(0, 1), (1, 0)])
    return (mine.astype(f32) + got.astype(f32)).astype(bf16)


def body(
    tokens,
    cotangent,
    segment_ids,
    owner_map,
    weights,
    norm_gains,
    left_stats,
    right_stats,
    left_root,
    right_root,
):
    model_width = tokens.shape[2]
    local_count = tokens.shape[1]
    slots, side = weights.shape[0], weights.shape[1]
    total_blocks = owner_map.shape[0]
    PN, S = lax.axis_size("hp"), lax.axis_size("seq")
    n = Z * PN * S
    rep = PN * S
    rows = side // n
    part = Z * rows
    head_size = model_width // HEADS
    quarter = model_width // Z
    score_scale = head_size ** (-0.5)
    zi, pi = lax.axis_index("hz"), lax.axis_index("hp")
    relative = (zi - jnp.arange(Z, dtype=jnp.int32)) % Z
    inputs = tokens[0]

    def zero_of(value):
        entry = value[(0,) * value.ndim]
        if value.dtype == jnp.int32:
            return (entry < 0).astype(jnp.int32)
        return (entry != entry).astype(jnp.int32)

    D, F = model_width // side, FF // side
    number = jnp.arange(total_blocks, dtype=jnp.int32)
    square, tall = D * D, D * F
    qkv_list = number[: 3 * square].reshape(3, D, Z).transpose(2, 1, 0)
    out_list = number[3 * square : 4 * square].reshape(Z, D, 1)
    attn_list = jnp.concatenate([qkv_list, out_list], axis=2).reshape(Z, -1)
    gateup_list = number[4 * square : 4 * square + 2 * tall].reshape(2, D, Z, F // Z)
    gateup_list = gateup_list.transpose(2, 1, 0, 3).reshape(Z, -1)
    down_list = number[4 * square + 2 * tall :].reshape(Z, -1)
    inverse = jnp.zeros((total_blocks,), jnp.int32).at[owner_map].set(number)

    low = weights.astype(bf16).reshape(slots, PN, S, Z, rows, side)
    low = low.transpose(3, 1, 2, 0, 4, 5).reshape(n * slots, rows, side)
    spread = lax.all_to_all(low, EVERY, 0, 0, tiled=True)
    tokens_g = lax.all_gather(inputs, "hz", axis=0, tiled=True)

    group = Z * PN
    own_ids = segment_ids + zero_of(tokens_g)
    row_ids = from_group(own_ids[0]).reshape(-1)
    length = row_ids.shape[0]

    def fetch(numbers, *others):
        places = inverse[numbers.reshape(-1)]
        for other in others:
            places = places + zero_of(other)
        picked = jnp.take(spread, places, axis=0, mode="clip")
        got = lax.all_to_all(picked, "hz", 0, 0, tiled=True)
        return got.reshape(Z, -1, rows, side).transpose(1, 0, 2, 3).reshape(-1, part, side)

    def all_plane(got, R):
        got = lax.all_gather(got, ("hp", "seq"), axis=0, tiled=False)
        return got.reshape(rep, R, -1, part, side)

    got_attn = fetch(attn_list, tokens_g)
    w_attn = all_plane(got_attn, D)
    def fetch_beside(numbers, other):
        def part_for(j):
            wanted = lax.dynamic_index_in_dim(numbers, (zi + j) % Z, 0, keepdims=False)
            return jnp.take(spread, inverse[wanted] + zero_of(other), axis=0, mode="clip")

        got = jnp.take(exchange_z(part_for), relative, axis=0, mode="clip")
        return got.transpose(1, 0, 2, 3).reshape(-1, part, side)

    w_gateup = all_plane(fetch_beside(gateup_list, got_attn), D)

    begins = begins_of(row_ids)
    places = jnp.arange(length, dtype=jnp.int32) - begins
    half_size = head_size // 2
    frequency = rope_base ** (-2.0 * jnp.arange(half_size, dtype=f32) / head_size)
    angles = places.astype(f32)[:, None] * frequency[None, :]
    cosine, sine = jnp.cos(angles), jnp.sin(angles)
    group_tokens = Z * local_count

    def rope(values, sign):
        first, second = values[:, :half_size], values[:, half_size:]
        return jnp.concatenate(
            [first * cosine - second * sine * sign, second * cosine + first * sine * sign], axis=-1
        )

    head = zi * PN + pi
    gains_head = lax.dynamic_slice_in_dim(norm_gains[2:4], head * head_size, head_size, axis=1)

    def to_heads(stack):
        m = stack.shape[0]
        shaped = stack.reshape(m, Z, local_count, PN, head_size).transpose(3, 0, 1, 2, 4)
        got = lax.all_to_all(shaped, "hp", 0, 0, tiled=True)
        return got.transpose(1, 2, 0, 3, 4).reshape(m, length, head_size)

    def to_groups(stack):
        m = stack.shape[0]
        shaped = stack.reshape(m, Z, PN, local_count, head_size).transpose(2, 0, 1, 3, 4)
        got = lax.all_to_all(shaped, "hp", 0, 0, tiled=True)
        return got.transpose(1, 2, 3, 0, 4).reshape(m, group_tokens, quarter)

    raw = nn(tokens_g, w_attn, columns=3)
    raw_three = raw.reshape(group_tokens, 3, quarter).transpose(1, 0, 2)
    squares = jnp.sum(raw_three[:2] * raw_three[:2], axis=-1)
    squares = from_group(squares).reshape(Z, PN, 2, Z, local_count)
    squares = jnp.sum(squares, axis=0).transpose(1, 2, 0, 3).reshape(2, length, 1)
    raw_row = to_heads(raw_three.astype(bf16))
    invs = lax.rsqrt(squares / model_width + epsilon)
    query_hat, key_hat = (raw_row[i].astype(f32) * invs[i] for i in range(2))
    query_row = rope(query_hat * gains_head[0], 1.0).astype(bf16)
    key_row = rope(key_hat * gains_head[1], 1.0).astype(bf16)
    value_row = raw_row[2]

    got_down = fetch_beside(down_list, raw_row)
    w_down = all_plane(after(got_down, w_gateup), F // Z)

    begin_line = begins[None, :]
    mixed, log_sums = attend(query_row, key_row, value_row, begin_line, score_scale)
    attended = to_groups(mixed[None]).reshape(Z, local_count, quarter)
    attended_rel = jnp.take(attended, relative, axis=0, mode="clip")
    attn_raw = ring_scatter(
        lambda k: nn(attended_rel[k], w_attn, *([got_down] if k == 2 else []), row=3)
    )
    resid = inputs.astype(f32) + rms_norm(attn_raw, norm_gains[0])

    resid_blocks = ring_gather(resid.astype(bf16))

    tokens_z = tokens_g.reshape(Z, local_count, model_width)
    middle = local_count // 2
    tok_one, tok_two = after(tokens_z[:, :middle], resid), after(tokens_z[:, middle:], resid)
    tok_one = jnp.stack([tok_one, swap(tok_one, 1)])
    tok_two = jnp.stack([tok_two, swap(tok_two, 2)])
    tok_parts = [tok_one, swap(tok_one, 2), tok_two, swap(tok_two, 1)]
    tok_parts = [t.reshape(-1, model_width) for t in tok_parts]
    tok_near, tok_far = tok_parts[::2], tok_parts[1::2]
    pairs = [resid_blocks[:2], resid_blocks[2:]]
    gates, ups, hiddens = zip(*[gate_up(pair, w_gateup) for pair in pairs])

    def entry(halves, k):
        return halves[k // 2][k % 2 * local_count : (k % 2 + 1) * local_count]

    downs = [nn(hiddens[0], w_down), nn(hiddens[1], w_down, *tok_near)]
    down_raw = ring_scatter(lambda k: entry(downs, k))
    output = (resid + rms_norm(down_raw, norm_gains[1])).astype(bf16)[None]

    upstream = cotangent[0].astype(f32)
    _, down_norm_back = jax.vjp(rms_norm, down_raw, norm_gains[1])
    down_grad, gain_mlp_grad = down_norm_back(upstream)
    down_blocks = ring_gather(down_grad.astype(bf16))
    gateup_grads = [
        hidden_back(down_blocks[2 * i : 2 * i + 2], w_down, gates[i], ups[i], *[[], tok_far][i])
        for i in range(2)
    ]
    def spread_z(summed):
        summed = summed.reshape(-1, Z, rows, side)
        return exchange_z(
            lambda j: lax.dynamic_index_in_dim(summed, (zi + j) % Z, 1, keepdims=False)
        )

    def blocks_of(pieces):
        return pieces.reshape(rep, -1, part, side)

    def sum_plane(pieces):
        return lax.psum_scatter(
            blocks_of(pieces), ("hp", "seq"), scatter_dimension=0, tiled=False
        )

    down_pieces = tn(hiddens, [b[None] for b in down_blocks], rep, side)
    gate_pieces = tn(resid_blocks, gateup_grads, rep, side, only=0)
    up_pieces = tn(resid_blocks, gateup_grads, rep, side, only=1)
    gate_sum = sum_plane(gate_pieces)
    up_sum = sum_plane(up_pieces)
    down_sum = sum_plane(down_pieces)
    resid_parts = [nt([grads], w_gateup) for grads in gateup_grads]
    resid_grad = upstream + ring_scatter(lambda k: entry(resid_parts, k))

    _, attn_norm_back = jax.vjp(rms_norm, attn_raw, norm_gains[0])
    attn_grad, gain_attn_grad = attn_norm_back(resid_grad)
    attn_low = attn_grad.astype(bf16)
    attn_blocks = ring_gather(attn_low)
    grad_rel = nt([b[None] for b in attn_blocks], w_attn, row=3).astype(bf16)
    grad_rel = grad_rel.reshape(Z, local_count, quarter)
    grad_abs = jnp.take(grad_rel, relative, axis=0, mode="clip")
    grad_row = to_heads(grad_abs.reshape(1, group_tokens, quarter))[0]
    out_pieces = tn(
        [attended_rel[k] for k in range(Z)], [b[None] for b in attn_blocks], rep, side
    )
    out_sum = plane_scatter(blocks_of(out_pieces))
    query_grad, key_grad, value_grad = attend_back(
        query_row,
        grad_row,
        key_row,
        value_row,
        begin_line,
        log_sums,
        score_scale,
    )
    gate_sent = spread_z(gate_sum)
    up_sent, down_sent = spread_z(up_sum), spread_z(down_sum)
    query_turn, key_turn = rope(query_grad.astype(f32), -1.0), rope(key_grad.astype(f32), -1.0)
    gain_query = jnp.sum(query_turn * query_hat, axis=0)
    gain_key = jnp.sum(key_turn * key_hat, axis=0)
    query_turn, key_turn = query_turn * gains_head[0], key_turn * gains_head[1]
    dots = jnp.stack([jnp.sum(query_turn * query_hat, -1), jnp.sum(key_turn * key_hat, -1)])
    dots = jnp.sum(from_group(dots).reshape(group, 2, length), axis=0) / model_width
    dots = dots[..., None]
    query_back = ((query_turn - query_hat * dots[0]) * invs[0]).astype(bf16)
    key_back = ((key_turn - key_hat * dots[1]) * invs[1]).astype(bf16)

    back_row = jnp.concatenate([query_back, key_back, value_grad], axis=1)
    by_half = back_row.reshape(Z, PN, 2, middle, 3 * head_size).transpose(1, 2, 0, 3, 4)

    def rows_of(half, *bits):
        picked = jnp.take(by_half[:, half], jnp.stack([pi ^ bit for bit in bits]), axis=0, mode="clip")
        return picked.reshape(-1, 3 * head_size)

    back_parts = [rows_of(0, 0, 1), rows_of(0, 2, 3), rows_of(1, 0, 2), rows_of(1, 1, 3)]
    heads_grad = heads_tn(tok_parts, back_parts, rep, side)
    heads_sum = sum_seq_scatter(heads_grad.reshape(PN, S, D, part, 3 * head_size), 1)
    heads_sum = heads_sum.reshape(PN, D, Z, rows, 3 * head_size).transpose(2, 0, 1, 3, 4)
    heads_sent = lax.all_to_all(
        heads_sum.reshape(group, D, rows, 3 * head_size), GROUP, 0, 0, tiled=True
    ).reshape(Z, PN, D, rows, 3, head_size)
    heads_sent = heads_sent.transpose(4, 2, 0, 3, 1, 5).reshape(3 * square, rows, side)

    back_abs = to_groups(jnp.stack([query_back, key_back, value_grad]))
    back_rel = jnp.take(
        back_abs.reshape(3, Z, local_count, quarter), relative, axis=1, mode="clip"
    )
    input_grad = resid_grad + ring_scatter(lambda k: nt([back_rel[:, k]], w_attn))

    out_sent = spread_z(out_sum)

    spots = jnp.zeros((2, model_width), f32)
    spots = lax.dynamic_update_slice(spots, jnp.stack([gain_query, gain_key]), (0, head * head_size))
    gain_local = jnp.concatenate([jnp.stack([gain_attn_grad, gain_mlp_grad]), spots])
    shares = lax.all_to_all(gain_local.reshape(n, -1), EVERY, 0, 0, tiled=True)
    share = jnp.sum(shares, axis=0)
    gain_grads = lax.all_to_all(
        jnp.broadcast_to(share, (n, share.shape[0])), EVERY, 0, 0, tiled=True
    ).reshape(gain_local.shape)

    flat = [heads_sent, out_sent, gate_sent, up_sent, down_sent]
    sent = jnp.concatenate([a.reshape(-1, rows, side) for a in flat])
    split = gateup_list.reshape(Z, D, 2, -1)
    order = [out_list, split[:, :, 0], split[:, :, 1], down_list]
    order = [jnp.take(o.reshape(Z, -1), relative, axis=0, mode="clip").reshape(-1) for o in order]
    order = jnp.concatenate([number[: 3 * square]] + order)
    where_is = jnp.zeros((total_blocks,), jnp.int32).at[order].set(number)
    to_slots = jnp.take(sent, where_is[owner_map] + zero_of(input_grad), axis=0, mode="clip")
    got = lax.all_to_all(to_slots, EVERY, 0, 0, tiled=True)
    got = got.reshape(Z, PN, S, slots, rows, side).transpose(3, 1, 2, 0, 4, 5)
    grad_slots, left_new, right_new, new_weights = shampoo(
        got.reshape(slots, side, side), left_stats, right_stats, left_root, right_root, weights
    )
    new_gains = norm_gains - gain_rate * gain_grads * lax.rsqrt(
        jnp.mean(gain_grads * gain_grads, axis=1, keepdims=True) + epsilon
    )
    return (
        output,
        input_grad[None],
        grad_slots,
        left_new,
        right_new,
        new_weights,
        gain_grads,
        new_gains,
    )


def solution(mesh):
    heads, seqs = mesh.shape["head"], mesh.shape["seq"]
    fine = Mesh(mesh.devices.reshape(Z, heads // Z, seqs), EVERY)
    tok = P("seq", GROUP, None)
    slot = P(EVERY, None, None)
    return jax.shard_map(
        body,
        mesh=fine,
        in_specs=(tok, tok, P("seq", GROUP), P(), slot, P(), slot, slot, slot, slot),
        out_specs=(tok, tok, slot, slot, slot, slot, P(), P()),
        check_vma=False,
    )
```

```python
import functools

import jax
import jax.numpy as jnp
from jax import lax
from jax.experimental import pallas as pl
from jax.experimental.pallas import tpu as pltpu
from jax.sharding import Mesh
from jax.sharding import PartitionSpec as P

FF = 8192
HEADS = 16
SEGMAX = 1024
QB = 256
Z = 4

epsilon = 1e-06
rope_base = 500000.0
decay_rate = 0.5
step_rate = 0.5
gain_rate = 0.3
bf16 = jnp.bfloat16
f32 = jnp.float32
EVERY = ("hz", "hp", "seq")
GROUP = ("hz", "hp")
VMEM_LIMIT = 48 * 1024 * 1024


def mm(left_side, right_side):
    return jnp.dot(left_side, right_side, preferred_element_type=f32)


def mm_nt(left_side, right_side):
    return lax.dot_general(
        left_side, right_side, (((1,), (1,)), ((), ())), preferred_element_type=f32
    )


def mm_tn(left_side, right_side):
    return lax.dot_general(
        left_side, right_side, (((0,), (0,)), ((), ())), preferred_element_type=f32
    )


def params():
    return pltpu.CompilerParams(vmem_limit_bytes=VMEM_LIMIT)


def cost(flops, nbytes, exps=0):
    part = 0.1
    return pl.CostEstimate(
        flops=int(part * flops), bytes_accessed=int(part * nbytes), transcendentals=int(part * exps)
    )


def nbytes(*arrays):
    return sum(a.size * a.dtype.itemsize for a in arrays)


def join(refs):
    return refs[0][...] if len(refs) == 1 else jnp.concatenate([r[...] for r in refs], axis=-2)


def whole(array):
    return pl.BlockSpec(array.shape, lambda *_: (0,) * array.ndim)


def gate_up_kernel(*refs):
    *x_refs, g_ref, u_ref, gate_ref, up_ref, hidden_ref = refs
    x, side = join(x_refs), g_ref.shape[-1]
    for w_ref, y_ref in ((g_ref, gate_ref), (u_ref, up_ref)):
        total = None
        for r in range(w_ref.shape[1]):
            part = mm(x[:, r * side : (r + 1) * side], w_ref[:, r, 0].reshape(side, side))
            total = part if total is None else total + part
        y_ref[...] = total
    gate = gate_ref[...]
    hidden_ref[...] = (gate * jax.nn.sigmoid(gate) * up_ref[...]).astype(bf16)


def gate_up(xs, w):
    rep, R, C, part, side = w.shape
    count, half = sum(x.shape[0] for x in xs), C // 2
    wide = jax.ShapeDtypeStruct((count, half * side), f32)
    outs = [wide, wide, jax.ShapeDtypeStruct((count, half * side), bf16)]
    col = pl.BlockSpec((count, side), lambda c: (0, c))
    return pl.pallas_call(
        gate_up_kernel,
        grid=(half,),
        in_specs=[
            *[whole(x) for x in xs],
            pl.BlockSpec((rep, R, 1, part, side), lambda c: (0, 0, c, 0, 0)),
            pl.BlockSpec((rep, R, 1, part, side), lambda c: (0, 0, c + half, 0, 0)),
        ],
        out_specs=[col, col, col],
        out_shape=outs,
        compiler_params=params(),
        cost_estimate=cost(2 * count * R * C * side * side, nbytes(*xs, w, *outs)),
    )(*xs, w, w)


def nn_kernel(x_ref, w_ref, *refs):
    y_ref = refs[-1]
    side = w_ref.shape[-1]
    total = None
    for r in range(w_ref.shape[1]):
        part = mm(x_ref[:, r * side : (r + 1) * side], w_ref[:, r, 0].reshape(side, side))
        total = part if total is None else total + part
    y_ref[...] = total


def nn(x, w, *others, columns=None, row=None):
    rep, R, C, part, side = w.shape
    count = x.shape[0]
    if row is None:
        block, index = (rep, R, 1, part, side), lambda c: (0, 0, c, 0, 0)
        steps = columns or C
    else:
        block, index = (rep, 1, 1, part, side), lambda c: (0, c, row, 0, 0)
        steps = R
    out = jax.ShapeDtypeStruct((count, steps * side), f32)
    return pl.pallas_call(
        nn_kernel,
        grid=(steps,),
        in_specs=[pl.BlockSpec(x.shape, lambda c: (0, 0)), pl.BlockSpec(block, index)]
        + [pl.BlockSpec(memory_space=pl.ANY)] * len(others),
        out_specs=pl.BlockSpec((count, side), lambda c: (0, c)),
        out_shape=out,
        compiler_params=params(),
        cost_estimate=cost(
            2 * count * x.shape[1] * steps * side, nbytes(x, out) + 2 * x.shape[1] * steps * side
        ),
    )(x, w, *others)


def hidden_back_kernel(half, *refs):
    w_ref, gate_ref, up_ref = refs[half : half + 3]
    x, y_ref, side = join(refs[:half]), refs[-1], w_ref.shape[-1]
    total = None
    for c in range(w_ref.shape[2]):
        part = mm_nt(x[:, c * side : (c + 1) * side], w_ref[:, 0, c].reshape(side, side))
        total = part if total is None else total + part
    gate = gate_ref[...]
    sigma = jax.nn.sigmoid(gate)
    y_ref[0] = (total * up_ref[...] * sigma * (1.0 + gate * (1.0 - sigma))).astype(bf16)
    y_ref[1] = (total * gate * sigma).astype(bf16)


def hidden_back(xs, w, gate, up, *others):
    rep, R, C, part, side = w.shape
    count = gate.shape[0]
    out = jax.ShapeDtypeStruct((2, count, R * side), bf16)
    col = pl.BlockSpec((count, side), lambda r: (0, r))
    return pl.pallas_call(
        functools.partial(hidden_back_kernel, len(xs)),
        grid=(R,),
        in_specs=[
            *[whole(x) for x in xs],
            pl.BlockSpec((rep, 1, C, part, side), lambda r: (0, r, 0, 0, 0)),
            col,
            col,
            *[pl.BlockSpec(memory_space=pl.ANY)] * len(others),
        ],
        out_specs=pl.BlockSpec((2, count, side), lambda r: (0, 0, r)),
        out_shape=out,
        compiler_params=params(),
        cost_estimate=cost(2 * count * R * C * side * side, nbytes(*xs, w, gate, up, out)),
    )(*xs, w, gate, up, *others)


def nt_kernel(half, *refs):
    x, w_ref, y_ref = join(refs[:half]), refs[half], refs[-1]
    side = w_ref.shape[-1]
    per = x.shape[2] // side
    total = None
    for c in range(w_ref.shape[1] * w_ref.shape[2]):
        left = x[c // per, :, (c % per) * side : (c % per + 1) * side]
        w = w_ref[:, c // w_ref.shape[2], c % w_ref.shape[2]].reshape(side, side)
        part = mm_nt(left, w)
        total = part if total is None else total + part
    y_ref[...] = total


def nt(xs, w, *others, row=None):
    rep, R, C, part, side = w.shape
    count, depth = sum(x.shape[1] for x in xs), xs[0].shape[0] * xs[0].shape[2]
    if row is None:
        block, index = (rep, 1, depth // side, part, side), lambda r: (0, r, 0, 0, 0)
        steps = R
    else:
        block, index = (rep, R, 1, part, side), lambda r: (0, 0, row, 0, 0)
        steps = 1
    out = jax.ShapeDtypeStruct((count, steps * side), f32)
    return pl.pallas_call(
        functools.partial(nt_kernel, len(xs)),
        grid=(steps,),
        in_specs=[
            *[whole(x) for x in xs],
            pl.BlockSpec(block, index),
            *[pl.BlockSpec(memory_space=pl.ANY)] * len(others),
        ],
        out_specs=pl.BlockSpec((count, side), lambda r: (0, r)),
        out_shape=out,
        compiler_params=params(),
        cost_estimate=cost(
            2 * count * depth * steps * side, nbytes(*xs, out) + 2 * depth * steps * side
        ),
    )(*xs, w, *others)


def tn_kernel(lefts, rights, *refs):
    y_ref = refs[-1]
    rep, _, _, part, side = y_ref.shape
    left, right = join(refs[:lefts]), join(refs[lefts : lefts + rights])
    y_ref[:, 0, 0] = mm_tn(left, right[0]).astype(bf16).reshape(rep, part, side)


def tn(lefts, rights, rep, side, *others, only=None, spare=0, base=None):
    R = lefts[0].shape[1] // side
    m, per = rights[0].shape[0], rights[0].shape[2] // side
    first, C = (0, m * per) if only is None else (only, per)
    out = jax.ShapeDtypeStruct((rep, R + spare, C, side // rep, side), bf16)
    start, aliases = 0, {}
    if base is not None:
        out = jax.ShapeDtypeStruct(base.shape, base.dtype)
        start, others = base.shape[1] - R, (*others, base)
        aliases = {len(lefts) + len(rights) + len(others) - 1: 0}
    total = sum(x.shape[0] for x in lefts)
    return pl.pallas_call(
        functools.partial(tn_kernel, len(lefts), len(rights)),
        grid=(R, C),
        in_specs=[pl.BlockSpec((x.shape[0], side), lambda r, c: (0, r)) for x in lefts]
        + [
            pl.BlockSpec((1, x.shape[1], side), lambda r, c: (first + c // per, 0, c % per))
            for x in rights
        ]
        + [pl.BlockSpec(memory_space=pl.ANY)] * len(others),
        out_specs=pl.BlockSpec((rep, 1, 1, side // rep, side), lambda r, c: (0, start + r, c, 0, 0)),
        out_shape=out,
        input_output_aliases=aliases,
        compiler_params=params(),
        cost_estimate=cost(2 * total * R * C * side * side, nbytes(*lefts, *rights, out)),
    )(*lefts, *rights, *others)


def heads_kernel(half, *refs):
    y_ref = refs[-1]
    rep, _, part, width = y_ref.shape
    left = jnp.concatenate([r[...] for r in refs[:half]], axis=0)
    right = jnp.concatenate([r[...] for r in refs[half : 2 * half]], axis=0)
    y_ref[:, 0] = mm_tn(left, right).astype(bf16).reshape(rep, part, width)


def heads_tn(lefts, rights, rep, side, *others):
    count, R = lefts[0].shape[0], lefts[0].shape[1] // side
    width = rights[0].shape[1]
    out = jax.ShapeDtypeStruct((rep, R, side // rep, width), bf16)
    return pl.pallas_call(
        functools.partial(heads_kernel, len(lefts)),
        grid=(R,),
        in_specs=[pl.BlockSpec((count, side), lambda r: (0, r))] * len(lefts)
        + [pl.BlockSpec((count, width), lambda r: (0, 0))] * len(rights)
        + [pl.BlockSpec(memory_space=pl.ANY)] * len(others),
        out_specs=pl.BlockSpec((rep, 1, side // rep, width), lambda r: (0, r, 0, 0)),
        out_shape=out,
        compiler_params=params(),
        cost_estimate=cost(
            2 * count * len(lefts) * R * side * width, nbytes(*lefts, *rights, out)
        ),
    )(*lefts, *rights, *others)


def scores_of(q, k, begin, q_start, k_start, scale):
    scores = mm_nt(k, q) * scale
    key_place = k_start + lax.broadcasted_iota(jnp.int32, scores.shape, 0)
    query_place = q_start + lax.broadcasted_iota(jnp.int32, scores.shape, 1)
    return jnp.where((key_place >= begin) & (key_place <= query_place), scores, -1e30)


def window_start(i, block, window, length):
    start = jnp.clip(i * block + block - window, 0, length - window)
    return pl.multiple_of(start, 128)


def attend_kernel(scale, window, q_ref, k_ref, v_ref, b_ref, o_ref, lse_ref):
    block, length = q_ref.shape[0], k_ref.shape[0]
    i = pl.program_id(0)
    start = window_start(i, block, window, length)
    scores = scores_of(
        q_ref[...], k_ref[pl.ds(start, window), :], b_ref[...], i * block, start, scale
    )
    top = jnp.max(scores, axis=0, keepdims=True)
    expo = jnp.exp(scores - top)
    total = jnp.sum(expo, axis=0, keepdims=True)
    attention = (expo * (1.0 / total)).astype(bf16)
    o_ref[...] = mm_tn(attention, v_ref[pl.ds(start, window), :]).astype(bf16)
    lse_ref[...] = top + jnp.log(total)


def attend(q, k, v, begins, scale):
    length, width = q.shape
    window = min(QB + SEGMAX, length)
    full = pl.BlockSpec((length, width), lambda i: (0, 0))
    rows = pl.BlockSpec((QB, width), lambda i: (i, 0))
    line = pl.BlockSpec((1, QB), lambda i: (0, i))
    return pl.pallas_call(
        functools.partial(attend_kernel, scale, window),
        grid=(length // QB,),
        in_specs=[rows, full, full, line],
        out_specs=[rows, line],
        out_shape=[
            jax.ShapeDtypeStruct((length, width), bf16),
            jax.ShapeDtypeStruct((1, length), f32),
        ],
        compiler_params=params(),
        cost_estimate=cost(4 * length * window * width, 4 * nbytes(q), length * window),
    )(q, k, v, begins)


def attend_back_kernel(
    scale, window, q_ref, d_ref, k_ref, v_ref, b_ref, lse_ref, *refs
):
    dq_ref, dk_ref, dv_ref, ka, va = refs[-5:]
    block, length = q_ref.shape[0], k_ref.shape[0]
    i = pl.program_id(0)
    start = window_start(i, block, window, length)
    span = pl.ds(start, window)

    @pl.when(i == 0)
    def _():
        ka[...] = jnp.zeros_like(ka)
        va[...] = jnp.zeros_like(va)

    q, d, k = q_ref[...], d_ref[...], k_ref[span, :]
    scores = scores_of(q, k, b_ref[...], i * block, start, scale)
    attention = jnp.exp(scores - lse_ref[...])
    prob_grad = mm_nt(v_ref[span, :], d)
    center = jnp.sum(attention * prob_grad, axis=0, keepdims=True)
    score_grad = (attention * (prob_grad - center)).astype(bf16)
    dq_ref[...] = (mm_tn(score_grad, k) * scale).astype(bf16)
    ka[span, :] += mm(score_grad, q) * scale
    va[span, :] += mm(attention.astype(bf16), d)

    @pl.when(i == pl.num_programs(0) - 1)
    def _():
        dk_ref[...] = ka[...].astype(bf16)
        dv_ref[...] = va[...].astype(bf16)


def attend_back(q, d, k, v, begins, lse, scale, *others):
    length, width = q.shape
    window = min(QB + SEGMAX, length)
    full = pl.BlockSpec((length, width), lambda i: (0, 0))
    rows = pl.BlockSpec((QB, width), lambda i: (i, 0))
    line = pl.BlockSpec((1, QB), lambda i: (0, i))
    return pl.pallas_call(
        functools.partial(attend_back_kernel, scale, window),
        grid=(length // QB,),
        in_specs=[rows, rows, full, full, line, line]
        + [pl.BlockSpec(memory_space=pl.ANY)] * len(others),
        out_specs=[rows, full, full],
        out_shape=[jax.ShapeDtypeStruct((length, width), bf16)] * 3,
        scratch_shapes=[pltpu.VMEM((length, width), f32)] * 2,
        compiler_params=params(),
        cost_estimate=cost(10 * length * window * width, 8 * nbytes(q), length * window),
    )(q, d, k, v, begins, lse, *others)


def shampoo_kernel(g_ref, ls_ref, rs_ref, lr_ref, rr_ref, w_ref, go_ref, lo_ref, ro_ref, wo_ref):
    g = g_ref[0]
    go_ref[0] = g.astype(f32)
    lo_ref[0] = decay_rate * ls_ref[0] + (1.0 - decay_rate) * mm_nt(g, g)
    ro_ref[0] = decay_rate * rs_ref[0] + (1.0 - decay_rate) * mm_tn(g, g)
    middle = mm(lr_ref[0].astype(bf16), g).astype(bf16)
    wo_ref[0] = w_ref[0] - step_rate * mm(middle, rr_ref[0].astype(bf16))


def shampoo(g, *rest):
    slots, side, _ = g.shape
    spec = pl.BlockSpec((1, side, side), lambda s: (s, 0, 0))
    return pl.pallas_call(
        shampoo_kernel,
        grid=(slots,),
        in_specs=[spec] * 6,
        out_specs=[spec] * 4,
        out_shape=[jax.ShapeDtypeStruct(g.shape, f32)] * 4,
        compiler_params=params(),
        cost_estimate=cost(8 * slots * side**3, 38 * g.size),
    )(g, *rest)


def rms_norm(values, gain_vec):
    return (
        values * lax.rsqrt(jnp.mean(values * values, axis=-1, keepdims=True) + epsilon) * gain_vec
    )


def begins_of(segment_row):
    length = segment_row.shape[0]
    indices = jnp.arange(length, dtype=jnp.int32)
    earlier = jnp.concatenate([jnp.full((1,), -1, jnp.int32), segment_row[:-1]])
    return lax.cummax(jnp.where(segment_row != earlier, indices, 0), axis=0)


UP = [(i, (i + 1) % Z) for i in range(Z)]


def ring_gather(block, first_use=None):
    blocks = [block]
    for k in range(Z - 1):
        blocks.append(lax.ppermute(blocks[-1], "hz", UP))
        if k == 0 and first_use:
            used = first_use(blocks[:2])
        if k == 1 and first_use:
            blocks[2] = after(blocks[2], used[0])
    return (blocks, used) if first_use else blocks


def ring_scatter(part_of):
    total = part_of(1).astype(bf16)
    for k in (2, 3):
        total = (lax.ppermute(total, "hz", UP).astype(f32) + part_of(k)).astype(bf16)
    return lax.ppermute(total, "hz", UP).astype(f32) + part_of(0)


def none_kernel(*refs):
    pass


def after(value, *others):
    anywhere = pl.BlockSpec(memory_space=pl.ANY)
    return pl.pallas_call(
        none_kernel,
        in_specs=[anywhere] * (1 + len(others)),
        out_specs=anywhere,
        out_shape=jax.ShapeDtypeStruct(value.shape, value.dtype),
        input_output_aliases={0: 0},
    )(value, *others)


def exchange_z(part_for):
    got = [part_for(0)]
    for j in range(1, Z):
        got.append(lax.ppermute(part_for(j), "hz", [(i, (i + j) % Z) for i in range(Z)]))
    return jnp.stack(got)


def swap(value, bit):
    size = lax.axis_size("hp")
    return lax.ppermute(value, "hp", [(i, i ^ bit) for i in range(size)])


def plane_scatter(pieces):
    PN, S = lax.axis_size("hp"), lax.axis_size("seq")
    if S != 2 or PN != 4:
        return lax.psum_scatter(pieces, ("hp", "seq"), scatter_dimension=0, tiled=False)
    p = lax.axis_index("hp")
    chip = sum_seq_scatter(pieces.reshape((PN, S) + pieces.shape[1:]), 1)
    half = chip.shape[1] // 2

    def add(mine, got):
        return (mine.astype(f32) + got.astype(f32)).astype(bf16)

    def pair(values, first, second):
        return jnp.take(values, jnp.stack([p ^ first, p ^ second]), axis=0, mode="clip")

    one, two = chip[:, :half], chip[:, half:]
    one_got, two_got = swap(pair(one, 1, 3), 1), swap(pair(two, 2, 3), 2)
    one, two = add(pair(one, 0, 2), one_got), add(pair(two, 0, 1), two_got)
    one_got, two_got = swap(one[1], 2), swap(two[1], 1)
    return jnp.concatenate([add(one[0], one_got), add(two[0], two_got)])


def from_group(values):
    size = lax.axis_size(GROUP)
    spread = jnp.broadcast_to(values, (size,) + values.shape)
    return lax.all_to_all(spread, GROUP, 0, 0, tiled=True)


def sum_seq_scatter(values, axis):
    S = lax.axis_size("seq")
    if S != 2:
        return lax.psum_scatter(values, "seq", scatter_dimension=axis, tiled=False)
    c = lax.axis_index("seq")
    mine = lax.dynamic_index_in_dim(values, c, axis, keepdims=False)
    other = lax.dynamic_index_in_dim(values, 1 - c, axis, keepdims=False)
    got = lax.ppermute(other, "seq", [(0, 1), (1, 0)])
    return (mine.astype(f32) + got.astype(f32)).astype(bf16)


def body(
    tokens,
    cotangent,
    segment_ids,
    owner_map,
    weights,
    norm_gains,
    left_stats,
    right_stats,
    left_root,
    right_root,
):
    model_width = tokens.shape[2]
    local_count = tokens.shape[1]
    slots, side = weights.shape[0], weights.shape[1]
    total_blocks = owner_map.shape[0]
    PN, S = lax.axis_size("hp"), lax.axis_size("seq")
    n = Z * PN * S
    rep = PN * S
    rows = side // n
    part = Z * rows
    head_size = model_width // HEADS
    quarter = model_width // Z
    score_scale = head_size ** (-0.5)
    zi, pi = lax.axis_index("hz"), lax.axis_index("hp")
    relative = (zi - jnp.arange(Z, dtype=jnp.int32)) % Z
    inputs = tokens[0]

    def zero_of(value):
        entry = value[(0,) * value.ndim]
        if value.dtype == jnp.int32:
            return (entry < 0).astype(jnp.int32)
        return (entry != entry).astype(jnp.int32)

    D, F = model_width // side, FF // side
    number = jnp.arange(total_blocks, dtype=jnp.int32)
    square, tall = D * D, D * F
    qkv_list = number[: 3 * square].reshape(3, D, Z).transpose(2, 1, 0)
    out_list = number[3 * square : 4 * square].reshape(Z, D, 1)
    attn_list = jnp.concatenate([qkv_list, out_list], axis=2).reshape(Z, -1)
    gateup_list = number[4 * square : 4 * square + 2 * tall].reshape(2, D, Z, F // Z)
    gateup_list = gateup_list.transpose(2, 1, 0, 3).reshape(Z, -1)
    down_list = number[4 * square + 2 * tall :].reshape(Z, -1)
    inverse = jnp.zeros((total_blocks,), jnp.int32).at[owner_map].set(number)

    low = weights.astype(bf16).reshape(slots, PN, S, Z, rows, side)
    low = low.transpose(3, 1, 2, 0, 4, 5).reshape(n * slots, rows, side)
    spread = lax.all_to_all(low, EVERY, 0, 0, tiled=True)
    tokens_g = lax.all_gather(inputs, "hz", axis=0, tiled=True)

    group = Z * PN
    own_ids = segment_ids + zero_of(tokens_g)
    row_ids = from_group(own_ids[0]).reshape(-1)
    length = row_ids.shape[0]

    def fetch(numbers, *others):
        places = inverse[numbers.reshape(-1)]
        for other in others:
            places = places + zero_of(other)
        picked = jnp.take(spread, places, axis=0, mode="clip")
        got = lax.all_to_all(picked, "hz", 0, 0, tiled=True)
        return got.reshape(Z, -1, rows, side).transpose(1, 0, 2, 3).reshape(-1, part, side)

    def all_plane(got, R):
        got = lax.all_gather(got, ("hp", "seq"), axis=0, tiled=False)
        return got.reshape(rep, R, -1, part, side)

    got_attn = fetch(attn_list, tokens_g)
    w_attn = all_plane(got_attn, D)
    def fetch_beside(numbers, other):
        def part_for(j):
            wanted = lax.dynamic_index_in_dim(numbers, (zi + j) % Z, 0, keepdims=False)
            return jnp.take(spread, inverse[wanted] + zero_of(other), axis=0, mode="clip")

        got = jnp.take(exchange_z(part_for), relative, axis=0, mode="clip")
        return got.transpose(1, 0, 2, 3).reshape(-1, part, side)

    w_gateup = all_plane(fetch_beside(gateup_list, got_attn), D)

    begins = begins_of(row_ids)
    places = jnp.arange(length, dtype=jnp.int32) - begins
    half_size = head_size // 2
    frequency = rope_base ** (-2.0 * jnp.arange(half_size, dtype=f32) / head_size)
    angles = places.astype(f32)[:, None] * frequency[None, :]
    cosine, sine = jnp.cos(angles), jnp.sin(angles)
    group_tokens = Z * local_count

    def rope(values, sign):
        first, second = values[:, :half_size], values[:, half_size:]
        return jnp.concatenate(
            [first * cosine - second * sine * sign, second * cosine + first * sine * sign], axis=-1
        )

    head = zi * PN + pi
    gains_head = lax.dynamic_slice_in_dim(norm_gains[2:4], head * head_size, head_size, axis=1)

    def to_heads(stack):
        m = stack.shape[0]
        shaped = stack.reshape(m, Z, local_count, PN, head_size).transpose(3, 0, 1, 2, 4)
        got = lax.all_to_all(shaped, "hp", 0, 0, tiled=True)
        return got.transpose(1, 2, 0, 3, 4).reshape(m, length, head_size)

    def to_groups(stack):
        m = stack.shape[0]
        shaped = stack.reshape(m, Z, PN, local_count, head_size).transpose(2, 0, 1, 3, 4)
        got = lax.all_to_all(shaped, "hp", 0, 0, tiled=True)
        return got.transpose(1, 2, 3, 0, 4).reshape(m, group_tokens, quarter)

    raw = nn(tokens_g, w_attn, columns=3)
    raw_three = raw.reshape(group_tokens, 3, quarter).transpose(1, 0, 2)
    squares = jnp.sum(raw_three[:2] * raw_three[:2], axis=-1)
    squares = from_group(squares).reshape(Z, PN, 2, Z, local_count)
    squares = jnp.sum(squares, axis=0).transpose(1, 2, 0, 3).reshape(2, length, 1)
    raw_row = to_heads(raw_three.astype(bf16))
    invs = lax.rsqrt(squares / model_width + epsilon)
    query_hat, key_hat = (raw_row[i].astype(f32) * invs[i] for i in range(2))
    query_row = rope(query_hat * gains_head[0], 1.0).astype(bf16)
    key_row = rope(key_hat * gains_head[1], 1.0).astype(bf16)
    value_row = raw_row[2]

    got_down = fetch_beside(down_list, raw_row)
    w_down = all_plane(after(got_down, w_gateup), F // Z)

    begin_line = begins[None, :]
    mixed, log_sums = attend(query_row, key_row, value_row, begin_line, score_scale)
    attended = to_groups(mixed[None]).reshape(Z, local_count, quarter)
    attended_rel = jnp.take(attended, relative, axis=0, mode="clip")
    attn_raw = ring_scatter(
        lambda k: nn(attended_rel[k], w_attn, *([got_down] if k == 2 else []), row=3)
    )
    resid = inputs.astype(f32) + rms_norm(attn_raw, norm_gains[0])

    resid_blocks, near = ring_gather(resid.astype(bf16), lambda pair: gate_up(pair, w_gateup))

    tokens_z = tokens_g.reshape(Z, local_count, model_width)
    middle = local_count // 2
    tok_one, tok_two = after(tokens_z[:, :middle], resid), after(tokens_z[:, middle:], resid)
    tok_one = jnp.stack([tok_one, swap(tok_one, 1)])
    tok_two = jnp.stack([tok_two, swap(tok_two, 2)])
    tok_parts = [tok_one, swap(tok_one, 2), tok_two, swap(tok_two, 1)]
    tok_parts = [t.reshape(-1, model_width) for t in tok_parts]
    tok_near, tok_far = tok_parts[::2], tok_parts[1::2]
    gates, ups, hiddens = zip(near, gate_up(resid_blocks[2:], w_gateup))

    def entry(halves, k):
        return halves[k // 2][k % 2 * local_count : (k % 2 + 1) * local_count]

    downs = [nn(hiddens[0], w_down), nn(hiddens[1], w_down, *tok_near)]
    down_raw = ring_scatter(lambda k: entry(downs, k))
    output = (resid + rms_norm(down_raw, norm_gains[1])).astype(bf16)[None]

    upstream = cotangent[0].astype(f32)
    _, down_norm_back = jax.vjp(rms_norm, down_raw, norm_gains[1])
    down_grad, gain_mlp_grad = down_norm_back(upstream)
    down_blocks, near = ring_gather(
        down_grad.astype(bf16),
        lambda pair: [hidden_back(pair, w_down, gates[0], ups[0])],
    )
    gateup_grads = near + [hidden_back(down_blocks[2:], w_down, gates[1], ups[1], *tok_far)]

    def spread_z(summed):
        summed = summed.reshape(-1, Z, rows, side)
        return exchange_z(
            lambda j: lax.dynamic_index_in_dim(summed, (zi + j) % Z, 1, keepdims=False)
        )

    def blocks_of(pieces):
        return pieces.reshape(rep, -1, part, side)

    def sum_plane(pieces):
        return lax.psum_scatter(
            blocks_of(pieces), ("hp", "seq"), scatter_dimension=0, tiled=False
        )

    down_pieces = tn(hiddens, [b[None] for b in down_blocks], rep, side, spare=quarter // side)
    gate_pieces = tn(resid_blocks, gateup_grads, rep, side, only=0)
    up_pieces = tn(resid_blocks, gateup_grads, rep, side, only=1)
    gate_sum = sum_plane(gate_pieces)
    up_sum = sum_plane(up_pieces)
    resid_parts = [nt([gateup_grads[0]], w_gateup), nt([gateup_grads[1]], w_gateup)]
    resid_grad = upstream + ring_scatter(lambda k: entry(resid_parts, k))

    _, attn_norm_back = jax.vjp(rms_norm, attn_raw, norm_gains[0])
    attn_grad, gain_attn_grad = attn_norm_back(resid_grad)
    attn_low = attn_grad.astype(bf16)
    attn_blocks = ring_gather(attn_low)
    grad_rel = nt([b[None] for b in attn_blocks], w_attn, row=3).astype(bf16)
    grad_rel = grad_rel.reshape(Z, local_count, quarter)
    grad_abs = jnp.take(grad_rel, relative, axis=0, mode="clip")
    grad_row = to_heads(grad_abs.reshape(1, group_tokens, quarter))[0]
    last_pieces = tn(
        [attended_rel[k] for k in range(Z)],
        [b[None] for b in attn_blocks],
        rep,
        side,
        base=down_pieces,
    )
    last_sum = sum_plane(last_pieces)
    gate_sent = spread_z(after(gate_sum, grad_abs))
    query_grad, key_grad, value_grad = attend_back(
        query_row,
        grad_row,
        key_row,
        value_row,
        begin_line,
        log_sums,
        score_scale,
    )
    query_turn, key_turn = rope(query_grad.astype(f32), -1.0), rope(key_grad.astype(f32), -1.0)
    gain_query = jnp.sum(query_turn * query_hat, axis=0)
    gain_key = jnp.sum(key_turn * key_hat, axis=0)
    query_turn, key_turn = query_turn * gains_head[0], key_turn * gains_head[1]
    dots = jnp.stack([jnp.sum(query_turn * query_hat, -1), jnp.sum(key_turn * key_hat, -1)])
    dots = jnp.sum(from_group(dots).reshape(group, 2, length), axis=0) / model_width
    up_sent, down_sent = spread_z(after(up_sum, dots)), spread_z(last_sum)
    dots = dots[..., None]
    query_back = ((query_turn - query_hat * dots[0]) * invs[0]).astype(bf16)
    key_back = ((key_turn - key_hat * dots[1]) * invs[1]).astype(bf16)

    back_row = jnp.concatenate([query_back, key_back, value_grad], axis=1)
    by_half = back_row.reshape(Z, PN, 2, middle, 3 * head_size).transpose(1, 2, 0, 3, 4)

    def rows_of(half, *bits):
        picked = jnp.take(by_half[:, half], jnp.stack([pi ^ bit for bit in bits]), axis=0, mode="clip")
        return picked.reshape(-1, 3 * head_size)

    back_parts = [rows_of(0, 0, 1), rows_of(0, 2, 3), rows_of(1, 0, 2), rows_of(1, 1, 3)]
    heads_grad = heads_tn(tok_parts, back_parts, rep, side, gate_sent)
    heads_sum = sum_seq_scatter(heads_grad.reshape(PN, S, D, part, 3 * head_size), 1)
    heads_sum = heads_sum.reshape(PN, D, Z, rows, 3 * head_size).transpose(2, 0, 1, 3, 4)
    heads_sent = lax.all_to_all(
        heads_sum.reshape(group, D, rows, 3 * head_size), GROUP, 0, 0, tiled=True
    ).reshape(Z, PN, D, rows, 3, head_size)
    heads_sent = heads_sent.transpose(4, 2, 0, 3, 1, 5).reshape(3 * square, rows, side)

    back_abs = to_groups(jnp.stack([query_back, key_back, value_grad]))
    back_rel = jnp.take(
        back_abs.reshape(3, Z, local_count, quarter), relative, axis=1, mode="clip"
    )
    near_back = nt([back_rel[:, 0], back_rel[:, 1]], w_attn, up_sent, heads_grad)
    back_parts = [near_back, nt([back_rel[:, 2], back_rel[:, 3]], w_attn)]
    input_grad = resid_grad + ring_scatter(lambda k: entry(back_parts, k))


    spots = jnp.zeros((2, model_width), f32)
    spots = lax.dynamic_update_slice(spots, jnp.stack([gain_query, gain_key]), (0, head * head_size))
    gain_local = jnp.concatenate([jnp.stack([gain_attn_grad, gain_mlp_grad]), spots])
    shares = lax.all_to_all(gain_local.reshape(n, -1), EVERY, 0, 0, tiled=True)
    share = jnp.sum(shares, axis=0)
    gain_grads = lax.all_to_all(
        jnp.broadcast_to(share, (n, share.shape[0])), EVERY, 0, 0, tiled=True
    ).reshape(gain_local.shape)

    flat = [heads_sent, gate_sent, up_sent, down_sent]
    sent = jnp.concatenate([a.reshape(-1, rows, side) for a in flat])
    split = gateup_list.reshape(Z, D, 2, -1)
    last = jnp.concatenate([down_list, out_list.reshape(Z, -1)], axis=1)
    order = [split[:, :, 0], split[:, :, 1], last]
    order = [jnp.take(o.reshape(Z, -1), relative, axis=0, mode="clip").reshape(-1) for o in order]
    order = jnp.concatenate([number[: 3 * square]] + order)
    where_is = jnp.zeros((total_blocks,), jnp.int32).at[order].set(number)
    to_slots = jnp.take(sent, where_is[owner_map] + zero_of(input_grad), axis=0, mode="clip")
    got = lax.all_to_all(to_slots, EVERY, 0, 0, tiled=True)
    got = got.reshape(Z, PN, S, slots, rows, side).transpose(3, 1, 2, 0, 4, 5)
    grad_slots, left_new, right_new, new_weights = shampoo(
        got.reshape(slots, side, side), left_stats, right_stats, left_root, right_root, weights
    )
    new_gains = norm_gains - gain_rate * gain_grads * lax.rsqrt(
        jnp.mean(gain_grads * gain_grads, axis=1, keepdims=True) + epsilon
    )
    return (
        output,
        input_grad[None],
        grad_slots,
        left_new,
        right_new,
        new_weights,
        gain_grads,
        new_gains,
    )


def solution(mesh):
    heads, seqs = mesh.shape["head"], mesh.shape["seq"]
    fine = Mesh(mesh.devices.reshape(Z, heads // Z, seqs), EVERY)
    tok = P("seq", GROUP, None)
    slot = P(EVERY, None, None)
    return jax.shard_map(
        body,
        mesh=fine,
        in_specs=(tok, tok, P("seq", GROUP), P(), slot, P(), slot, slot, slot, slot),
        out_specs=(tok, tok, slot, slot, slot, slot, P(), P()),
        check_vma=False,
    )
```

```python
import functools

import jax
import jax.numpy as jnp
from jax import lax
from jax.experimental import pallas as pl
from jax.experimental.pallas import tpu as pltpu
from jax.sharding import Mesh
from jax.sharding import PartitionSpec as P

FF = 8192
HEADS = 16
SEGMAX = 1024
QB = 256
Z = 4

epsilon = 1e-06
rope_base = 500000.0
decay_rate = 0.5
step_rate = 0.5
gain_rate = 0.3
bf16 = jnp.bfloat16
f32 = jnp.float32
EVERY = ("hz", "hp", "seq")
GROUP = ("hz", "hp")
VMEM_LIMIT = 48 * 1024 * 1024


def mm(left_side, right_side):
    return jnp.dot(left_side, right_side, preferred_element_type=f32)


def mm_nt(left_side, right_side):
    return lax.dot_general(
        left_side, right_side, (((1,), (1,)), ((), ())), preferred_element_type=f32
    )


def mm_tn(left_side, right_side):
    return lax.dot_general(
        left_side, right_side, (((0,), (0,)), ((), ())), preferred_element_type=f32
    )


def params():
    return pltpu.CompilerParams(vmem_limit_bytes=VMEM_LIMIT)


def cost(flops, nbytes, exps=0):
    part = 0.1
    return pl.CostEstimate(
        flops=int(part * flops), bytes_accessed=int(part * nbytes), transcendentals=int(part * exps)
    )


def nbytes(*arrays):
    return sum(a.size * a.dtype.itemsize for a in arrays)


def join(refs):
    return refs[0][...] if len(refs) == 1 else jnp.concatenate([r[...] for r in refs], axis=-2)


def whole(array):
    return pl.BlockSpec(array.shape, lambda *_: (0,) * array.ndim)


def gate_up_kernel(*refs):
    *x_refs, g_ref, u_ref, gate_ref, up_ref, hidden_ref = refs
    x, side = join(x_refs), g_ref.shape[-1]
    for w_ref, y_ref in ((g_ref, gate_ref), (u_ref, up_ref)):
        total = None
        for r in range(w_ref.shape[1]):
            part = mm(x[:, r * side : (r + 1) * side], w_ref[:, r, 0].reshape(side, side))
            total = part if total is None else total + part
        y_ref[...] = total
    gate = gate_ref[...]
    hidden_ref[...] = (gate * jax.nn.sigmoid(gate) * up_ref[...]).astype(bf16)


def gate_up(xs, w):
    rep, R, C, part, side = w.shape
    count, half = sum(x.shape[0] for x in xs), C // 2
    wide = jax.ShapeDtypeStruct((count, half * side), f32)
    outs = [wide, wide, jax.ShapeDtypeStruct((count, half * side), bf16)]
    col = pl.BlockSpec((count, side), lambda c: (0, c))
    return pl.pallas_call(
        gate_up_kernel,
        grid=(half,),
        in_specs=[
            *[whole(x) for x in xs],
            pl.BlockSpec((rep, R, 1, part, side), lambda c: (0, 0, c, 0, 0)),
            pl.BlockSpec((rep, R, 1, part, side), lambda c: (0, 0, c + half, 0, 0)),
        ],
        out_specs=[col, col, col],
        out_shape=outs,
        compiler_params=params(),
        cost_estimate=cost(2 * count * R * C * side * side, nbytes(*xs, w, *outs)),
    )(*xs, w, w)


def nn_kernel(x_ref, w_ref, *refs):
    y_ref = refs[-1]
    side = w_ref.shape[-1]
    total = None
    for r in range(w_ref.shape[1]):
        part = mm(x_ref[:, r * side : (r + 1) * side], w_ref[:, r, 0].reshape(side, side))
        total = part if total is None else total + part
    y_ref[...] = total


def nn(x, w, *others, columns=None, row=None):
    rep, R, C, part, side = w.shape
    count = x.shape[0]
    if row is None:
        block, index = (rep, R, 1, part, side), lambda c: (0, 0, c, 0, 0)
        steps = columns or C
    else:
        block, index = (rep, 1, 1, part, side), lambda c: (0, c, row, 0, 0)
        steps = R
    out = jax.ShapeDtypeStruct((count, steps * side), f32)
    return pl.pallas_call(
        nn_kernel,
        grid=(steps,),
        in_specs=[pl.BlockSpec(x.shape, lambda c: (0, 0)), pl.BlockSpec(block, index)]
        + [pl.BlockSpec(memory_space=pl.ANY)] * len(others),
        out_specs=pl.BlockSpec((count, side), lambda c: (0, c)),
        out_shape=out,
        compiler_params=params(),
        cost_estimate=cost(
            2 * count * x.shape[1] * steps * side, nbytes(x, out) + 2 * x.shape[1] * steps * side
        ),
    )(x, w, *others)


def hidden_back_kernel(half, *refs):
    w_ref, gate_ref, up_ref = refs[half : half + 3]
    x, y_ref, side = join(refs[:half]), refs[-1], w_ref.shape[-1]
    total = None
    for c in range(w_ref.shape[2]):
        part = mm_nt(x[:, c * side : (c + 1) * side], w_ref[:, 0, c].reshape(side, side))
        total = part if total is None else total + part
    gate = gate_ref[...]
    sigma = jax.nn.sigmoid(gate)
    y_ref[0] = (total * up_ref[...] * sigma * (1.0 + gate * (1.0 - sigma))).astype(bf16)
    y_ref[1] = (total * gate * sigma).astype(bf16)


def hidden_back(xs, w, gate, up, *others):
    rep, R, C, part, side = w.shape
    count = gate.shape[0]
    out = jax.ShapeDtypeStruct((2, count, R * side), bf16)
    col = pl.BlockSpec((count, side), lambda r: (0, r))
    return pl.pallas_call(
        functools.partial(hidden_back_kernel, len(xs)),
        grid=(R,),
        in_specs=[
            *[whole(x) for x in xs],
            pl.BlockSpec((rep, 1, C, part, side), lambda r: (0, r, 0, 0, 0)),
            col,
            col,
            *[pl.BlockSpec(memory_space=pl.ANY)] * len(others),
        ],
        out_specs=pl.BlockSpec((2, count, side), lambda r: (0, 0, r)),
        out_shape=out,
        compiler_params=params(),
        cost_estimate=cost(2 * count * R * C * side * side, nbytes(*xs, w, gate, up, out)),
    )(*xs, w, gate, up, *others)


def nt_kernel(half, *refs):
    x, w_ref, y_ref = join(refs[:half]), refs[half], refs[-1]
    side = w_ref.shape[-1]
    per = x.shape[2] // side
    total = None
    for c in range(w_ref.shape[1] * w_ref.shape[2]):
        left = x[c // per, :, (c % per) * side : (c % per + 1) * side]
        w = w_ref[:, c // w_ref.shape[2], c % w_ref.shape[2]].reshape(side, side)
        part = mm_nt(left, w)
        total = part if total is None else total + part
    y_ref[...] = total


def nt(xs, w, *others, row=None):
    rep, R, C, part, side = w.shape
    count, depth = sum(x.shape[1] for x in xs), xs[0].shape[0] * xs[0].shape[2]
    if row is None:
        block, index = (rep, 1, depth // side, part, side), lambda r: (0, r, 0, 0, 0)
        steps = R
    else:
        block, index = (rep, R, 1, part, side), lambda r: (0, 0, row, 0, 0)
        steps = 1
    out = jax.ShapeDtypeStruct((count, steps * side), f32)
    return pl.pallas_call(
        functools.partial(nt_kernel, len(xs)),
        grid=(steps,),
        in_specs=[
            *[whole(x) for x in xs],
            pl.BlockSpec(block, index),
            *[pl.BlockSpec(memory_space=pl.ANY)] * len(others),
        ],
        out_specs=pl.BlockSpec((count, side), lambda r: (0, r)),
        out_shape=out,
        compiler_params=params(),
        cost_estimate=cost(
            2 * count * depth * steps * side, nbytes(*xs, out) + 2 * depth * steps * side
        ),
    )(*xs, w, *others)


def tn_kernel(lefts, rights, *refs):
    y_ref = refs[-1]
    rep, _, _, part, side = y_ref.shape
    left, right = join(refs[:lefts]), join(refs[lefts : lefts + rights])
    y_ref[:, 0, 0] = mm_tn(left, right[0]).astype(bf16).reshape(rep, part, side)


def tn(lefts, rights, rep, side, *others, only=None, spare=0, base=None):
    R = lefts[0].shape[1] // side
    m, per = rights[0].shape[0], rights[0].shape[2] // side
    first, C = (0, m * per) if only is None else (only, per)
    out = jax.ShapeDtypeStruct((rep, R + spare, C, side // rep, side), bf16)
    start, aliases = 0, {}
    if base is not None:
        out = jax.ShapeDtypeStruct(base.shape, base.dtype)
        start, others = base.shape[1] - R, (*others, base)
        aliases = {len(lefts) + len(rights) + len(others) - 1: 0}
    total = sum(x.shape[0] for x in lefts)
    return pl.pallas_call(
        functools.partial(tn_kernel, len(lefts), len(rights)),
        grid=(R, C),
        in_specs=[pl.BlockSpec((x.shape[0], side), lambda r, c: (0, r)) for x in lefts]
        + [
            pl.BlockSpec((1, x.shape[1], side), lambda r, c: (first + c // per, 0, c % per))
            for x in rights
        ]
        + [pl.BlockSpec(memory_space=pl.ANY)] * len(others),
        out_specs=pl.BlockSpec((rep, 1, 1, side // rep, side), lambda r, c: (0, start + r, c, 0, 0)),
        out_shape=out,
        input_output_aliases=aliases,
        compiler_params=params(),
        cost_estimate=cost(2 * total * R * C * side * side, nbytes(*lefts, *rights, out)),
    )(*lefts, *rights, *others)


def heads_kernel(half, *refs):
    y_ref = refs[-1]
    rep, _, part, width = y_ref.shape
    left = jnp.concatenate([r[...] for r in refs[:half]], axis=0)
    right = jnp.concatenate([r[...] for r in refs[half : 2 * half]], axis=0)
    y_ref[:, 0] = mm_tn(left, right).astype(bf16).reshape(rep, part, width)


def heads_tn(lefts, rights, rep, side, *others):
    count, R = lefts[0].shape[0], lefts[0].shape[1] // side
    width = rights[0].shape[1]
    out = jax.ShapeDtypeStruct((rep, R, side // rep, width), bf16)
    return pl.pallas_call(
        functools.partial(heads_kernel, len(lefts)),
        grid=(R,),
        in_specs=[pl.BlockSpec((count, side), lambda r: (0, r))] * len(lefts)
        + [pl.BlockSpec((count, width), lambda r: (0, 0))] * len(rights)
        + [pl.BlockSpec(memory_space=pl.ANY)] * len(others),
        out_specs=pl.BlockSpec((rep, 1, side // rep, width), lambda r: (0, r, 0, 0)),
        out_shape=out,
        compiler_params=params(),
        cost_estimate=cost(
            2 * count * len(lefts) * R * side * width, nbytes(*lefts, *rights, out)
        ),
    )(*lefts, *rights, *others)


def scores_of(q, k, begin, q_start, k_start, scale):
    scores = mm_nt(k, q) * scale
    key_place = k_start + lax.broadcasted_iota(jnp.int32, scores.shape, 0)
    query_place = q_start + lax.broadcasted_iota(jnp.int32, scores.shape, 1)
    return jnp.where((key_place >= begin) & (key_place <= query_place), scores, -1e30)


def window_start(i, block, window, length):
    start = jnp.clip(i * block + block - window, 0, length - window)
    return pl.multiple_of(start, 128)


def attend_kernel(scale, window, q_ref, k_ref, v_ref, b_ref, o_ref, lse_ref):
    block, length = q_ref.shape[0], k_ref.shape[0]
    i = pl.program_id(0)
    start = window_start(i, block, window, length)
    scores = scores_of(
        q_ref[...], k_ref[pl.ds(start, window), :], b_ref[...], i * block, start, scale
    )
    top = jnp.max(scores, axis=0, keepdims=True)
    expo = jnp.exp(scores - top)
    total = jnp.sum(expo, axis=0, keepdims=True)
    attention = (expo * (1.0 / total)).astype(bf16)
    o_ref[...] = mm_tn(attention, v_ref[pl.ds(start, window), :]).astype(bf16)
    lse_ref[...] = top + jnp.log(total)


def attend(q, k, v, begins, scale):
    length, width = q.shape
    window = min(QB + SEGMAX, length)
    full = pl.BlockSpec((length, width), lambda i: (0, 0))
    rows = pl.BlockSpec((QB, width), lambda i: (i, 0))
    line = pl.BlockSpec((1, QB), lambda i: (0, i))
    return pl.pallas_call(
        functools.partial(attend_kernel, scale, window),
        grid=(length // QB,),
        in_specs=[rows, full, full, line],
        out_specs=[rows, line],
        out_shape=[
            jax.ShapeDtypeStruct((length, width), bf16),
            jax.ShapeDtypeStruct((1, length), f32),
        ],
        compiler_params=params(),
        cost_estimate=cost(4 * length * window * width, 4 * nbytes(q), length * window),
    )(q, k, v, begins)


def attend_back_kernel(
    scale, window, q_ref, d_ref, k_ref, v_ref, b_ref, lse_ref, *refs
):
    dq_ref, dk_ref, dv_ref, ka, va = refs[-5:]
    block, length = q_ref.shape[0], k_ref.shape[0]
    i = pl.program_id(0)
    start = window_start(i, block, window, length)
    span = pl.ds(start, window)

    @pl.when(i == 0)
    def _():
        ka[...] = jnp.zeros_like(ka)
        va[...] = jnp.zeros_like(va)

    q, d, k = q_ref[...], d_ref[...], k_ref[span, :]
    scores = scores_of(q, k, b_ref[...], i * block, start, scale)
    attention = jnp.exp(scores - lse_ref[...])
    prob_grad = mm_nt(v_ref[span, :], d)
    center = jnp.sum(attention * prob_grad, axis=0, keepdims=True)
    score_grad = (attention * (prob_grad - center)).astype(bf16)
    dq_ref[...] = (mm_tn(score_grad, k) * scale).astype(bf16)
    ka[span, :] += mm(score_grad, q) * scale
    va[span, :] += mm(attention.astype(bf16), d)

    @pl.when(i == pl.num_programs(0) - 1)
    def _():
        dk_ref[...] = ka[...].astype(bf16)
        dv_ref[...] = va[...].astype(bf16)


def attend_back(q, d, k, v, begins, lse, scale, *others):
    length, width = q.shape
    window = min(QB + SEGMAX, length)
    full = pl.BlockSpec((length, width), lambda i: (0, 0))
    rows = pl.BlockSpec((QB, width), lambda i: (i, 0))
    line = pl.BlockSpec((1, QB), lambda i: (0, i))
    return pl.pallas_call(
        functools.partial(attend_back_kernel, scale, window),
        grid=(length // QB,),
        in_specs=[rows, rows, full, full, line, line]
        + [pl.BlockSpec(memory_space=pl.ANY)] * len(others),
        out_specs=[rows, full, full],
        out_shape=[jax.ShapeDtypeStruct((length, width), bf16)] * 3,
        scratch_shapes=[pltpu.VMEM((length, width), f32)] * 2,
        compiler_params=params(),
        cost_estimate=cost(10 * length * window * width, 8 * nbytes(q), length * window),
    )(q, d, k, v, begins, lse, *others)


def shampoo_kernel(g_ref, ls_ref, rs_ref, lr_ref, rr_ref, w_ref, go_ref, lo_ref, ro_ref, wo_ref):
    g = g_ref[0]
    go_ref[0] = g.astype(f32)
    lo_ref[0] = decay_rate * ls_ref[0] + (1.0 - decay_rate) * mm_nt(g, g)
    ro_ref[0] = decay_rate * rs_ref[0] + (1.0 - decay_rate) * mm_tn(g, g)
    middle = mm(lr_ref[0].astype(bf16), g).astype(bf16)
    wo_ref[0] = w_ref[0] - step_rate * mm(middle, rr_ref[0].astype(bf16))


def shampoo(g, *rest):
    slots, side, _ = g.shape
    spec = pl.BlockSpec((1, side, side), lambda s: (s, 0, 0))
    return pl.pallas_call(
        shampoo_kernel,
        grid=(slots,),
        in_specs=[spec] * 6,
        out_specs=[spec] * 4,
        out_shape=[jax.ShapeDtypeStruct(g.shape, f32)] * 4,
        compiler_params=params(),
        cost_estimate=cost(8 * slots * side**3, 38 * g.size),
    )(g, *rest)


def rms_norm(values, gain_vec):
    return (
        values * lax.rsqrt(jnp.mean(values * values, axis=-1, keepdims=True) + epsilon) * gain_vec
    )


def begins_of(segment_row):
    length = segment_row.shape[0]
    indices = jnp.arange(length, dtype=jnp.int32)
    earlier = jnp.concatenate([jnp.full((1,), -1, jnp.int32), segment_row[:-1]])
    return lax.cummax(jnp.where(segment_row != earlier, indices, 0), axis=0)


UP = [(i, (i + 1) % Z) for i in range(Z)]


def ring_gather(block, first_use=None):
    blocks = [block]
    for k in range(Z - 1):
        blocks.append(lax.ppermute(blocks[-1], "hz", UP))
        if k == 0 and first_use:
            used = first_use(blocks[:2])
        if k == 1 and first_use:
            blocks[2] = after(blocks[2], used[0])
    return (blocks, used) if first_use else blocks


def ring_scatter(part_of):
    total = part_of(1).astype(bf16)
    for k in (2, 3):
        total = (lax.ppermute(total, "hz", UP).astype(f32) + part_of(k)).astype(bf16)
    return lax.ppermute(total, "hz", UP).astype(f32) + part_of(0)


def none_kernel(*refs):
    pass


def after(value, *others):
    anywhere = pl.BlockSpec(memory_space=pl.ANY)
    return pl.pallas_call(
        none_kernel,
        in_specs=[anywhere] * (1 + len(others)),
        out_specs=anywhere,
        out_shape=jax.ShapeDtypeStruct(value.shape, value.dtype),
        input_output_aliases={0: 0},
    )(value, *others)


def exchange_z(part_for):
    got = [part_for(0)]
    for j in range(1, Z):
        got.append(lax.ppermute(part_for(j), "hz", [(i, (i + j) % Z) for i in range(Z)]))
    return jnp.stack(got)


def swap(value, bit):
    size = lax.axis_size("hp")
    return lax.ppermute(value, "hp", [(i, i ^ bit) for i in range(size)])


def plane_scatter(pieces):
    PN, S = lax.axis_size("hp"), lax.axis_size("seq")
    if S != 2 or PN != 4:
        return lax.psum_scatter(pieces, ("hp", "seq"), scatter_dimension=0, tiled=False)
    p = lax.axis_index("hp")
    chip = sum_seq_scatter(pieces.reshape((PN, S) + pieces.shape[1:]), 1)
    half = chip.shape[1] // 2

    def add(mine, got):
        return (mine.astype(f32) + got.astype(f32)).astype(bf16)

    def pair(values, first, second):
        return jnp.take(values, jnp.stack([p ^ first, p ^ second]), axis=0, mode="clip")

    one, two = chip[:, :half], chip[:, half:]
    one_got, two_got = swap(pair(one, 1, 3), 1), swap(pair(two, 2, 3), 2)
    one, two = add(pair(one, 0, 2), one_got), add(pair(two, 0, 1), two_got)
    one_got, two_got = swap(one[1], 2), swap(two[1], 1)
    return jnp.concatenate([add(one[0], one_got), add(two[0], two_got)])


def from_group(values):
    size = lax.axis_size(GROUP)
    spread = jnp.broadcast_to(values, (size,) + values.shape)
    return lax.all_to_all(spread, GROUP, 0, 0, tiled=True)


def sum_seq_scatter(values, axis):
    S = lax.axis_size("seq")
    if S != 2:
        return lax.psum_scatter(values, "seq", scatter_dimension=axis, tiled=False)
    c = lax.axis_index("seq")
    mine = lax.dynamic_index_in_dim(values, c, axis, keepdims=False)
    other = lax.dynamic_index_in_dim(values, 1 - c, axis, keepdims=False)
    got = lax.ppermute(other, "seq", [(0, 1), (1, 0)])
    return (mine.astype(f32) + got.astype(f32)).astype(bf16)


def body(
    tokens,
    cotangent,
    segment_ids,
    owner_map,
    weights,
    norm_gains,
    left_stats,
    right_stats,
    left_root,
    right_root,
):
    model_width = tokens.shape[2]
    local_count = tokens.shape[1]
    slots, side = weights.shape[0], weights.shape[1]
    total_blocks = owner_map.shape[0]
    PN, S = lax.axis_size("hp"), lax.axis_size("seq")
    n = Z * PN * S
    rep = PN * S
    rows = side // n
    part = Z * rows
    head_size = model_width // HEADS
    quarter = model_width // Z
    score_scale = head_size ** (-0.5)
    zi, pi = lax.axis_index("hz"), lax.axis_index("hp")
    relative = (zi - jnp.arange(Z, dtype=jnp.int32)) % Z
    inputs = tokens[0]

    def zero_of(value):
        entry = value[(0,) * value.ndim]
        if value.dtype == jnp.int32:
            return (entry < 0).astype(jnp.int32)
        return (entry != entry).astype(jnp.int32)

    D, F = model_width // side, FF // side
    number = jnp.arange(total_blocks, dtype=jnp.int32)
    square, tall = D * D, D * F
    qkv_list = number[: 3 * square].reshape(3, D, Z).transpose(2, 1, 0)
    out_list = number[3 * square : 4 * square].reshape(Z, D, 1)
    attn_list = jnp.concatenate([qkv_list, out_list], axis=2).reshape(Z, -1)
    gateup_list = number[4 * square : 4 * square + 2 * tall].reshape(2, D, Z, F // Z)
    gateup_list = gateup_list.transpose(2, 1, 0, 3).reshape(Z, -1)
    down_list = number[4 * square + 2 * tall :].reshape(Z, -1)
    inverse = jnp.zeros((total_blocks,), jnp.int32).at[owner_map].set(number)

    low = weights.astype(bf16).reshape(slots, PN, S, Z, rows, side)
    low = low.transpose(3, 1, 2, 0, 4, 5).reshape(n * slots, rows, side)
    spread = lax.all_to_all(low, EVERY, 0, 0, tiled=True)
    tokens_g = lax.all_gather(inputs, "hz", axis=0, tiled=True)

    group, group_tokens = Z * PN, Z * local_count

    def fetch(numbers, *others):
        places = inverse[numbers.reshape(-1)]
        for other in others:
            places = places + zero_of(other)
        picked = jnp.take(spread, places, axis=0, mode="clip")
        got = lax.all_to_all(picked, "hz", 0, 0, tiled=True)
        return got.reshape(Z, -1, rows, side).transpose(1, 0, 2, 3).reshape(-1, part, side)

    def all_plane(got, R):
        got = lax.all_gather(got, ("hp", "seq"), axis=0, tiled=False)
        return got.reshape(rep, R, -1, part, side)

    got_attn = fetch(attn_list, tokens_g)
    w_attn = all_plane(got_attn, D)
    def fetch_beside(numbers, other):
        def part_for(j):
            wanted = lax.dynamic_index_in_dim(numbers, (zi + j) % Z, 0, keepdims=False)
            return jnp.take(spread, inverse[wanted] + zero_of(other), axis=0, mode="clip")

        got = jnp.take(exchange_z(part_for), relative, axis=0, mode="clip")
        return got.transpose(1, 0, 2, 3).reshape(-1, part, side)

    w_gateup = all_plane(fetch_beside(gateup_list, got_attn), D)

    def rope(values, sign):
        first, second = values[:, :half_size], values[:, half_size:]
        return jnp.concatenate(
            [first * cosine - second * sine * sign, second * cosine + first * sine * sign], axis=-1
        )

    head = zi * PN + pi
    gains_head = lax.dynamic_slice_in_dim(norm_gains[2:4], head * head_size, head_size, axis=1)

    def to_heads(stack):
        m = stack.shape[0]
        shaped = stack.reshape(m, Z, local_count, PN, head_size).transpose(3, 0, 1, 2, 4)
        got = lax.all_to_all(shaped, "hp", 0, 0, tiled=True)
        return got.transpose(1, 2, 0, 3, 4).reshape(m, length, head_size)

    def to_groups(stack):
        m = stack.shape[0]
        shaped = stack.reshape(m, Z, PN, local_count, head_size).transpose(2, 0, 1, 3, 4)
        got = lax.all_to_all(shaped, "hp", 0, 0, tiled=True)
        return got.transpose(1, 2, 3, 0, 4).reshape(m, group_tokens, quarter)

    raw = nn(tokens_g, w_attn, columns=3)
    raw_three = raw.reshape(group_tokens, 3, quarter).transpose(1, 0, 2)
    squares = jnp.sum(raw_three[:2] * raw_three[:2], axis=-1)
    ids = jnp.pad(segment_ids.astype(f32), ((0, 0), (0, group_tokens - local_count)))
    shared = from_group(jnp.concatenate([squares, ids])).reshape(Z, PN, 3, Z, local_count)
    squares, row_ids = shared[:, :, :2], shared[:, :, 2, 0].reshape(-1).astype(jnp.int32)
    length = row_ids.shape[0]
    begins = begins_of(row_ids)
    places = jnp.arange(length, dtype=jnp.int32) - begins
    half_size = head_size // 2
    frequency = rope_base ** (-2.0 * jnp.arange(half_size, dtype=f32) / head_size)
    angles = places.astype(f32)[:, None] * frequency[None, :]
    cosine, sine = jnp.cos(angles), jnp.sin(angles)

    squares = jnp.sum(squares, axis=0).transpose(1, 2, 0, 3).reshape(2, length, 1)
    raw_row = to_heads(raw_three.astype(bf16))
    invs = lax.rsqrt(squares / model_width + epsilon)
    query_hat, key_hat = (raw_row[i].astype(f32) * invs[i] for i in range(2))
    query_row = rope(query_hat * gains_head[0], 1.0).astype(bf16)
    key_row = rope(key_hat * gains_head[1], 1.0).astype(bf16)
    value_row = raw_row[2]

    got_down = fetch_beside(down_list, squares)

    begin_line = begins[None, :]
    mixed, log_sums = attend(query_row, key_row, value_row, begin_line, score_scale)
    attended = to_groups(mixed[None]).reshape(Z, local_count, quarter)
    attended_rel = jnp.take(attended, relative, axis=0, mode="clip")
    attn_parts = [nn(attended_rel[k], w_attn, row=3) for k in range(Z)]
    attn_raw = ring_scatter(lambda k: attn_parts[k])
    w_down = all_plane(after(got_down, w_gateup, attn_parts[1]), F // Z)
    resid = inputs.astype(f32) + rms_norm(attn_raw, norm_gains[0])

    resid_blocks, near = ring_gather(resid.astype(bf16), lambda pair: gate_up(pair, w_gateup))

    tokens_z = tokens_g.reshape(Z, local_count, model_width)
    middle = local_count // 2
    tok_one, tok_two = after(tokens_z[:, :middle], resid), after(tokens_z[:, middle:], resid)
    tok_one = jnp.stack([tok_one, swap(tok_one, 1)])
    tok_two = jnp.stack([tok_two, swap(tok_two, 2)])
    tok_parts = [tok_one, swap(tok_one, 2), tok_two, swap(tok_two, 1)]
    tok_parts = [t.reshape(-1, model_width) for t in tok_parts]
    tok_near, tok_far = tok_parts[::2], tok_parts[1::2]
    gates, ups, hiddens = zip(near, gate_up(resid_blocks[2:], w_gateup))

    def entry(halves, k):
        return halves[k // 2][k % 2 * local_count : (k % 2 + 1) * local_count]

    downs = [nn(hiddens[0], w_down), nn(hiddens[1], w_down, *tok_near)]
    down_raw = ring_scatter(lambda k: entry(downs, k))
    output = (resid + rms_norm(down_raw, norm_gains[1])).astype(bf16)[None]

    upstream = cotangent[0].astype(f32)
    _, down_norm_back = jax.vjp(rms_norm, down_raw, norm_gains[1])
    down_grad, gain_mlp_grad = down_norm_back(upstream)
    down_blocks, near = ring_gather(
        down_grad.astype(bf16),
        lambda pair: [hidden_back(pair, w_down, gates[0], ups[0])],
    )
    gateup_grads = near + [hidden_back(down_blocks[2:], w_down, gates[1], ups[1], *tok_far)]

    def spread_z(summed):
        summed = summed.reshape(-1, Z, rows, side)
        return exchange_z(
            lambda j: lax.dynamic_index_in_dim(summed, (zi + j) % Z, 1, keepdims=False)
        )

    def blocks_of(pieces):
        return pieces.reshape(rep, -1, part, side)

    def sum_plane(pieces):
        return lax.psum_scatter(
            blocks_of(pieces), ("hp", "seq"), scatter_dimension=0, tiled=False
        )

    down_pieces = tn(hiddens, [b[None] for b in down_blocks], rep, side, spare=quarter // side)
    gate_pieces = tn(resid_blocks, gateup_grads, rep, side, only=0)
    up_pieces = tn(resid_blocks, gateup_grads, rep, side, only=1)
    gate_sum = sum_plane(gate_pieces)
    up_sum = sum_plane(up_pieces)
    resid_parts = [nt([gateup_grads[0]], w_gateup), nt([gateup_grads[1]], w_gateup)]
    resid_grad = upstream + ring_scatter(lambda k: entry(resid_parts, k))

    _, attn_norm_back = jax.vjp(rms_norm, attn_raw, norm_gains[0])
    attn_grad, gain_attn_grad = attn_norm_back(resid_grad)
    attn_low = attn_grad.astype(bf16)
    attn_blocks = ring_gather(attn_low)
    grad_rel = nt([b[None] for b in attn_blocks], w_attn, row=3).astype(bf16)
    grad_rel = grad_rel.reshape(Z, local_count, quarter)
    grad_abs = jnp.take(grad_rel, relative, axis=0, mode="clip")
    grad_row = to_heads(grad_abs.reshape(1, group_tokens, quarter))[0]
    last_pieces = tn(
        [attended_rel[k] for k in range(Z)],
        [b[None] for b in attn_blocks],
        rep,
        side,
        base=down_pieces,
    )
    last_sum = sum_plane(last_pieces)
    gate_sent = spread_z(after(gate_sum, grad_abs))
    query_grad, key_grad, value_grad = attend_back(
        query_row,
        grad_row,
        key_row,
        value_row,
        begin_line,
        log_sums,
        score_scale,
    )
    query_turn, key_turn = rope(query_grad.astype(f32), -1.0), rope(key_grad.astype(f32), -1.0)
    gain_query = jnp.sum(query_turn * query_hat, axis=0)
    gain_key = jnp.sum(key_turn * key_hat, axis=0)
    query_turn, key_turn = query_turn * gains_head[0], key_turn * gains_head[1]
    dots = jnp.stack([jnp.sum(query_turn * query_hat, -1), jnp.sum(key_turn * key_hat, -1)])
    dots = jnp.sum(from_group(dots).reshape(group, 2, length), axis=0) / model_width
    up_sent, down_sent = spread_z(after(up_sum, dots)), spread_z(last_sum)
    dots = dots[..., None]
    query_back = ((query_turn - query_hat * dots[0]) * invs[0]).astype(bf16)
    key_back = ((key_turn - key_hat * dots[1]) * invs[1]).astype(bf16)

    back_row = jnp.concatenate([query_back, key_back, value_grad], axis=1)
    by_half = back_row.reshape(Z, PN, 2, middle, 3 * head_size).transpose(1, 2, 0, 3, 4)

    def rows_of(half, *bits):
        picked = jnp.take(by_half[:, half], jnp.stack([pi ^ bit for bit in bits]), axis=0, mode="clip")
        return picked.reshape(-1, 3 * head_size)

    back_parts = [rows_of(0, 0, 1), rows_of(0, 2, 3), rows_of(1, 0, 2), rows_of(1, 1, 3)]
    heads_grad = heads_tn(tok_parts, back_parts, rep, side, gate_sent)
    heads_sum = sum_seq_scatter(heads_grad.reshape(PN, S, D, part, 3 * head_size), 1)
    heads_sum = heads_sum.reshape(PN, D, Z, rows, 3 * head_size).transpose(2, 0, 1, 3, 4)
    heads_sent = lax.all_to_all(
        heads_sum.reshape(group, D, rows, 3 * head_size), GROUP, 0, 0, tiled=True
    ).reshape(Z, PN, D, rows, 3, head_size)
    heads_sent = heads_sent.transpose(4, 2, 0, 3, 1, 5).reshape(3 * square, rows, side)

    back_abs = to_groups(jnp.stack([query_back, key_back, value_grad]))
    back_rel = jnp.take(
        back_abs.reshape(3, Z, local_count, quarter), relative, axis=1, mode="clip"
    )
    near_back = nt([back_rel[:, 0], back_rel[:, 1]], w_attn, up_sent, heads_grad)
    back_parts = [near_back, nt([back_rel[:, 2], back_rel[:, 3]], w_attn)]
    input_grad = resid_grad + ring_scatter(lambda k: entry(back_parts, k))


    spots = jnp.zeros((2, model_width), f32)
    spots = lax.dynamic_update_slice(spots, jnp.stack([gain_query, gain_key]), (0, head * head_size))
    gain_local = jnp.concatenate([jnp.stack([gain_attn_grad, gain_mlp_grad]), spots])
    shares = lax.all_to_all(gain_local.reshape(n, -1), EVERY, 0, 0, tiled=True)
    share = jnp.sum(shares, axis=0)
    gain_grads = lax.all_to_all(
        jnp.broadcast_to(share, (n, share.shape[0])), EVERY, 0, 0, tiled=True
    ).reshape(gain_local.shape)

    flat = [heads_sent, gate_sent, up_sent, down_sent]
    sent = jnp.concatenate([a.reshape(-1, rows, side) for a in flat])
    split = gateup_list.reshape(Z, D, 2, -1)
    last = jnp.concatenate([down_list, out_list.reshape(Z, -1)], axis=1)
    order = [split[:, :, 0], split[:, :, 1], last]
    order = [jnp.take(o.reshape(Z, -1), relative, axis=0, mode="clip").reshape(-1) for o in order]
    order = jnp.concatenate([number[: 3 * square]] + order)
    where_is = jnp.zeros((total_blocks,), jnp.int32).at[order].set(number)
    to_slots = jnp.take(sent, where_is[owner_map] + zero_of(input_grad), axis=0, mode="clip")
    got = lax.all_to_all(to_slots, EVERY, 0, 0, tiled=True)
    got = got.reshape(Z, PN, S, slots, rows, side).transpose(3, 1, 2, 0, 4, 5)
    grad_slots, left_new, right_new, new_weights = shampoo(
        got.reshape(slots, side, side), left_stats, right_stats, left_root, right_root, weights
    )
    new_gains = norm_gains - gain_rate * gain_grads * lax.rsqrt(
        jnp.mean(gain_grads * gain_grads, axis=1, keepdims=True) + epsilon
    )
    return (
        output,
        input_grad[None],
        grad_slots,
        left_new,
        right_new,
        new_weights,
        gain_grads,
        new_gains,
    )


def solution(mesh):
    heads, seqs = mesh.shape["head"], mesh.shape["seq"]
    fine = Mesh(mesh.devices.reshape(Z, heads // Z, seqs), EVERY)
    tok = P("seq", GROUP, None)
    slot = P(EVERY, None, None)
    return jax.shard_map(
        body,
        mesh=fine,
        in_specs=(tok, tok, P("seq", GROUP), P(), slot, P(), slot, slot, slot, slot),
        out_specs=(tok, tok, slot, slot, slot, slot, P(), P()),
        check_vma=False,
    )
```

```python
import functools

import jax
import jax.numpy as jnp
from jax import lax
from jax.experimental import pallas as pl
from jax.experimental.pallas import tpu as pltpu
from jax.sharding import Mesh
from jax.sharding import PartitionSpec as P

FF = 8192
HEADS = 16
SEGMAX = 1024
QB = 256
Z = 4

epsilon = 1e-06
rope_base = 500000.0
decay_rate = 0.5
step_rate = 0.5
gain_rate = 0.3
bf16 = jnp.bfloat16
f32 = jnp.float32
EVERY = ("hz", "hp", "seq")
GROUP = ("hz", "hp")
VMEM_LIMIT = 48 * 1024 * 1024


def mm(left_side, right_side):
    return jnp.dot(left_side, right_side, preferred_element_type=f32)


def mm_nt(left_side, right_side):
    return lax.dot_general(
        left_side, right_side, (((1,), (1,)), ((), ())), preferred_element_type=f32
    )


def mm_tn(left_side, right_side):
    return lax.dot_general(
        left_side, right_side, (((0,), (0,)), ((), ())), preferred_element_type=f32
    )


def params():
    return pltpu.CompilerParams(vmem_limit_bytes=VMEM_LIMIT)


def cost(flops, nbytes, exps=0):
    part = 0.1
    return pl.CostEstimate(
        flops=int(part * flops), bytes_accessed=int(part * nbytes), transcendentals=int(part * exps)
    )


def nbytes(*arrays):
    return sum(a.size * a.dtype.itemsize for a in arrays)


def join(refs):
    return refs[0][...] if len(refs) == 1 else jnp.concatenate([r[...] for r in refs], axis=-2)


def whole(array):
    return pl.BlockSpec(array.shape, lambda *_: (0,) * array.ndim)


def gate_up_kernel(*refs):
    *x_refs, g_ref, u_ref, gate_ref, up_ref, hidden_ref = refs
    x, side = join(x_refs), g_ref.shape[-1]
    for w_ref, y_ref in ((g_ref, gate_ref), (u_ref, up_ref)):
        total = None
        for r in range(w_ref.shape[1]):
            part = mm(x[:, r * side : (r + 1) * side], w_ref[:, r, 0].reshape(side, side))
            total = part if total is None else total + part
        y_ref[...] = total
    gate = gate_ref[...]
    hidden_ref[...] = (gate * jax.nn.sigmoid(gate) * up_ref[...]).astype(bf16)


def gate_up(xs, w):
    rep, R, C, part, side = w.shape
    count, half = sum(x.shape[0] for x in xs), C // 2
    wide = jax.ShapeDtypeStruct((count, half * side), f32)
    outs = [wide, wide, jax.ShapeDtypeStruct((count, half * side), bf16)]
    col = pl.BlockSpec((count, side), lambda c: (0, c))
    return pl.pallas_call(
        gate_up_kernel,
        grid=(half,),
        in_specs=[
            *[whole(x) for x in xs],
            pl.BlockSpec((rep, R, 1, part, side), lambda c: (0, 0, c, 0, 0)),
            pl.BlockSpec((rep, R, 1, part, side), lambda c: (0, 0, c + half, 0, 0)),
        ],
        out_specs=[col, col, col],
        out_shape=outs,
        compiler_params=params(),
        cost_estimate=cost(2 * count * R * C * side * side, nbytes(*xs, w, *outs)),
    )(*xs, w, w)


def nn_kernel(x_ref, w_ref, *refs):
    y_ref = refs[-1]
    side = w_ref.shape[-1]
    total = None
    for r in range(w_ref.shape[1]):
        part = mm(x_ref[:, r * side : (r + 1) * side], w_ref[:, r, 0].reshape(side, side))
        total = part if total is None else total + part
    y_ref[...] = total


def nn(x, w, *others, columns=None, row=None):
    rep, R, C, part, side = w.shape
    count = x.shape[0]
    if row is None:
        block, index = (rep, R, 1, part, side), lambda c: (0, 0, c, 0, 0)
        steps = columns or C
    else:
        block, index = (rep, 1, 1, part, side), lambda c: (0, c, row, 0, 0)
        steps = R
    out = jax.ShapeDtypeStruct((count, steps * side), f32)
    return pl.pallas_call(
        nn_kernel,
        grid=(steps,),
        in_specs=[pl.BlockSpec(x.shape, lambda c: (0, 0)), pl.BlockSpec(block, index)]
        + [pl.BlockSpec(memory_space=pl.ANY)] * len(others),
        out_specs=pl.BlockSpec((count, side), lambda c: (0, c)),
        out_shape=out,
        compiler_params=params(),
        cost_estimate=cost(
            2 * count * x.shape[1] * steps * side, nbytes(x, out) + 2 * x.shape[1] * steps * side
        ),
    )(x, w, *others)


def hidden_back_kernel(half, *refs):
    w_ref, gate_ref, up_ref = refs[half : half + 3]
    x, y_ref, side = join(refs[:half]), refs[-1], w_ref.shape[-1]
    total = None
    for c in range(w_ref.shape[2]):
        part = mm_nt(x[:, c * side : (c + 1) * side], w_ref[:, 0, c].reshape(side, side))
        total = part if total is None else total + part
    gate = gate_ref[...]
    sigma = jax.nn.sigmoid(gate)
    y_ref[0] = (total * up_ref[...] * sigma * (1.0 + gate * (1.0 - sigma))).astype(bf16)
    y_ref[1] = (total * gate * sigma).astype(bf16)


def hidden_back(xs, w, gate, up, *others):
    rep, R, C, part, side = w.shape
    count = gate.shape[0]
    out = jax.ShapeDtypeStruct((2, count, R * side), bf16)
    col = pl.BlockSpec((count, side), lambda r: (0, r))
    return pl.pallas_call(
        functools.partial(hidden_back_kernel, len(xs)),
        grid=(R,),
        in_specs=[
            *[whole(x) for x in xs],
            pl.BlockSpec((rep, 1, C, part, side), lambda r: (0, r, 0, 0, 0)),
            col,
            col,
            *[pl.BlockSpec(memory_space=pl.ANY)] * len(others),
        ],
        out_specs=pl.BlockSpec((2, count, side), lambda r: (0, 0, r)),
        out_shape=out,
        compiler_params=params(),
        cost_estimate=cost(2 * count * R * C * side * side, nbytes(*xs, w, gate, up, out)),
    )(*xs, w, gate, up, *others)


def nt_kernel(half, *refs):
    x, w_ref, y_ref = join(refs[:half]), refs[half], refs[-1]
    side = w_ref.shape[-1]
    per = x.shape[2] // side
    total = None
    for c in range(w_ref.shape[1] * w_ref.shape[2]):
        left = x[c // per, :, (c % per) * side : (c % per + 1) * side]
        w = w_ref[:, c // w_ref.shape[2], c % w_ref.shape[2]].reshape(side, side)
        part = mm_nt(left, w)
        total = part if total is None else total + part
    y_ref[...] = total


def nt(xs, w, *others, row=None):
    rep, R, C, part, side = w.shape
    count, depth = sum(x.shape[1] for x in xs), xs[0].shape[0] * xs[0].shape[2]
    if row is None:
        block, index = (rep, 1, depth // side, part, side), lambda r: (0, r, 0, 0, 0)
        steps = R
    else:
        block, index = (rep, R, 1, part, side), lambda r: (0, 0, row, 0, 0)
        steps = 1
    out = jax.ShapeDtypeStruct((count, steps * side), f32)
    return pl.pallas_call(
        functools.partial(nt_kernel, len(xs)),
        grid=(steps,),
        in_specs=[
            *[whole(x) for x in xs],
            pl.BlockSpec(block, index),
            *[pl.BlockSpec(memory_space=pl.ANY)] * len(others),
        ],
        out_specs=pl.BlockSpec((count, side), lambda r: (0, r)),
        out_shape=out,
        compiler_params=params(),
        cost_estimate=cost(
            2 * count * depth * steps * side, nbytes(*xs, out) + 2 * depth * steps * side
        ),
    )(*xs, w, *others)


def tn_kernel(lefts, rights, *refs):
    y_ref = refs[-1]
    rep, _, _, part, side = y_ref.shape
    left, right = join(refs[:lefts]), join(refs[lefts : lefts + rights])
    whole_row = mm_tn(left, right[0]).astype(bf16)
    for c in range(y_ref.shape[2]):
        block = whole_row[:, c * side : (c + 1) * side]
        y_ref[:, 0, c] = block.reshape(rep, part, side)


def tn(lefts, rights, rep, side, *others, only=None, spare=0, base=None):
    R = lefts[0].shape[1] // side
    m, per = rights[0].shape[0], rights[0].shape[2] // side
    first, steps = (0, m) if only is None else (only, 1)
    C = steps * per
    out = jax.ShapeDtypeStruct((rep, R + spare, C, side // rep, side), bf16)
    start, aliases = 0, {}
    if base is not None:
        out = jax.ShapeDtypeStruct(base.shape, base.dtype)
        start, others = base.shape[1] - R, (*others, base)
        aliases = {len(lefts) + len(rights) + len(others) - 1: 0}
    total = sum(x.shape[0] for x in lefts)
    return pl.pallas_call(
        functools.partial(tn_kernel, len(lefts), len(rights)),
        grid=(steps, R),
        in_specs=[pl.BlockSpec((x.shape[0], side), lambda j, r: (0, r)) for x in lefts]
        + [
            pl.BlockSpec((1, x.shape[1], per * side), lambda j, r: (first + j, 0, 0))
            for x in rights
        ]
        + [pl.BlockSpec(memory_space=pl.ANY)] * len(others),
        out_specs=pl.BlockSpec(
            (rep, 1, per, side // rep, side), lambda j, r: (0, start + r, j, 0, 0)
        ),
        out_shape=out,
        input_output_aliases=aliases,
        compiler_params=params(),
        cost_estimate=cost(2 * total * R * C * side * side, nbytes(*lefts, *rights, out)),
    )(*lefts, *rights, *others)


def heads_kernel(half, *refs):
    y_ref = refs[-1]
    rep, _, part, width = y_ref.shape
    left = jnp.concatenate([r[...] for r in refs[:half]], axis=0)
    right = jnp.concatenate([r[...] for r in refs[half : 2 * half]], axis=0)
    y_ref[:, 0] = mm_tn(left, right).astype(bf16).reshape(rep, part, width)


def heads_tn(lefts, rights, rep, side, *others):
    count, R = lefts[0].shape[0], lefts[0].shape[1] // side
    width = rights[0].shape[1]
    out = jax.ShapeDtypeStruct((rep, R, side // rep, width), bf16)
    return pl.pallas_call(
        functools.partial(heads_kernel, len(lefts)),
        grid=(R,),
        in_specs=[pl.BlockSpec((count, side), lambda r: (0, r))] * len(lefts)
        + [pl.BlockSpec((count, width), lambda r: (0, 0))] * len(rights)
        + [pl.BlockSpec(memory_space=pl.ANY)] * len(others),
        out_specs=pl.BlockSpec((rep, 1, side // rep, width), lambda r: (0, r, 0, 0)),
        out_shape=out,
        compiler_params=params(),
        cost_estimate=cost(
            2 * count * len(lefts) * R * side * width, nbytes(*lefts, *rights, out)
        ),
    )(*lefts, *rights, *others)


def scores_of(q, k, begin, q_start, k_start, scale):
    scores = mm_nt(k, q) * scale
    key_place = k_start + lax.broadcasted_iota(jnp.int32, scores.shape, 0)
    query_place = q_start + lax.broadcasted_iota(jnp.int32, scores.shape, 1)
    return jnp.where((key_place >= begin) & (key_place <= query_place), scores, -1e30)


def window_start(i, block, window, length):
    start = jnp.clip(i * block + block - window, 0, length - window)
    return pl.multiple_of(start, 128)


def attend_kernel(scale, window, q_ref, k_ref, v_ref, b_ref, o_ref, lse_ref):
    block, length = q_ref.shape[0], k_ref.shape[0]
    i = pl.program_id(0)
    start = window_start(i, block, window, length)
    scores = scores_of(
        q_ref[...], k_ref[pl.ds(start, window), :], b_ref[...], i * block, start, scale
    )
    top = jnp.max(scores, axis=0, keepdims=True)
    expo = jnp.exp(scores - top)
    total = jnp.sum(expo, axis=0, keepdims=True)
    attention = (expo * (1.0 / total)).astype(bf16)
    o_ref[...] = mm_tn(attention, v_ref[pl.ds(start, window), :]).astype(bf16)
    lse_ref[...] = top + jnp.log(total)


def attend(q, k, v, begins, scale):
    length, width = q.shape
    window = min(QB + SEGMAX, length)
    full = pl.BlockSpec((length, width), lambda i: (0, 0))
    rows = pl.BlockSpec((QB, width), lambda i: (i, 0))
    line = pl.BlockSpec((1, QB), lambda i: (0, i))
    return pl.pallas_call(
        functools.partial(attend_kernel, scale, window),
        grid=(length // QB,),
        in_specs=[rows, full, full, line],
        out_specs=[rows, line],
        out_shape=[
            jax.ShapeDtypeStruct((length, width), bf16),
            jax.ShapeDtypeStruct((1, length), f32),
        ],
        compiler_params=params(),
        cost_estimate=cost(4 * length * window * width, 4 * nbytes(q), length * window),
    )(q, k, v, begins)


def attend_back_kernel(
    scale, window, q_ref, d_ref, k_ref, v_ref, b_ref, lse_ref, *refs
):
    dq_ref, dk_ref, dv_ref, ka, va = refs[-5:]
    block, length = q_ref.shape[0], k_ref.shape[0]
    i = pl.program_id(0)
    start = window_start(i, block, window, length)
    span = pl.ds(start, window)

    @pl.when(i == 0)
    def _():
        ka[...] = jnp.zeros_like(ka)
        va[...] = jnp.zeros_like(va)

    q, d, k = q_ref[...], d_ref[...], k_ref[span, :]
    scores = scores_of(q, k, b_ref[...], i * block, start, scale)
    attention = jnp.exp(scores - lse_ref[...])
    prob_grad = mm_nt(v_ref[span, :], d)
    center = jnp.sum(attention * prob_grad, axis=0, keepdims=True)
    score_grad = (attention * (prob_grad - center)).astype(bf16)
    dq_ref[...] = (mm_tn(score_grad, k) * scale).astype(bf16)
    ka[span, :] += mm(score_grad, q) * scale
    va[span, :] += mm(attention.astype(bf16), d)

    @pl.when(i == pl.num_programs(0) - 1)
    def _():
        dk_ref[...] = ka[...].astype(bf16)
        dv_ref[...] = va[...].astype(bf16)


def attend_back(q, d, k, v, begins, lse, scale, *others):
    length, width = q.shape
    window = min(QB + SEGMAX, length)
    full = pl.BlockSpec((length, width), lambda i: (0, 0))
    rows = pl.BlockSpec((QB, width), lambda i: (i, 0))
    line = pl.BlockSpec((1, QB), lambda i: (0, i))
    return pl.pallas_call(
        functools.partial(attend_back_kernel, scale, window),
        grid=(length // QB,),
        in_specs=[rows, rows, full, full, line, line]
        + [pl.BlockSpec(memory_space=pl.ANY)] * len(others),
        out_specs=[rows, full, full],
        out_shape=[jax.ShapeDtypeStruct((length, width), bf16)] * 3,
        scratch_shapes=[pltpu.VMEM((length, width), f32)] * 2,
        compiler_params=params(),
        cost_estimate=cost(10 * length * window * width, 8 * nbytes(q), length * window),
    )(q, d, k, v, begins, lse, *others)


def shampoo_kernel(g_ref, ls_ref, rs_ref, lr_ref, rr_ref, w_ref, go_ref, lo_ref, ro_ref, wo_ref):
    g = g_ref[0]
    go_ref[0] = g.astype(f32)
    lo_ref[0] = decay_rate * ls_ref[0] + (1.0 - decay_rate) * mm_nt(g, g)
    ro_ref[0] = decay_rate * rs_ref[0] + (1.0 - decay_rate) * mm_tn(g, g)
    middle = mm(lr_ref[0].astype(bf16), g).astype(bf16)
    wo_ref[0] = w_ref[0] - step_rate * mm(middle, rr_ref[0].astype(bf16))


def shampoo(g, *rest):
    slots, side, _ = g.shape
    spec = pl.BlockSpec((1, side, side), lambda s: (s, 0, 0))
    return pl.pallas_call(
        shampoo_kernel,
        grid=(slots,),
        in_specs=[spec] * 6,
        out_specs=[spec] * 4,
        out_shape=[jax.ShapeDtypeStruct(g.shape, f32)] * 4,
        compiler_params=params(),
        cost_estimate=cost(8 * slots * side**3, 38 * g.size),
    )(g, *rest)


def rms_norm(values, gain_vec):
    return (
        values * lax.rsqrt(jnp.mean(values * values, axis=-1, keepdims=True) + epsilon) * gain_vec
    )


def begins_of(segment_row):
    length = segment_row.shape[0]
    indices = jnp.arange(length, dtype=jnp.int32)
    earlier = jnp.concatenate([jnp.full((1,), -1, jnp.int32), segment_row[:-1]])
    return lax.cummax(jnp.where(segment_row != earlier, indices, 0), axis=0)


UP = [(i, (i + 1) % Z) for i in range(Z)]


def ring_gather(block, first_use=None):
    blocks = [block]
    for k in range(Z - 1):
        blocks.append(lax.ppermute(blocks[-1], "hz", UP))
        if k == 0 and first_use:
            used = first_use(blocks[:2])
        if k == 1 and first_use:
            blocks[2] = after(blocks[2], used[0])
    return (blocks, used) if first_use else blocks


def ring_scatter(part_of):
    total = part_of(1).astype(bf16)
    for k in (2, 3):
        total = (lax.ppermute(total, "hz", UP).astype(f32) + part_of(k)).astype(bf16)
    return lax.ppermute(total, "hz", UP).astype(f32) + part_of(0)


def none_kernel(*refs):
    pass


def after(value, *others):
    anywhere = pl.BlockSpec(memory_space=pl.ANY)
    return pl.pallas_call(
        none_kernel,
        in_specs=[anywhere] * (1 + len(others)),
        out_specs=anywhere,
        out_shape=jax.ShapeDtypeStruct(value.shape, value.dtype),
        input_output_aliases={0: 0},
    )(value, *others)


def exchange_z(part_for):
    got = [part_for(0)]
    for j in range(1, Z):
        got.append(lax.ppermute(part_for(j), "hz", [(i, (i + j) % Z) for i in range(Z)]))
    return jnp.stack(got)


def swap(value, bit):
    size = lax.axis_size("hp")
    return lax.ppermute(value, "hp", [(i, i ^ bit) for i in range(size)])


def plane_scatter(pieces):
    PN, S = lax.axis_size("hp"), lax.axis_size("seq")
    if S != 2 or PN != 4:
        return lax.psum_scatter(pieces, ("hp", "seq"), scatter_dimension=0, tiled=False)
    p = lax.axis_index("hp")
    chip = sum_seq_scatter(pieces.reshape((PN, S) + pieces.shape[1:]), 1)
    half = chip.shape[1] // 2

    def add(mine, got):
        return (mine.astype(f32) + got.astype(f32)).astype(bf16)

    def pair(values, first, second):
        return jnp.take(values, jnp.stack([p ^ first, p ^ second]), axis=0, mode="clip")

    one, two = chip[:, :half], chip[:, half:]
    one_got, two_got = swap(pair(one, 1, 3), 1), swap(pair(two, 2, 3), 2)
    one, two = add(pair(one, 0, 2), one_got), add(pair(two, 0, 1), two_got)
    one_got, two_got = swap(one[1], 2), swap(two[1], 1)
    return jnp.concatenate([add(one[0], one_got), add(two[0], two_got)])


def from_group(values):
    size = lax.axis_size(GROUP)
    spread = jnp.broadcast_to(values, (size,) + values.shape)
    return lax.all_to_all(spread, GROUP, 0, 0, tiled=True)


def sum_seq_scatter(values, axis):
    S = lax.axis_size("seq")
    if S != 2:
        return lax.psum_scatter(values, "seq", scatter_dimension=axis, tiled=False)
    c = lax.axis_index("seq")
    mine = lax.dynamic_index_in_dim(values, c, axis, keepdims=False)
    other = lax.dynamic_index_in_dim(values, 1 - c, axis, keepdims=False)
    got = lax.ppermute(other, "seq", [(0, 1), (1, 0)])
    return (mine.astype(f32) + got.astype(f32)).astype(bf16)


def body(
    tokens,
    cotangent,
    segment_ids,
    owner_map,
    weights,
    norm_gains,
    left_stats,
    right_stats,
    left_root,
    right_root,
):
    model_width = tokens.shape[2]
    local_count = tokens.shape[1]
    slots, side = weights.shape[0], weights.shape[1]
    total_blocks = owner_map.shape[0]
    PN, S = lax.axis_size("hp"), lax.axis_size("seq")
    n = Z * PN * S
    rep = PN * S
    rows = side // n
    part = Z * rows
    head_size = model_width // HEADS
    quarter = model_width // Z
    score_scale = head_size ** (-0.5)
    zi, pi = lax.axis_index("hz"), lax.axis_index("hp")
    relative = (zi - jnp.arange(Z, dtype=jnp.int32)) % Z
    inputs = tokens[0]

    def zero_of(value):
        entry = value[(0,) * value.ndim]
        if value.dtype == jnp.int32:
            return (entry < 0).astype(jnp.int32)
        return (entry != entry).astype(jnp.int32)

    D, F = model_width // side, FF // side
    number = jnp.arange(total_blocks, dtype=jnp.int32)
    square, tall = D * D, D * F
    qkv_list = number[: 3 * square].reshape(3, D, Z).transpose(2, 1, 0)
    out_list = number[3 * square : 4 * square].reshape(Z, D, 1)
    attn_list = jnp.concatenate([qkv_list, out_list], axis=2).reshape(Z, -1)
    gateup_list = number[4 * square : 4 * square + 2 * tall].reshape(2, D, Z, F // Z)
    gateup_list = gateup_list.transpose(2, 1, 0, 3).reshape(Z, -1)
    down_list = number[4 * square + 2 * tall :].reshape(Z, -1)
    inverse = jnp.zeros((total_blocks,), jnp.int32).at[owner_map].set(number)

    low = weights.astype(bf16).reshape(slots, PN, S, Z, rows, side)
    low = low.transpose(3, 1, 2, 0, 4, 5).reshape(n * slots, rows, side)
    spread = lax.all_to_all(low, EVERY, 0, 0, tiled=True)
    tokens_g = lax.all_gather(inputs, "hz", axis=0, tiled=True)

    group, group_tokens = Z * PN, Z * local_count

    def fetch(numbers, *others):
        places = inverse[numbers.reshape(-1)]
        for other in others:
            places = places + zero_of(other)
        picked = jnp.take(spread, places, axis=0, mode="clip")
        got = lax.all_to_all(picked, "hz", 0, 0, tiled=True)
        return got.reshape(Z, -1, rows, side).transpose(1, 0, 2, 3).reshape(-1, part, side)

    def all_plane(got, R):
        got = lax.all_gather(got, ("hp", "seq"), axis=0, tiled=False)
        return got.reshape(rep, R, -1, part, side)

    got_attn = fetch(attn_list, tokens_g)
    w_attn = all_plane(got_attn, D)
    def fetch_beside(numbers, other):
        def part_for(j):
            wanted = lax.dynamic_index_in_dim(numbers, (zi + j) % Z, 0, keepdims=False)
            return jnp.take(spread, inverse[wanted] + zero_of(other), axis=0, mode="clip")

        got = jnp.take(exchange_z(part_for), relative, axis=0, mode="clip")
        return got.transpose(1, 0, 2, 3).reshape(-1, part, side)

    w_gateup = all_plane(fetch_beside(gateup_list, got_attn), D)

    def rope(values, sign):
        first, second = values[:, :half_size], values[:, half_size:]
        return jnp.concatenate(
            [first * cosine - second * sine * sign, second * cosine + first * sine * sign], axis=-1
        )

    head = zi * PN + pi
    gains_head = lax.dynamic_slice_in_dim(norm_gains[2:4], head * head_size, head_size, axis=1)

    def to_heads(stack):
        m = stack.shape[0]
        shaped = stack.reshape(m, Z, local_count, PN, head_size).transpose(3, 0, 1, 2, 4)
        got = lax.all_to_all(shaped, "hp", 0, 0, tiled=True)
        return got.transpose(1, 2, 0, 3, 4).reshape(m, length, head_size)

    def to_groups(stack):
        m = stack.shape[0]
        shaped = stack.reshape(m, Z, PN, local_count, head_size).transpose(2, 0, 1, 3, 4)
        got = lax.all_to_all(shaped, "hp", 0, 0, tiled=True)
        return got.transpose(1, 2, 3, 0, 4).reshape(m, group_tokens, quarter)

    raw = nn(tokens_g, w_attn, columns=3)
    raw_three = raw.reshape(group_tokens, 3, quarter).transpose(1, 0, 2)
    squares = jnp.sum(raw_three[:2] * raw_three[:2], axis=-1)
    ids = jnp.pad(segment_ids.astype(f32), ((0, 0), (0, group_tokens - local_count)))
    shared = from_group(jnp.concatenate([squares, ids])).reshape(Z, PN, 3, Z, local_count)
    squares, row_ids = shared[:, :, :2], shared[:, :, 2, 0].reshape(-1).astype(jnp.int32)
    length = row_ids.shape[0]
    begins = begins_of(row_ids)
    places = jnp.arange(length, dtype=jnp.int32) - begins
    half_size = head_size // 2
    frequency = rope_base ** (-2.0 * jnp.arange(half_size, dtype=f32) / head_size)
    angles = places.astype(f32)[:, None] * frequency[None, :]
    cosine, sine = jnp.cos(angles), jnp.sin(angles)

    squares = jnp.sum(squares, axis=0).transpose(1, 2, 0, 3).reshape(2, length, 1)
    raw_row = to_heads(raw_three.astype(bf16))
    invs = lax.rsqrt(squares / model_width + epsilon)
    query_hat, key_hat = (raw_row[i].astype(f32) * invs[i] for i in range(2))
    query_row = rope(query_hat * gains_head[0], 1.0).astype(bf16)
    key_row = rope(key_hat * gains_head[1], 1.0).astype(bf16)
    value_row = raw_row[2]

    got_down = fetch_beside(down_list, squares)

    begin_line = begins[None, :]
    mixed, log_sums = attend(query_row, key_row, value_row, begin_line, score_scale)
    attended = to_groups(mixed[None]).reshape(Z, local_count, quarter)
    attended_rel = jnp.take(attended, relative, axis=0, mode="clip")
    attn_parts = [nn(attended_rel[k], w_attn, row=3) for k in range(Z)]
    attn_raw = ring_scatter(lambda k: attn_parts[k])
    w_down = all_plane(after(got_down, w_gateup, attn_parts[1]), F // Z)
    resid = inputs.astype(f32) + rms_norm(attn_raw, norm_gains[0])

    resid_blocks, near = ring_gather(resid.astype(bf16), lambda pair: gate_up(pair, w_gateup))

    tokens_z = tokens_g.reshape(Z, local_count, model_width)
    middle = local_count // 2
    tok_one, tok_two = after(tokens_z[:, :middle], resid), after(tokens_z[:, middle:], resid)
    tok_one = jnp.stack([tok_one, swap(tok_one, 1)])
    tok_two = jnp.stack([tok_two, swap(tok_two, 2)])
    tok_parts = [tok_one, swap(tok_one, 2), tok_two, swap(tok_two, 1)]
    tok_parts = [t.reshape(-1, model_width) for t in tok_parts]
    tok_near, tok_far = tok_parts[::2], tok_parts[1::2]
    gates, ups, hiddens = zip(near, gate_up(resid_blocks[2:], w_gateup))

    def entry(halves, k):
        return halves[k // 2][k % 2 * local_count : (k % 2 + 1) * local_count]

    downs = [nn(hiddens[0], w_down), nn(hiddens[1], w_down, *tok_near)]
    down_raw = ring_scatter(lambda k: entry(downs, k))
    output = (resid + rms_norm(down_raw, norm_gains[1])).astype(bf16)[None]

    upstream = cotangent[0].astype(f32)
    _, down_norm_back = jax.vjp(rms_norm, down_raw, norm_gains[1])
    down_grad, gain_mlp_grad = down_norm_back(upstream)
    down_blocks, near = ring_gather(
        down_grad.astype(bf16),
        lambda pair: [hidden_back(pair, w_down, gates[0], ups[0])],
    )
    gateup_grads = near + [hidden_back(down_blocks[2:], w_down, gates[1], ups[1], *tok_far)]

    def spread_z(summed):
        summed = summed.reshape(-1, Z, rows, side)
        return exchange_z(
            lambda j: lax.dynamic_index_in_dim(summed, (zi + j) % Z, 1, keepdims=False)
        )

    def blocks_of(pieces):
        return pieces.reshape(rep, -1, part, side)

    def sum_plane(pieces):
        return lax.psum_scatter(
            blocks_of(pieces), ("hp", "seq"), scatter_dimension=0, tiled=False
        )

    down_pieces = tn(hiddens, [b[None] for b in down_blocks], rep, side, spare=quarter // side)
    gate_pieces = tn(resid_blocks, gateup_grads, rep, side, only=0)
    up_pieces = tn(resid_blocks, gateup_grads, rep, side, only=1)
    gate_sum = sum_plane(gate_pieces)
    up_sum = sum_plane(up_pieces)
    resid_parts = [nt([gateup_grads[0]], w_gateup), nt([gateup_grads[1]], w_gateup)]
    resid_grad = upstream + ring_scatter(lambda k: entry(resid_parts, k))

    _, attn_norm_back = jax.vjp(rms_norm, attn_raw, norm_gains[0])
    attn_grad, gain_attn_grad = attn_norm_back(resid_grad)
    attn_low = attn_grad.astype(bf16)
    attn_blocks = ring_gather(attn_low)
    grad_rel = nt([b[None] for b in attn_blocks], w_attn, row=3).astype(bf16)
    grad_rel = grad_rel.reshape(Z, local_count, quarter)
    grad_abs = jnp.take(grad_rel, relative, axis=0, mode="clip")
    grad_row = to_heads(grad_abs.reshape(1, group_tokens, quarter))[0]
    last_pieces = tn(
        [attended_rel[k] for k in range(Z)],
        [b[None] for b in attn_blocks],
        rep,
        side,
        base=down_pieces,
    )
    last_sum = sum_plane(last_pieces)
    gate_sent = spread_z(after(gate_sum, grad_abs))
    query_grad, key_grad, value_grad = attend_back(
        query_row,
        grad_row,
        key_row,
        value_row,
        begin_line,
        log_sums,
        score_scale,
    )
    query_turn, key_turn = rope(query_grad.astype(f32), -1.0), rope(key_grad.astype(f32), -1.0)
    gain_query = jnp.sum(query_turn * query_hat, axis=0)
    gain_key = jnp.sum(key_turn * key_hat, axis=0)
    query_turn, key_turn = query_turn * gains_head[0], key_turn * gains_head[1]
    dots = jnp.stack([jnp.sum(query_turn * query_hat, -1), jnp.sum(key_turn * key_hat, -1)])
    dots = jnp.sum(from_group(dots).reshape(group, 2, length), axis=0) / model_width
    up_sent, down_sent = spread_z(after(up_sum, dots)), spread_z(last_sum)
    dots = dots[..., None]
    query_back = ((query_turn - query_hat * dots[0]) * invs[0]).astype(bf16)
    key_back = ((key_turn - key_hat * dots[1]) * invs[1]).astype(bf16)

    back_row = jnp.concatenate([query_back, key_back, value_grad], axis=1)
    by_half = back_row.reshape(Z, PN, 2, middle, 3 * head_size).transpose(1, 2, 0, 3, 4)

    def rows_of(half, *bits):
        picked = jnp.take(by_half[:, half], jnp.stack([pi ^ bit for bit in bits]), axis=0, mode="clip")
        return picked.reshape(-1, 3 * head_size)

    back_parts = [rows_of(0, 0, 1), rows_of(0, 2, 3), rows_of(1, 0, 2), rows_of(1, 1, 3)]
    heads_grad = heads_tn(tok_parts, back_parts, rep, side, gate_sent)
    heads_sum = sum_seq_scatter(heads_grad.reshape(PN, S, D, part, 3 * head_size), 1)
    heads_sum = heads_sum.reshape(PN, D, Z, rows, 3 * head_size).transpose(2, 0, 1, 3, 4)
    heads_sent = lax.all_to_all(
        heads_sum.reshape(group, D, rows, 3 * head_size), GROUP, 0, 0, tiled=True
    ).reshape(Z, PN, D, rows, 3, head_size)
    heads_sent = heads_sent.transpose(4, 2, 0, 3, 1, 5).reshape(3 * square, rows, side)

    back_abs = to_groups(jnp.stack([query_back, key_back, value_grad]))
    back_rel = jnp.take(
        back_abs.reshape(3, Z, local_count, quarter), relative, axis=1, mode="clip"
    )
    near_back = nt([back_rel[:, 0], back_rel[:, 1]], w_attn, up_sent, heads_grad)
    back_parts = [near_back, nt([back_rel[:, 2], back_rel[:, 3]], w_attn)]
    input_grad = resid_grad + ring_scatter(lambda k: entry(back_parts, k))


    spots = jnp.zeros((2, model_width), f32)
    spots = lax.dynamic_update_slice(spots, jnp.stack([gain_query, gain_key]), (0, head * head_size))
    gain_local = jnp.concatenate([jnp.stack([gain_attn_grad, gain_mlp_grad]), spots])
    shares = lax.all_to_all(gain_local.reshape(n, -1), EVERY, 0, 0, tiled=True)
    share = jnp.sum(shares, axis=0)
    gain_grads = lax.all_to_all(
        jnp.broadcast_to(share, (n, share.shape[0])), EVERY, 0, 0, tiled=True
    ).reshape(gain_local.shape)

    flat = [heads_sent, gate_sent, up_sent, down_sent]
    sent = jnp.concatenate([a.reshape(-1, rows, side) for a in flat])
    split = gateup_list.reshape(Z, D, 2, -1)
    last = jnp.concatenate([down_list, out_list.reshape(Z, -1)], axis=1)
    order = [split[:, :, 0], split[:, :, 1], last]
    order = [jnp.take(o.reshape(Z, -1), relative, axis=0, mode="clip").reshape(-1) for o in order]
    order = jnp.concatenate([number[: 3 * square]] + order)
    where_is = jnp.zeros((total_blocks,), jnp.int32).at[order].set(number)
    to_slots = jnp.take(sent, where_is[owner_map] + zero_of(input_grad), axis=0, mode="clip")
    got = lax.all_to_all(to_slots, EVERY, 0, 0, tiled=True)
    got = got.reshape(Z, PN, S, slots, rows, side).transpose(3, 1, 2, 0, 4, 5)
    grad_slots, left_new, right_new, new_weights = shampoo(
        got.reshape(slots, side, side), left_stats, right_stats, left_root, right_root, weights
    )
    new_gains = norm_gains - gain_rate * gain_grads * lax.rsqrt(
        jnp.mean(gain_grads * gain_grads, axis=1, keepdims=True) + epsilon
    )
    return (
        output,
        input_grad[None],
        grad_slots,
        left_new,
        right_new,
        new_weights,
        gain_grads,
        new_gains,
    )


def solution(mesh):
    heads, seqs = mesh.shape["head"], mesh.shape["seq"]
    fine = Mesh(mesh.devices.reshape(Z, heads // Z, seqs), EVERY)
    tok = P("seq", GROUP, None)
    slot = P(EVERY, None, None)
    return jax.shard_map(
        body,
        mesh=fine,
        in_specs=(tok, tok, P("seq", GROUP), P(), slot, P(), slot, slot, slot, slot),
        out_specs=(tok, tok, slot, slot, slot, slot, P(), P()),
        check_vma=False,
    )
```

```python
import functools

import jax
import jax.numpy as jnp
from jax import lax
from jax.experimental import pallas as pl
from jax.experimental.pallas import tpu as pltpu
from jax.sharding import Mesh
from jax.sharding import PartitionSpec as P

FF = 8192
HEADS = 16
SEGMAX = 1024
QB = 256
Z = 4

epsilon = 1e-06
rope_base = 500000.0
decay_rate = 0.5
step_rate = 0.5
gain_rate = 0.3
bf16 = jnp.bfloat16
f32 = jnp.float32
EVERY = ("hz", "hp", "seq")
GROUP = ("hz", "hp")
VMEM_LIMIT = 48 * 1024 * 1024


def mm(left_side, right_side):
    return jnp.dot(left_side, right_side, preferred_element_type=f32)


def mm_nt(left_side, right_side):
    return lax.dot_general(
        left_side, right_side, (((1,), (1,)), ((), ())), preferred_element_type=f32
    )


def mm_tn(left_side, right_side):
    return lax.dot_general(
        left_side, right_side, (((0,), (0,)), ((), ())), preferred_element_type=f32
    )


def params():
    return pltpu.CompilerParams(vmem_limit_bytes=VMEM_LIMIT)


def cost(flops, nbytes, exps=0):
    part = 0.1
    return pl.CostEstimate(
        flops=int(part * flops), bytes_accessed=int(part * nbytes), transcendentals=int(part * exps)
    )


def nbytes(*arrays):
    return sum(a.size * a.dtype.itemsize for a in arrays)


def join(refs):
    return refs[0][...] if len(refs) == 1 else jnp.concatenate([r[...] for r in refs], axis=-2)


def whole(array):
    return pl.BlockSpec(array.shape, lambda *_: (0,) * array.ndim)


def gate_up_kernel(*refs):
    *x_refs, g_ref, u_ref, gate_ref, up_ref, hidden_ref = refs
    x, side = join(x_refs), g_ref.shape[-1]
    for w_ref, y_ref in ((g_ref, gate_ref), (u_ref, up_ref)):
        total = None
        for r in range(w_ref.shape[1]):
            part = mm(x[:, r * side : (r + 1) * side], w_ref[:, r, 0].reshape(side, side))
            total = part if total is None else total + part
        y_ref[...] = total
    gate = gate_ref[...]
    hidden_ref[...] = (gate * jax.nn.sigmoid(gate) * up_ref[...]).astype(bf16)


def gate_up(xs, w):
    rep, R, C, part, side = w.shape
    count, half = sum(x.shape[0] for x in xs), C // 2
    wide = jax.ShapeDtypeStruct((count, half * side), f32)
    outs = [wide, wide, jax.ShapeDtypeStruct((count, half * side), bf16)]
    col = pl.BlockSpec((count, side), lambda c: (0, c))
    return pl.pallas_call(
        gate_up_kernel,
        grid=(half,),
        in_specs=[
            *[whole(x) for x in xs],
            pl.BlockSpec((rep, R, 1, part, side), lambda c: (0, 0, c, 0, 0)),
            pl.BlockSpec((rep, R, 1, part, side), lambda c: (0, 0, c + half, 0, 0)),
        ],
        out_specs=[col, col, col],
        out_shape=outs,
        compiler_params=params(),
        cost_estimate=cost(2 * count * R * C * side * side, nbytes(*xs, w, *outs)),
    )(*xs, w, w)


def nn_kernel(x_ref, w_ref, *refs):
    y_ref = refs[-1]
    side = w_ref.shape[-1]
    total = None
    for r in range(w_ref.shape[1]):
        part = mm(x_ref[:, r * side : (r + 1) * side], w_ref[:, r, 0].reshape(side, side))
        total = part if total is None else total + part
    y_ref[...] = total


def nn(x, w, *others, columns=None, row=None):
    rep, R, C, part, side = w.shape
    count = x.shape[0]
    if row is None:
        block, index = (rep, R, 1, part, side), lambda c: (0, 0, c, 0, 0)
        steps = columns or C
    else:
        block, index = (rep, 1, 1, part, side), lambda c: (0, c, row, 0, 0)
        steps = R
    out = jax.ShapeDtypeStruct((count, steps * side), f32)
    return pl.pallas_call(
        nn_kernel,
        grid=(steps,),
        in_specs=[pl.BlockSpec(x.shape, lambda c: (0, 0)), pl.BlockSpec(block, index)]
        + [pl.BlockSpec(memory_space=pl.ANY)] * len(others),
        out_specs=pl.BlockSpec((count, side), lambda c: (0, c)),
        out_shape=out,
        compiler_params=params(),
        cost_estimate=cost(
            2 * count * x.shape[1] * steps * side, nbytes(x, out) + 2 * x.shape[1] * steps * side
        ),
    )(x, w, *others)


def hidden_back_kernel(half, *refs):
    w_ref, gate_ref, up_ref = refs[half : half + 3]
    x, y_ref, side = join(refs[:half]), refs[-1], w_ref.shape[-1]
    total = None
    for c in range(w_ref.shape[2]):
        part = mm_nt(x[:, c * side : (c + 1) * side], w_ref[:, 0, c].reshape(side, side))
        total = part if total is None else total + part
    gate = gate_ref[...]
    sigma = jax.nn.sigmoid(gate)
    y_ref[0] = (total * up_ref[...] * sigma * (1.0 + gate * (1.0 - sigma))).astype(bf16)
    y_ref[1] = (total * gate * sigma).astype(bf16)


def hidden_back(xs, w, gate, up, *others):
    rep, R, C, part, side = w.shape
    count = gate.shape[0]
    out = jax.ShapeDtypeStruct((2, count, R * side), bf16)
    col = pl.BlockSpec((count, side), lambda r: (0, r))
    return pl.pallas_call(
        functools.partial(hidden_back_kernel, len(xs)),
        grid=(R,),
        in_specs=[
            *[whole(x) for x in xs],
            pl.BlockSpec((rep, 1, C, part, side), lambda r: (0, r, 0, 0, 0)),
            col,
            col,
            *[pl.BlockSpec(memory_space=pl.ANY)] * len(others),
        ],
        out_specs=pl.BlockSpec((2, count, side), lambda r: (0, 0, r)),
        out_shape=out,
        compiler_params=params(),
        cost_estimate=cost(2 * count * R * C * side * side, nbytes(*xs, w, gate, up, out)),
    )(*xs, w, gate, up, *others)


def nt_kernel(half, *refs):
    x, w_ref, y_ref = join(refs[:half]), refs[half], refs[-1]
    side = w_ref.shape[-1]
    per = x.shape[2] // side
    total = None
    for c in range(w_ref.shape[1] * w_ref.shape[2]):
        left = x[c // per, :, (c % per) * side : (c % per + 1) * side]
        w = w_ref[:, c // w_ref.shape[2], c % w_ref.shape[2]].reshape(side, side)
        part = mm_nt(left, w)
        total = part if total is None else total + part
    y_ref[...] = total


def nt(xs, w, *others, row=None):
    rep, R, C, part, side = w.shape
    count, depth = sum(x.shape[1] for x in xs), xs[0].shape[0] * xs[0].shape[2]
    if row is None:
        block, index = (rep, 1, depth // side, part, side), lambda r: (0, r, 0, 0, 0)
        steps = R
    else:
        block, index = (rep, R, 1, part, side), lambda r: (0, 0, row, 0, 0)
        steps = 1
    out = jax.ShapeDtypeStruct((count, steps * side), f32)
    return pl.pallas_call(
        functools.partial(nt_kernel, len(xs)),
        grid=(steps,),
        in_specs=[
            *[whole(x) for x in xs],
            pl.BlockSpec(block, index),
            *[pl.BlockSpec(memory_space=pl.ANY)] * len(others),
        ],
        out_specs=pl.BlockSpec((count, side), lambda r: (0, r)),
        out_shape=out,
        compiler_params=params(),
        cost_estimate=cost(
            2 * count * depth * steps * side, nbytes(*xs, out) + 2 * depth * steps * side
        ),
    )(*xs, w, *others)


def tn_kernel(lefts, rights, *refs):
    y_ref = refs[-1]
    rep, _, _, part, side = y_ref.shape
    left, right = join(refs[:lefts]), join(refs[lefts : lefts + rights])
    whole_row = mm_tn(left, right[0]).astype(bf16)
    for c in range(y_ref.shape[2]):
        block = whole_row[:, c * side : (c + 1) * side]
        y_ref[:, 0, c] = block.reshape(rep, part, side)


def tn(lefts, rights, rep, side, *others, only=None, spare=0, base=None):
    R = lefts[0].shape[1] // side
    m, per = rights[0].shape[0], rights[0].shape[2] // side
    first, steps = (0, m) if only is None else (only, 1)
    C = steps * per
    out = jax.ShapeDtypeStruct((rep, R + spare, C, side // rep, side), bf16)
    start, aliases = 0, {}
    if base is not None:
        out = jax.ShapeDtypeStruct(base.shape, base.dtype)
        start, others = base.shape[1] - R, (*others, base)
        aliases = {len(lefts) + len(rights) + len(others) - 1: 0}
    total = sum(x.shape[0] for x in lefts)
    return pl.pallas_call(
        functools.partial(tn_kernel, len(lefts), len(rights)),
        grid=(steps, R),
        in_specs=[pl.BlockSpec((x.shape[0], side), lambda j, r: (0, r)) for x in lefts]
        + [
            pl.BlockSpec((1, x.shape[1], per * side), lambda j, r: (first + j, 0, 0))
            for x in rights
        ]
        + [pl.BlockSpec(memory_space=pl.ANY)] * len(others),
        out_specs=pl.BlockSpec(
            (rep, 1, per, side // rep, side), lambda j, r: (0, start + r, j, 0, 0)
        ),
        out_shape=out,
        input_output_aliases=aliases,
        compiler_params=params(),
        cost_estimate=cost(2 * total * R * C * side * side, nbytes(*lefts, *rights, out)),
    )(*lefts, *rights, *others)


def heads_kernel(half, *refs):
    y_ref = refs[-1]
    rep, _, part, width = y_ref.shape
    left = jnp.concatenate([r[...] for r in refs[:half]], axis=0)
    right = jnp.concatenate([r[...] for r in refs[half : 2 * half]], axis=0)
    y_ref[:, 0] = mm_tn(left, right).astype(bf16).reshape(rep, part, width)


def heads_tn(lefts, rights, rep, side, *others):
    count, R = lefts[0].shape[0], lefts[0].shape[1] // side
    width = rights[0].shape[1]
    out = jax.ShapeDtypeStruct((rep, R, side // rep, width), bf16)
    return pl.pallas_call(
        functools.partial(heads_kernel, len(lefts)),
        grid=(R,),
        in_specs=[pl.BlockSpec((count, side), lambda r: (0, r))] * len(lefts)
        + [pl.BlockSpec((count, width), lambda r: (0, 0))] * len(rights)
        + [pl.BlockSpec(memory_space=pl.ANY)] * len(others),
        out_specs=pl.BlockSpec((rep, 1, side // rep, width), lambda r: (0, r, 0, 0)),
        out_shape=out,
        compiler_params=params(),
        cost_estimate=cost(
            2 * count * len(lefts) * R * side * width, nbytes(*lefts, *rights, out)
        ),
    )(*lefts, *rights, *others)


def scores_of(q, k, begin, q_start, k_start, scale):
    scores = mm_nt(k, q) * scale
    key_place = k_start + lax.broadcasted_iota(jnp.int32, scores.shape, 0)
    query_place = q_start + lax.broadcasted_iota(jnp.int32, scores.shape, 1)
    return jnp.where((key_place >= begin) & (key_place <= query_place), scores, -1e30)


def by_window(block, window, work):
    i, full = pl.program_id(0), window // block

    for j in range(full - 1):

        @pl.when(i == j)
        def _(j=j):
            work(0, (j + 1) * block)

    @pl.when(i >= full - 1)
    def _():
        work(pl.multiple_of((i + 1) * block - window, 128), window)


def attend_kernel(scale, window, q_ref, k_ref, v_ref, b_ref, o_ref, lse_ref):
    block = q_ref.shape[0]

    def work(start, size):
        span = pl.ds(start, size)
        scores = scores_of(
            q_ref[...], k_ref[span, :], b_ref[...], pl.program_id(0) * block, start, scale
        )
        top = jnp.max(scores, axis=0, keepdims=True)
        expo = jnp.exp(scores - top)
        total = jnp.sum(expo, axis=0, keepdims=True)
        attention = (expo * (1.0 / total)).astype(bf16)
        o_ref[...] = mm_tn(attention, v_ref[span, :]).astype(bf16)
        lse_ref[...] = top + jnp.log(total)

    by_window(block, window, work)


def attend(q, k, v, begins, scale):
    length, width = q.shape
    window = min(QB + SEGMAX, length)
    full = pl.BlockSpec((length, width), lambda i: (0, 0))
    rows = pl.BlockSpec((QB, width), lambda i: (i, 0))
    line = pl.BlockSpec((1, QB), lambda i: (0, i))
    return pl.pallas_call(
        functools.partial(attend_kernel, scale, window),
        grid=(length // QB,),
        in_specs=[rows, full, full, line],
        out_specs=[rows, line],
        out_shape=[
            jax.ShapeDtypeStruct((length, width), bf16),
            jax.ShapeDtypeStruct((1, length), f32),
        ],
        compiler_params=params(),
        cost_estimate=cost(4 * length * window * width, 4 * nbytes(q), length * window),
    )(q, k, v, begins)


def attend_back_kernel(
    scale, window, q_ref, d_ref, k_ref, v_ref, b_ref, lse_ref, *refs
):
    dq_ref, dk_ref, dv_ref, ka, va = refs[-5:]
    block, i = q_ref.shape[0], pl.program_id(0)

    @pl.when(i == 0)
    def _():
        ka[...] = jnp.zeros_like(ka)
        va[...] = jnp.zeros_like(va)

    def work(start, size):
        span = pl.ds(start, size)
        q, d, k = q_ref[...], d_ref[...], k_ref[span, :]
        scores = scores_of(q, k, b_ref[...], i * block, start, scale)
        attention = jnp.exp(scores - lse_ref[...])
        prob_grad = mm_nt(v_ref[span, :], d)
        center = jnp.sum(attention * prob_grad, axis=0, keepdims=True)
        score_grad = (attention * (prob_grad - center)).astype(bf16)
        dq_ref[...] = (mm_tn(score_grad, k) * scale).astype(bf16)
        ka[span, :] += mm(score_grad, q) * scale
        va[span, :] += mm(attention.astype(bf16), d)

    by_window(block, window, work)

    @pl.when(i == pl.num_programs(0) - 1)
    def _():
        dk_ref[...] = ka[...].astype(bf16)
        dv_ref[...] = va[...].astype(bf16)


def attend_back(q, d, k, v, begins, lse, scale, *others):
    length, width = q.shape
    window = min(QB + SEGMAX, length)
    full = pl.BlockSpec((length, width), lambda i: (0, 0))
    rows = pl.BlockSpec((QB, width), lambda i: (i, 0))
    line = pl.BlockSpec((1, QB), lambda i: (0, i))
    return pl.pallas_call(
        functools.partial(attend_back_kernel, scale, window),
        grid=(length // QB,),
        in_specs=[rows, rows, full, full, line, line]
        + [pl.BlockSpec(memory_space=pl.ANY)] * len(others),
        out_specs=[rows, full, full],
        out_shape=[jax.ShapeDtypeStruct((length, width), bf16)] * 3,
        scratch_shapes=[pltpu.VMEM((length, width), f32)] * 2,
        compiler_params=params(),
        cost_estimate=cost(10 * length * window * width, 8 * nbytes(q), length * window),
    )(q, d, k, v, begins, lse, *others)


def shampoo_kernel(g_ref, ls_ref, rs_ref, lr_ref, rr_ref, w_ref, go_ref, lo_ref, ro_ref, wo_ref):
    g = g_ref[0]
    go_ref[0] = g.astype(f32)
    lo_ref[0] = decay_rate * ls_ref[0] + (1.0 - decay_rate) * mm_nt(g, g)
    ro_ref[0] = decay_rate * rs_ref[0] + (1.0 - decay_rate) * mm_tn(g, g)
    middle = mm(lr_ref[0].astype(bf16), g).astype(bf16)
    wo_ref[0] = w_ref[0] - step_rate * mm(middle, rr_ref[0].astype(bf16))


def shampoo(g, *rest):
    slots, side, _ = g.shape
    spec = pl.BlockSpec((1, side, side), lambda s: (s, 0, 0))
    return pl.pallas_call(
        shampoo_kernel,
        grid=(slots,),
        in_specs=[spec] * 6,
        out_specs=[spec] * 4,
        out_shape=[jax.ShapeDtypeStruct(g.shape, f32)] * 4,
        compiler_params=params(),
        cost_estimate=cost(8 * slots * side**3, 38 * g.size),
    )(g, *rest)


def rms_norm(values, gain_vec):
    return (
        values * lax.rsqrt(jnp.mean(values * values, axis=-1, keepdims=True) + epsilon) * gain_vec
    )


def begins_of(segment_row):
    length = segment_row.shape[0]
    indices = jnp.arange(length, dtype=jnp.int32)
    earlier = jnp.concatenate([jnp.full((1,), -1, jnp.int32), segment_row[:-1]])
    return lax.cummax(jnp.where(segment_row != earlier, indices, 0), axis=0)


UP = [(i, (i + 1) % Z) for i in range(Z)]


def ring_gather(block, first_use=None):
    blocks = [block]
    for k in range(Z - 1):
        blocks.append(lax.ppermute(blocks[-1], "hz", UP))
        if k == 0 and first_use:
            used = first_use(blocks[:2])
        if k == 1 and first_use:
            blocks[2] = after(blocks[2], used[0])
    return (blocks, used) if first_use else blocks


def ring_scatter(part_of):
    total = part_of(1).astype(bf16)
    for k in (2, 3):
        total = (lax.ppermute(total, "hz", UP).astype(f32) + part_of(k)).astype(bf16)
    return lax.ppermute(total, "hz", UP).astype(f32) + part_of(0)


def none_kernel(*refs):
    pass


def after(value, *others):
    anywhere = pl.BlockSpec(memory_space=pl.ANY)
    return pl.pallas_call(
        none_kernel,
        in_specs=[anywhere] * (1 + len(others)),
        out_specs=anywhere,
        out_shape=jax.ShapeDtypeStruct(value.shape, value.dtype),
        input_output_aliases={0: 0},
    )(value, *others)


def exchange_z(part_for):
    got = [part_for(0)]
    for j in range(1, Z):
        got.append(lax.ppermute(part_for(j), "hz", [(i, (i + j) % Z) for i in range(Z)]))
    return jnp.stack(got)


def swap(value, bit):
    size = lax.axis_size("hp")
    return lax.ppermute(value, "hp", [(i, i ^ bit) for i in range(size)])


def plane_scatter(pieces):
    PN, S = lax.axis_size("hp"), lax.axis_size("seq")
    if S != 2 or PN != 4:
        return lax.psum_scatter(pieces, ("hp", "seq"), scatter_dimension=0, tiled=False)
    p = lax.axis_index("hp")
    chip = sum_seq_scatter(pieces.reshape((PN, S) + pieces.shape[1:]), 1)
    half = chip.shape[1] // 2

    def add(mine, got):
        return (mine.astype(f32) + got.astype(f32)).astype(bf16)

    def pair(values, first, second):
        return jnp.take(values, jnp.stack([p ^ first, p ^ second]), axis=0, mode="clip")

    one, two = chip[:, :half], chip[:, half:]
    one_got, two_got = swap(pair(one, 1, 3), 1), swap(pair(two, 2, 3), 2)
    one, two = add(pair(one, 0, 2), one_got), add(pair(two, 0, 1), two_got)
    one_got, two_got = swap(one[1], 2), swap(two[1], 1)
    return jnp.concatenate([add(one[0], one_got), add(two[0], two_got)])


def from_group(values):
    size = lax.axis_size(GROUP)
    spread = jnp.broadcast_to(values, (size,) + values.shape)
    return lax.all_to_all(spread, GROUP, 0, 0, tiled=True)


def sum_seq_scatter(values, axis):
    S = lax.axis_size("seq")
    if S != 2:
        return lax.psum_scatter(values, "seq", scatter_dimension=axis, tiled=False)
    c = lax.axis_index("seq")
    mine = lax.dynamic_index_in_dim(values, c, axis, keepdims=False)
    other = lax.dynamic_index_in_dim(values, 1 - c, axis, keepdims=False)
    got = lax.ppermute(other, "seq", [(0, 1), (1, 0)])
    return (mine.astype(f32) + got.astype(f32)).astype(bf16)


def body(
    tokens,
    cotangent,
    segment_ids,
    owner_map,
    weights,
    norm_gains,
    left_stats,
    right_stats,
    left_root,
    right_root,
):
    model_width = tokens.shape[2]
    local_count = tokens.shape[1]
    slots, side = weights.shape[0], weights.shape[1]
    total_blocks = owner_map.shape[0]
    PN, S = lax.axis_size("hp"), lax.axis_size("seq")
    n = Z * PN * S
    rep = PN * S
    rows = side // n
    part = Z * rows
    head_size = model_width // HEADS
    quarter = model_width // Z
    score_scale = head_size ** (-0.5)
    zi, pi = lax.axis_index("hz"), lax.axis_index("hp")
    relative = (zi - jnp.arange(Z, dtype=jnp.int32)) % Z
    inputs = tokens[0]

    def zero_of(value):
        entry = value[(0,) * value.ndim]
        if value.dtype == jnp.int32:
            return (entry < 0).astype(jnp.int32)
        return (entry != entry).astype(jnp.int32)

    D, F = model_width // side, FF // side
    number = jnp.arange(total_blocks, dtype=jnp.int32)
    square, tall = D * D, D * F
    qkv_list = number[: 3 * square].reshape(3, D, Z).transpose(2, 1, 0)
    out_list = number[3 * square : 4 * square].reshape(Z, D, 1)
    attn_list = jnp.concatenate([qkv_list, out_list], axis=2).reshape(Z, -1)
    gateup_list = number[4 * square : 4 * square + 2 * tall].reshape(2, D, Z, F // Z)
    gateup_list = gateup_list.transpose(2, 1, 0, 3).reshape(Z, -1)
    down_list = number[4 * square + 2 * tall :].reshape(Z, -1)
    inverse = jnp.zeros((total_blocks,), jnp.int32).at[owner_map].set(number)

    low = weights.astype(bf16).reshape(slots, PN, S, Z, rows, side)
    low = low.transpose(3, 1, 2, 0, 4, 5).reshape(n * slots, rows, side)
    spread = lax.all_to_all(low, EVERY, 0, 0, tiled=True)
    tokens_g = lax.all_gather(inputs, "hz", axis=0, tiled=True)

    group, group_tokens = Z * PN, Z * local_count

    def fetch(numbers, *others):
        places = inverse[numbers.reshape(-1)]
        for other in others:
            places = places + zero_of(other)
        picked = jnp.take(spread, places, axis=0, mode="clip")
        got = lax.all_to_all(picked, "hz", 0, 0, tiled=True)
        return got.reshape(Z, -1, rows, side).transpose(1, 0, 2, 3).reshape(-1, part, side)

    def all_plane(got, R):
        got = lax.all_gather(got, ("hp", "seq"), axis=0, tiled=False)
        return got.reshape(rep, R, -1, part, side)

    got_attn = fetch(attn_list, tokens_g)
    w_attn = all_plane(got_attn, D)
    def fetch_beside(numbers, other):
        def part_for(j):
            wanted = lax.dynamic_index_in_dim(numbers, (zi + j) % Z, 0, keepdims=False)
            return jnp.take(spread, inverse[wanted] + zero_of(other), axis=0, mode="clip")

        got = jnp.take(exchange_z(part_for), relative, axis=0, mode="clip")
        return got.transpose(1, 0, 2, 3).reshape(-1, part, side)

    w_gateup = all_plane(fetch_beside(gateup_list, got_attn), D)

    def rope(values, sign):
        first, second = values[:, :half_size], values[:, half_size:]
        return jnp.concatenate(
            [first * cosine - second * sine * sign, second * cosine + first * sine * sign], axis=-1
        )

    head = zi * PN + pi
    gains_head = lax.dynamic_slice_in_dim(norm_gains[2:4], head * head_size, head_size, axis=1)

    def to_heads(stack):
        m = stack.shape[0]
        shaped = stack.reshape(m, Z, local_count, PN, head_size).transpose(3, 0, 1, 2, 4)
        got = lax.all_to_all(shaped, "hp", 0, 0, tiled=True)
        return got.transpose(1, 2, 0, 3, 4).reshape(m, length, head_size)

    def to_groups(stack):
        m = stack.shape[0]
        shaped = stack.reshape(m, Z, PN, local_count, head_size).transpose(2, 0, 1, 3, 4)
        got = lax.all_to_all(shaped, "hp", 0, 0, tiled=True)
        return got.transpose(1, 2, 3, 0, 4).reshape(m, group_tokens, quarter)

    raw = nn(tokens_g, w_attn, columns=3)
    raw_three = raw.reshape(group_tokens, 3, quarter).transpose(1, 0, 2)
    squares = jnp.sum(raw_three[:2] * raw_three[:2], axis=-1)
    ids = jnp.pad(segment_ids.astype(f32), ((0, 0), (0, group_tokens - local_count)))
    shared = from_group(jnp.concatenate([squares, ids])).reshape(Z, PN, 3, Z, local_count)
    squares, row_ids = shared[:, :, :2], shared[:, :, 2, 0].reshape(-1).astype(jnp.int32)
    length = row_ids.shape[0]
    begins = begins_of(row_ids)
    places = jnp.arange(length, dtype=jnp.int32) - begins
    half_size = head_size // 2
    frequency = rope_base ** (-2.0 * jnp.arange(half_size, dtype=f32) / head_size)
    angles = places.astype(f32)[:, None] * frequency[None, :]
    cosine, sine = jnp.cos(angles), jnp.sin(angles)

    squares = jnp.sum(squares, axis=0).transpose(1, 2, 0, 3).reshape(2, length, 1)
    raw_row = to_heads(raw_three.astype(bf16))
    invs = lax.rsqrt(squares / model_width + epsilon)
    query_hat, key_hat = (raw_row[i].astype(f32) * invs[i] for i in range(2))
    query_row = rope(query_hat * gains_head[0], 1.0).astype(bf16)
    key_row = rope(key_hat * gains_head[1], 1.0).astype(bf16)
    value_row = raw_row[2]

    got_down = fetch_beside(down_list, squares)

    begin_line = begins[None, :]
    mixed, log_sums = attend(query_row, key_row, value_row, begin_line, score_scale)
    attended = to_groups(mixed[None]).reshape(Z, local_count, quarter)
    attended_rel = jnp.take(attended, relative, axis=0, mode="clip")
    attn_parts = [nn(attended_rel[k], w_attn, row=3) for k in range(Z)]
    attn_raw = ring_scatter(lambda k: attn_parts[k])
    w_down = all_plane(after(got_down, w_gateup, attn_parts[1]), F // Z)
    resid = inputs.astype(f32) + rms_norm(attn_raw, norm_gains[0])

    resid_blocks, near = ring_gather(resid.astype(bf16), lambda pair: gate_up(pair, w_gateup))

    tokens_z = tokens_g.reshape(Z, local_count, model_width)
    middle = local_count // 2
    tok_one, tok_two = after(tokens_z[:, :middle], resid), after(tokens_z[:, middle:], resid)
    tok_one = jnp.stack([tok_one, swap(tok_one, 1)])
    tok_two = jnp.stack([tok_two, swap(tok_two, 2)])
    tok_parts = [tok_one, swap(tok_one, 2), tok_two, swap(tok_two, 1)]
    tok_parts = [t.reshape(-1, model_width) for t in tok_parts]
    tok_near, tok_far = tok_parts[::2], tok_parts[1::2]
    gates, ups, hiddens = zip(near, gate_up(resid_blocks[2:], w_gateup))

    def entry(halves, k):
        return halves[k // 2][k % 2 * local_count : (k % 2 + 1) * local_count]

    downs = [nn(hiddens[0], w_down), nn(hiddens[1], w_down, *tok_near)]
    down_raw = ring_scatter(lambda k: entry(downs, k))
    output = (resid + rms_norm(down_raw, norm_gains[1])).astype(bf16)[None]

    upstream = cotangent[0].astype(f32)
    _, down_norm_back = jax.vjp(rms_norm, down_raw, norm_gains[1])
    down_grad, gain_mlp_grad = down_norm_back(upstream)
    down_blocks, near = ring_gather(
        down_grad.astype(bf16),
        lambda pair: [hidden_back(pair, w_down, gates[0], ups[0])],
    )
    gateup_grads = near + [hidden_back(down_blocks[2:], w_down, gates[1], ups[1], *tok_far)]

    def spread_z(summed):
        summed = summed.reshape(-1, Z, rows, side)
        return exchange_z(
            lambda j: lax.dynamic_index_in_dim(summed, (zi + j) % Z, 1, keepdims=False)
        )

    def blocks_of(pieces):
        return pieces.reshape(rep, -1, part, side)

    def sum_plane(pieces):
        return lax.psum_scatter(
            blocks_of(pieces), ("hp", "seq"), scatter_dimension=0, tiled=False
        )

    down_pieces = tn(hiddens, [b[None] for b in down_blocks], rep, side, spare=quarter // side)
    gate_pieces = tn(resid_blocks, gateup_grads, rep, side, only=0)
    up_pieces = tn(resid_blocks, gateup_grads, rep, side, only=1)
    gate_sum = sum_plane(gate_pieces)
    up_sum = sum_plane(up_pieces)
    resid_parts = [nt([gateup_grads[0]], w_gateup), nt([gateup_grads[1]], w_gateup)]
    resid_grad = upstream + ring_scatter(lambda k: entry(resid_parts, k))

    _, attn_norm_back = jax.vjp(rms_norm, attn_raw, norm_gains[0])
    attn_grad, gain_attn_grad = attn_norm_back(resid_grad)
    attn_low = attn_grad.astype(bf16)
    attn_blocks = ring_gather(attn_low)
    grad_rel = nt([b[None] for b in attn_blocks], w_attn, row=3).astype(bf16)
    grad_rel = grad_rel.reshape(Z, local_count, quarter)
    grad_abs = jnp.take(grad_rel, relative, axis=0, mode="clip")
    grad_row = to_heads(grad_abs.reshape(1, group_tokens, quarter))[0]
    last_pieces = tn(
        [attended_rel[k] for k in range(Z)],
        [b[None] for b in attn_blocks],
        rep,
        side,
        base=down_pieces,
    )
    last_sum = sum_plane(last_pieces)
    gate_sent = spread_z(after(gate_sum, grad_abs))
    query_grad, key_grad, value_grad = attend_back(
        query_row,
        grad_row,
        key_row,
        value_row,
        begin_line,
        log_sums,
        score_scale,
    )
    query_turn, key_turn = rope(query_grad.astype(f32), -1.0), rope(key_grad.astype(f32), -1.0)
    gain_query = jnp.sum(query_turn * query_hat, axis=0)
    gain_key = jnp.sum(key_turn * key_hat, axis=0)
    query_turn, key_turn = query_turn * gains_head[0], key_turn * gains_head[1]
    dots = jnp.stack([jnp.sum(query_turn * query_hat, -1), jnp.sum(key_turn * key_hat, -1)])
    dots = jnp.sum(from_group(dots).reshape(group, 2, length), axis=0) / model_width
    up_sent, down_sent = spread_z(after(up_sum, dots)), spread_z(last_sum)
    dots = dots[..., None]
    query_back = ((query_turn - query_hat * dots[0]) * invs[0]).astype(bf16)
    key_back = ((key_turn - key_hat * dots[1]) * invs[1]).astype(bf16)

    back_row = jnp.concatenate([query_back, key_back, value_grad], axis=1)
    by_half = back_row.reshape(Z, PN, 2, middle, 3 * head_size).transpose(1, 2, 0, 3, 4)

    def rows_of(half, *bits):
        picked = jnp.take(by_half[:, half], jnp.stack([pi ^ bit for bit in bits]), axis=0, mode="clip")
        return picked.reshape(-1, 3 * head_size)

    back_parts = [rows_of(0, 0, 1), rows_of(0, 2, 3), rows_of(1, 0, 2), rows_of(1, 1, 3)]
    heads_grad = heads_tn(tok_parts, back_parts, rep, side, gate_sent)
    heads_sum = sum_seq_scatter(heads_grad.reshape(PN, S, D, part, 3 * head_size), 1)
    heads_sum = heads_sum.reshape(PN, D, Z, rows, 3 * head_size).transpose(2, 0, 1, 3, 4)
    heads_sent = lax.all_to_all(
        heads_sum.reshape(group, D, rows, 3 * head_size), GROUP, 0, 0, tiled=True
    ).reshape(Z, PN, D, rows, 3, head_size)
    heads_sent = heads_sent.transpose(4, 2, 0, 3, 1, 5).reshape(3 * square, rows, side)

    back_abs = to_groups(jnp.stack([query_back, key_back, value_grad]))
    back_rel = jnp.take(
        back_abs.reshape(3, Z, local_count, quarter), relative, axis=1, mode="clip"
    )
    near_back = nt([back_rel[:, 0], back_rel[:, 1]], w_attn, up_sent, heads_grad)
    back_parts = [near_back, nt([back_rel[:, 2], back_rel[:, 3]], w_attn)]
    input_grad = resid_grad + ring_scatter(lambda k: entry(back_parts, k))


    spots = jnp.zeros((2, model_width), f32)
    spots = lax.dynamic_update_slice(spots, jnp.stack([gain_query, gain_key]), (0, head * head_size))
    gain_local = jnp.concatenate([jnp.stack([gain_attn_grad, gain_mlp_grad]), spots])
    shares = lax.all_to_all(gain_local.reshape(n, -1), EVERY, 0, 0, tiled=True)
    share = jnp.sum(shares, axis=0)
    gain_grads = lax.all_to_all(
        jnp.broadcast_to(share, (n, share.shape[0])), EVERY, 0, 0, tiled=True
    ).reshape(gain_local.shape)

    flat = [heads_sent, gate_sent, up_sent, down_sent]
    sent = jnp.concatenate([a.reshape(-1, rows, side) for a in flat])
    split = gateup_list.reshape(Z, D, 2, -1)
    last = jnp.concatenate([down_list, out_list.reshape(Z, -1)], axis=1)
    order = [split[:, :, 0], split[:, :, 1], last]
    order = [jnp.take(o.reshape(Z, -1), relative, axis=0, mode="clip").reshape(-1) for o in order]
    order = jnp.concatenate([number[: 3 * square]] + order)
    where_is = jnp.zeros((total_blocks,), jnp.int32).at[order].set(number)
    to_slots = jnp.take(sent, where_is[owner_map] + zero_of(input_grad), axis=0, mode="clip")
    got = lax.all_to_all(to_slots, EVERY, 0, 0, tiled=True)
    got = got.reshape(Z, PN, S, slots, rows, side).transpose(3, 1, 2, 0, 4, 5)
    grad_slots, left_new, right_new, new_weights = shampoo(
        got.reshape(slots, side, side), left_stats, right_stats, left_root, right_root, weights
    )
    new_gains = norm_gains - gain_rate * gain_grads * lax.rsqrt(
        jnp.mean(gain_grads * gain_grads, axis=1, keepdims=True) + epsilon
    )
    return (
        output,
        input_grad[None],
        grad_slots,
        left_new,
        right_new,
        new_weights,
        gain_grads,
        new_gains,
    )


def solution(mesh):
    heads, seqs = mesh.shape["head"], mesh.shape["seq"]
    fine = Mesh(mesh.devices.reshape(Z, heads // Z, seqs), EVERY)
    tok = P("seq", GROUP, None)
    slot = P(EVERY, None, None)
    return jax.shard_map(
        body,
        mesh=fine,
        in_specs=(tok, tok, P("seq", GROUP), P(), slot, P(), slot, slot, slot, slot),
        out_specs=(tok, tok, slot, slot, slot, slot, P(), P()),
        check_vma=False,
    )
```
